128 devices in a mesh: grp: 4 (over y_lo, core), blk: 32 (over y_hi, z, x).
Axes of the slice: x: 4, y: 4 (y_hi: 2, y_lo: 2; y = y_hi * 2 + y_lo), z: 4, core: 2. Of those that a mesh axis runs over, the one named last changes fastest.
Arguments:
- volume: float32 [256, 768, 768], P(('grp', 'blk')), may hold values from 0 to 2
- voxel_norm: float32 [256, 768, 768], P(('grp', 'blk')), may hold values from 0.6 to 2.4
- measured: float32 [768, 32, 1024], P('grp', 'blk'), may hold values from -6 to 6
- ray_norm: float32 [768, 32, 1024], P('grp', 'blk'), may hold values from 0.5 to 2
- axial_weights: float32 [256, 32, 8], P(('grp', 'blk')), may hold values from 0.05 to 1
- row_start: int32 [32, 128], replicated, may hold values from 0 to 760, as said below
- row_order: int32 [768], replicated, may hold values from 0 to 767, each once
- subset: int32 [32], replicated, may hold values from 0 to 1023
Outputs:
- new_volume: float32 [256, 768, 768], P(('grp', 'blk'))
- residual: float32 [768, 32, 1024], P('grp', 'blk')
The draws below stay inside these ranges and needn't reach their ends.
Inputs may be any that keep to these rules, and one draw needn't show every extreme that they name: row_start[a, s] rises strictly with s, every footprint lies on the detector, and within each group of 32 consecutive slabs (equal s // 32) a slab's footprint starts at most 155 rows after the group's first slab's; both bounds are reached. `row_order`: a permutation of the detector rows.
All inputs are finite; a program needn't handle non-finite values.
Results may differ from the reference program's by a relative error of at most 0.0015.
Values may be sent and summed in bfloat16 or wider, within the bound.
A program may use at most 128 MiB of HBM per device.

```python
import math
import jax
import jax.numpy as jnp
from jax import lax

NX = 768
NY = 768
NU = 1024
NV = 768
TOTAL_ANG = 1024
FOOT = 8
Z_DEV = 2
SLABS = 128
NZ = 256
ANGLES = 32
STRIDE_MAX = 5


def draw_row_start(key, part):
    key = jax.random.fold_in(key, 7)
    key_steps, key_full, key_room = jax.random.split(key, 3)
    strides = jax.random.randint(key_steps, (ANGLES, SLABS - 1), 1, STRIDE_MAX + 1)
    chosen = jax.random.randint(key_full, (), 0, ANGLES)
    marked = jnp.arange(ANGLES, dtype=jnp.int32) == chosen
    strides = jnp.where(marked[:, None], STRIDE_MAX, strides)
    spans = jnp.sum(strides, axis=1)
    room = NV - FOOT - spans
    shifts = jax.random.randint(key_room, (ANGLES,), 0, room + 1)
    shifts = jnp.where(marked, room, shifts)
    rising = jnp.concatenate([jnp.zeros((ANGLES, 1), jnp.int32), jnp.cumsum(strides, axis=1).astype(jnp.int32)], axis=1)
    return (rising + shifts[:, None]).astype(jnp.int32)


def place_ends(array, key, smallest, high):
    longest = array.shape.index(max(array.shape))
    spots = []
    for shift in (0, 1):
        where = [jax.random.randint(jax.random.fold_in(key, axis), (), 0, length) for axis, length in enumerate(array.shape)]
        where[longest] = (where[longest] + shift) % array.shape[longest]
        spots.append(tuple(where))
    return array.at[spots[0]].set(smallest).at[spots[1]].set(high)


def level_of(rng, extent, cuts, smallest, high):
    level, own = 1.0, jax.random.fold_in(rng, 6)
    for dim, blocks in cuts:
        draws = jnp.exp(jax.random.uniform(jax.random.fold_in(own, dim), (blocks,), jnp.float32, smallest / len(cuts), high / len(cuts)))
        level = level * jnp.repeat(draws, extent[dim] // blocks).reshape([-1 if axis == dim else 1 for axis in range(len(extent))])
    return level


def noise(key, extent, scale, bound, shards=(), kind=jnp.bfloat16):
    gain = level_of(key, extent, shards, -0.22, 0.18) if shards else 1.0
    drawn = jax.random.normal(key, extent, jnp.float32) * scale * gain
    return jnp.minimum(jnp.maximum(drawn, -bound), bound).astype(kind)


def setup_inputs(seed: int = 0) -> dict:
    key_of = jax.random.split(jax.random.key(seed), 9)
    return {
        "volume": jnp.clip(2.0 * jax.random.uniform(key_of[0], (NZ, NY, NX), jnp.float32) ** level_of(key_of[0], (NZ, NY, NX), ((0, 128),), -0.2, 0.2), 0.0, 2.0),
        "voxel_norm": jnp.clip(jnp.exp(math.log(2.4) - 1.3862944 * jax.random.uniform(key_of[1], (NZ, NY, NX), jnp.float32) ** level_of(key_of[1], (NZ, NY, NX), ((0, 128),), -0.2, 0.2)), 0.6, 2.4),
        "measured": noise(key_of[2], (NV, ANGLES, NU), 1.0, 6.0, ((0, 4), (1, 32)), jnp.float32),
        "ray_norm": jnp.clip(jnp.exp(math.log(2.0) - 1.3862944 * jax.random.uniform(key_of[3], (NV, ANGLES, NU), jnp.float32) ** level_of(key_of[3], (NV, ANGLES, NU), ((0, 4), (1, 32)), -0.2, 0.2)), 0.5, 2.0),
        "axial_weights": jnp.clip(0.05 + 0.95 * jax.random.uniform(key_of[4], (NZ, ANGLES, FOOT), jnp.float32) ** level_of(key_of[4], (NZ, ANGLES, FOOT), ((0, 128),), -0.2, 0.2), 0.05, 1.0),
        "row_start": draw_row_start(jax.random.fold_in(key_of[8], 71), 0),
        "row_order": jax.random.permutation(key_of[6], NV).astype(jnp.int32),
        "subset": place_ends(jax.random.randint(key_of[7], (ANGLES,), 0, TOTAL_ANG), jax.random.fold_in(key_of[7], 1), 0, TOTAL_ANG - 1).astype(jnp.int32),
    }


precise = lax.Precision.HIGHEST


def view_angles(subset):
    return (2.0 * math.pi / TOTAL_ANG) * subset.astype(jnp.float32)


def transaxial_weights(view_angle, detector_cols, volume_cols):
    positions = jnp.arange(volume_cols, dtype=jnp.float32)
    detector_pos = jnp.arange(detector_cols, dtype=jnp.float32)
    centre = (detector_cols - 1) / 2.0 + (0.8 * detector_cols / volume_cols) * (positions - (volume_cols - 1) / 2.0)[None, :] + (0.05 * detector_cols) * jnp.sin(view_angle)[:, None]
    return jnp.maximum(0.0, 1.0 - jnp.abs(detector_pos[None, :, None] - centre[:, None, :]))


def depth_weights(view_angle, depth_cells):
    positions = jnp.arange(depth_cells, dtype=jnp.float32)
    middle = ((depth_cells - 1) / 2.0) * (1.0 + 0.8 * jnp.sin(view_angle))
    bump = jnp.maximum(0.0, 1.0 - jnp.abs(positions[None, :] - middle[:, None]) / (0.1 * depth_cells))
    return (1.0 + 2.0 * bump) / depth_cells


def reference(volume, voxel_norm, measured, ray_norm, axial_weights, row_start, row_order, subset):
    view_angle = view_angles(subset)
    depth_weight = depth_weights(view_angle, NY)
    blocks = ANGLES // 8
    summed = jnp.einsum("ay,zyx->azx", depth_weight, volume, precision=precise)

    def project(pieces):
        return jnp.einsum("aux,azx->azu", transaxial_weights(pieces[0], NU, NX), pieces[1], precision=precise)

    sinogram = lax.map(project, (view_angle.reshape(blocks, 8), summed.reshape(blocks, 8, NZ, NX))).reshape(ANGLES, NZ, NU)
    grouped = axial_weights.reshape(SLABS, Z_DEV, ANGLES, FOOT)
    weighted = jnp.einsum("sqar,asqu->asru", grouped, sinogram.reshape(ANGLES, SLABS, Z_DEV, NU), precision=precise)
    row_index = row_start[:, :, None] + jnp.arange(FOOT, dtype=jnp.int32)[None, None, :]
    angle_index = jnp.broadcast_to(jnp.arange(ANGLES, dtype=jnp.int32)[:, None, None], row_index.shape)
    forward = jnp.zeros((ANGLES, NV, NU), jnp.float32).at[angle_index, row_index].add(weighted)
    residual = ray_norm * (measured - jnp.transpose(forward[:, row_order, :], (1, 0, 2)))
    ratio_rows = residual.astype(jnp.bfloat16)
    natural = jnp.zeros((NV, ANGLES, NU), jnp.bfloat16).at[row_order].set(ratio_rows)
    picked = natural[row_index, angle_index, :].astype(jnp.float32)
    back_terms = jnp.einsum("sqar,asru->asqu", grouped, picked, precision=precise).reshape(ANGLES, NZ, NU)

    def spread_block(pieces):
        return jnp.einsum("aux,azu->azx", transaxial_weights(pieces[0], NU, NX), pieces[1], precision=precise)

    spread = lax.map(spread_block, (view_angle.reshape(blocks, 8), back_terms.reshape(blocks, 8, NZ, NU))).reshape(ANGLES, NZ, NX)
    update = jnp.einsum("ay,azx->zyx", depth_weight, spread, precision=precise)
    return jnp.maximum(0.0, volume + voxel_norm * update), residual
```

```python
import functools
import math

import jax
import jax.numpy as jnp
from jax import lax
from jax.experimental import pallas as pl
from jax.experimental.pallas import tpu as pltpu
from jax.sharding import PartitionSpec as P

TOTAL_ANG = 1024
MESH = pl.DeviceIdType.MESH
LANES = 128
ANGLES = 32
FOOT = 8
COLS = 768
DEPTH = 768
CELLS = 1024
ROWS = 192
STEP = 0.8 * CELLS / COLS


def halves(value):
    high = value.astype(jnp.bfloat16)
    return high, (value - high.astype(jnp.float32)).astype(jnp.bfloat16)


def dot(left, right):
    return jnp.dot(left, right, preferred_element_type=jnp.float32)


def depth_weight(cell, sine):
    middle = (DEPTH - 1) / 2.0 * (1.0 + 0.8 * sine)
    bump = jnp.maximum(0.0, 1.0 - jnp.abs(cell - middle) / (0.1 * DEPTH))
    return (1.0 + 2.0 * bump) / DEPTH


def centre_of(col, shift):
    return ((CELLS - 1) / 2.0 + STEP * (col - (COLS - 1) / 2.0)) + shift


def pick(tiles, first, last, index):
    inside = index & (LANES - 1)
    tile = index >> 7
    value = None
    for number in range(first, last + 1):
        found = jnp.take_along_axis(tiles[number], inside, axis=1, mode="promise_in_bounds")
        value = found if value is None else jnp.where(tile == number, found, value)
    return value


def span(low, high, tiles):
    first = max(0, min(tiles - 1, math.floor(low) // LANES))
    return first, max(first, min(tiles - 1, math.floor(high) // LANES))


def forward_kernel(sine_ref, volume_ref, out_ref, total):
    slice_index, part = pl.program_id(0), pl.program_id(1)
    block = volume_ref.shape[1]
    cell = (lax.broadcasted_iota(jnp.int32, (ANGLES, block), 1) + part * block).astype(jnp.float32)
    high, low = halves(depth_weight(cell, sine_ref[:, :1]))
    volume_high, volume_low = halves(volume_ref[0])
    both = dot(jnp.concatenate([high, low], axis=0), volume_high)
    piece = both[:ANGLES] + (both[ANGLES:] + dot(high, volume_low))

    @pl.when(part == 0)
    def _():
        total[...] = piece

    @pl.when(part > 0)
    def _():
        total[...] += piece

    @pl.when(part == pl.num_programs(1) - 1)
    def _():
        shift = (0.05 * CELLS) * sine_ref[...]
        tiles = [total[:, t * LANES:(t + 1) * LANES] for t in range(COLS // LANES)]
        lane = lax.broadcasted_iota(jnp.int32, (ANGLES, LANES), 1).astype(jnp.float32)
        for chunk in range(CELLS // LANES):
            detector = lane + chunk * LANES
            nearest = jnp.floor((detector - (CELLS - 1) / 2.0 - shift) * (1.0 / STEP) + (COLS - 1) / 2.0)
            middle = (chunk * LANES - (CELLS - 1) / 2.0) / STEP + (COLS - 1) / 2.0
            first, last = span(middle - 49.5, middle + 49.5 + 128 / STEP + 1, COLS // LANES)
            value = None
            for near in (0.0, 1.0):
                col = nearest + near
                weight = jnp.maximum(0.0, 1.0 - jnp.abs(detector - centre_of(col, shift)))
                weight = jnp.where((col >= 0.0) & (col <= COLS - 1.0), weight, 0.0)
                term = weight * pick(tiles, first, last, col.astype(jnp.int32))
                value = term if value is None else value + term
            out_ref[pl.ds(slice_index * 8 + chunk, ANGLES, stride=16), :] = value


def final_kernel(sine_ref, row_ref, back_ref, volume_ref, norm_ref, out_ref, spread):
    slice_index, part = pl.program_id(0), pl.program_id(1)
    block = volume_ref.shape[1]

    @pl.when(part == 0)
    def _():
        shift = (0.05 * CELLS) * sine_ref[...]
        tiles = [
            back_ref[pl.ds(slice_index * 8 + chunk, ANGLES, stride=16), :]
            for chunk in range(CELLS // LANES)
        ]
        lane = lax.broadcasted_iota(jnp.int32, (ANGLES, LANES), 1).astype(jnp.float32)
        for chunk in range(COLS // LANES):
            centre = centre_of(lane + chunk * LANES, shift)
            left = jnp.floor(centre)
            middle = (CELLS - 1) / 2.0 + STEP * (chunk * LANES - (COLS - 1) / 2.0)
            first, last = span(middle - 52.5, middle + 52.5 + STEP * 128 + 1, CELLS // LANES)
            value = None
            for near in (0.0, 1.0):
                detector = left + near
                weight = jnp.maximum(0.0, 1.0 - jnp.abs(detector - centre))
                term = weight * pick(tiles, first, last, detector.astype(jnp.int32))
                value = term if value is None else value + term
            high, low = halves(value)
            here = slice(chunk * LANES, (chunk + 1) * LANES)
            spread[0:ANGLES, here] = high
            spread[ANGLES:2 * ANGLES, here] = low
            spread[2 * ANGLES:3 * ANGLES, here] = high
            spread[3 * ANGLES:4 * ANGLES, here] = jnp.zeros_like(high)

    cell = (lax.broadcasted_iota(jnp.int32, (block, LANES), 0) + part * block).astype(jnp.float32)
    lane = lax.broadcasted_iota(jnp.int32, (block, LANES), 1)
    weight = depth_weight(cell, row_ref[0:1, :])
    high = weight.astype(jnp.bfloat16).astype(jnp.float32)
    weight = jnp.where(lane < 2 * ANGLES, high, weight - high).astype(jnp.bfloat16)
    update = dot(weight, spread[...])
    out_ref[0] = jnp.maximum(0.0, volume_ref[0] + norm_ref[0] * update)


def exchange_kernel(
    sino, aux, wanted, measured_hbm, norm_hbm, back, residual,
    every, every_aux, measured, norm, weight, ratio, partial, from_sibling, ahead, from_far,
    linear, arrived, load_sem, send_sem, recv_sem, aux_send, aux_recv, far_send, far_recv,
    near_send, near_recv, pass_send, pass_recv, aux2_send, aux2_recv, sum_send, sum_recv,
    out_send, out_recv,
):
    g, m = lax.axis_index("grp"), lax.axis_index("blk")
    core, y_lo = g % 2, g // 2
    y_hi, z, x = m // 16, (m // 4) % 4, m % 4
    sibling = (y_lo * 2 + (1 - core), m)
    far = ((1 - y_lo) * 2 + core, m)
    far_sibling = (1 - y_lo) * 2 + (1 - core)

    def partner(d):
        flip = d // 16
        return ((y_lo + flip) % 2) * 2 + core, ((y_hi + flip) % 2) * 16 + ((z + (d // 4) % 4) % 4) * 4 + (x + d % 4) % 4

    def source(d):
        flip = d // 16
        return ((y_hi + flip) % 2) * 16 + ((z + 4 - (d // 4) % 4) % 4) * 4 + (x + 4 - d % 4) % 4

    def slot(group, member, members=1):
        return pl.ds(pl.multiple_of((group * 32 + member) * 16, 16), members * 16)

    load = [
        pltpu.make_async_copy(measured_hbm, measured, load_sem.at[0]),
        pltpu.make_async_copy(norm_hbm, norm, load_sem.at[1]),
    ]
    for copy in load:
        copy.start()

    barrier = pltpu.get_barrier_semaphore()

    def greet(d, carry):
        pl.semaphore_signal(barrier, inc=1, device_id=partner(d), device_id_type=MESH)
        return carry

    lax.fori_loop(1, 32, greet, 0)
    for device in (sibling, far):
        pl.semaphore_signal(barrier, inc=1, device_id=device, device_id_type=MESH)
    pl.semaphore_wait(barrier, 33)

    def remote(source_ref, target_ref, send, recv, device):
        return pltpu.make_async_remote_copy(
            src_ref=source_ref, dst_ref=target_ref, send_sem=send, recv_sem=recv,
            device_id=device, device_id_type=MESH,
        )

    def first_copy(d, member_from):
        device = partner(d)
        return remote(
            sino.at[slot(0, device[1])], every.at[slot(device[0] if member_from is None else g, m if member_from is None else member_from)],
            send_sem.at[d], recv_sem.at[d], device,
        )

    def first_aux(d, member_from):
        device = partner(d)
        row = device[0] * 32 + m if member_from is None else g * 32 + member_from
        return remote(aux.at[device[1]], every_aux.at[row], aux_send.at[d], aux_recv.at[d], device)

    def send(d, carry):
        first_aux(d, None).start()
        first_copy(d, None).start()
        return carry

    lax.fori_loop(1, 32, send, 0)
    every[slot(g, m)] = sino[slot(0, m)]
    every_aux[g * 32 + m] = aux[m]

    def run(group, k):
        return slot(group, ((y_hi + k // 4) % 2) * 16 + ((z + 4 - k % 4) % 4) * 4, 4)

    def to_far(k, group):
        return remote(every.at[run(group, k)], every.at[run(group, k)], far_send.at[k], far_recv.at[k], far)

    def to_near(k, group):
        return remote(every.at[run(group, k)], every.at[run(group, k)], near_send.at[k], near_recv.at[k], sibling)

    def pass_on(k, group):
        return remote(every.at[run(group, k)], every.at[run(group, k)], pass_send.at[k], pass_recv.at[k], sibling)

    def hand(k, carry):
        def arrive(d, carry):
            first_copy(d, source(d)).wait_recv()
            first_aux(d, source(d)).wait_recv()
            return carry

        lax.fori_loop(jnp.where(k == 0, 1, 4 * k), 4 * k + 4, arrive, 0)
        to_far(k, g).start()
        to_near(k, g).start()
        return carry

    lax.fori_loop(0, 8, hand, 0)

    def aux_copy(number, group, device):
        rows = pl.ds(group * 32, 32)
        return remote(every_aux.at[rows], every_aux.at[rows], aux2_send.at[number], aux2_recv.at[number], device)

    aux_copy(0, g, far).start()
    aux_copy(1, g, sibling).start()
    aux_copy(0, far[0], far).wait_recv()
    aux_copy(2, far[0], sibling).start()

    def forward_on(k, carry):
        to_far(k, far[0]).wait_recv()
        pass_on(k, far[0]).start()
        return carry

    lax.fori_loop(0, 8, forward_on, 0)
    aux_copy(1, sibling[0], sibling).wait_recv()
    aux_copy(2, far_sibling, sibling).wait_recv()

    table = every_aux[...].reshape(ANGLES * 4, LANES)
    offset = wanted[0:1, :] - table[:, 16:17]
    tall = [None] * 8
    for q in range(2):
        value = jnp.zeros_like(offset)
        for r in range(FOOT):
            value = jnp.where(offset == float(r), table[:, q * FOOT + r:q * FOOT + r + 1], value)
        for h in range(4):
            tall[h * 2 + q] = value[h * 32:(h + 1) * 32]
    tall = jnp.concatenate(tall, axis=0)
    tall_high, tall_low = halves(tall)
    for h in range(4):
        weight[h * 128:h * 128 + 64, :] = tall_high[h * 64:(h + 1) * 64]
        weight[h * 128 + 64:(h + 1) * 128, :] = tall_low[h * 64:(h + 1) * 64]
    wide_high, wide_low = halves(tall.T[:ROWS])
    wide = jnp.concatenate([wide_high, wide_high, wide_low], axis=1)

    def settle(k, carry):
        to_near(k, sibling[0]).wait_recv()
        pass_on(k, far_sibling).wait_recv()
        return carry

    lax.fori_loop(0, 8, settle, 0)
    for copy in load:
        copy.wait()

    for pair in range(4):
        columns = []
        for chunk in (2 * pair, 2 * pair + 1):
            columns.append(jnp.concatenate(
                [every[pl.ds(h * 512 + q * 8 + chunk, 32, stride=16), :] for h in range(4) for q in range(2)], axis=0
            ))
        high, low = halves(jnp.concatenate(columns, axis=1))
        forward = dot(wide, jnp.concatenate([high, low, high], axis=0))
        for side in range(2):
            chunk = 2 * pair + side
            rows = pl.ds(chunk, ROWS, stride=8)
            value = norm[rows, :] * (measured[rows, :] - forward[:, side * LANES:(side + 1) * LANES])
            residual[rows, :] = value
            ratio[:, chunk * LANES:(chunk + 1) * LANES] = value.astype(jnp.bfloat16)

    def part_of(group):
        both = dot(weight[pl.ds(pl.multiple_of(group * 128, 128), 128), :ROWS], ratio[...])
        return both[:64] + both[64:]

    def to_sibling(number):
        return remote(partial.at[number], from_sibling.at[number], sum_send.at[number], sum_recv.at[number], sibling)

    partial[0] = part_of(far_sibling)
    to_sibling(0).start()
    partial[1] = part_of(sibling[0])
    to_sibling(1).start()
    ahead[...] = part_of(far[0])
    to_sibling(0).wait_recv()
    ahead[...] += from_sibling[0]
    over = remote(ahead, from_far, sum_send.at[2], sum_recv.at[2], far)
    over.start()
    own = part_of(g)
    to_sibling(1).wait_recv()
    own = own + from_sibling[1]
    over.wait_recv()
    own = own + from_far[...]
    for q in range(2):
        for chunk in range(8):
            linear[pl.ds(q * 8 + chunk, 32, stride=16), :] = own[q * 32:(q + 1) * 32, chunk * LANES:(chunk + 1) * LANES]

    def last_copy(d, member_from):
        device = partner(d)
        return remote(
            linear.at[slot(0, device[1])], arrived.at[slot(0, m if member_from is None else member_from)],
            out_send.at[d], out_recv.at[d], device,
        )

    def give(d, carry):
        last_copy(d, None).start()
        return carry

    lax.fori_loop(1, 32, give, 0)
    arrived[slot(0, m)] = linear[slot(0, m)]

    def take(d, carry):
        last_copy(d, source(d)).wait_recv()
        return carry

    lax.fori_loop(1, 32, take, 0)
    back[...] = arrived[...]

    def sent(d, carry):
        first_copy(d, None).wait_send()
        first_aux(d, None).wait_send()
        last_copy(d, None).wait_send()
        return carry

    lax.fori_loop(1, 32, sent, 0)

    def sent_runs(k, carry):
        to_far(k, g).wait_send()
        to_near(k, g).wait_send()
        pass_on(k, far[0]).wait_send()
        return carry

    lax.fori_loop(0, 8, sent_runs, 0)
    aux_copy(0, g, far).wait_send()
    aux_copy(1, g, sibling).wait_send()
    aux_copy(2, far[0], sibling).wait_send()
    to_sibling(0).wait_send()
    to_sibling(1).wait_send()
    over.wait_send()


def shards(volume, voxel_norm, measured, ray_norm, axial_weights, row_start, row_order, subset):
    f32, bf16 = jnp.float32, jnp.bfloat16
    g, m = lax.axis_index("grp"), lax.axis_index("blk")
    sine = jnp.sin(2.0 * math.pi / TOTAL_ANG * subset.astype(f32))
    sine_wide = jnp.broadcast_to(sine[:, None], (ANGLES, LANES))
    sine_row = jnp.broadcast_to(jnp.tile(sine, 4)[None, :], (8, LANES))
    starts = lax.dynamic_slice_in_dim(row_start, g * 32 + m, 1, 1).astype(f32)
    aux = jnp.concatenate(
        [axial_weights[0], axial_weights[1], starts, jnp.zeros((ANGLES, LANES - 17), f32)], axis=1
    ).reshape(ANGLES, 1, LANES)
    wanted = lax.dynamic_slice_in_dim(row_order, g * ROWS, ROWS, 0).astype(f32)
    wanted = jnp.broadcast_to(jnp.pad(wanted, (0, 64), constant_values=-1000.0)[None, :], (8, 256))

    block = 256
    whole = lambda shape: pl.BlockSpec(shape, lambda z, y: (0,) * len(shape))
    sliced = pl.BlockSpec((1, block, COLS), lambda z, y: (z, y, 0))
    sino = pl.pallas_call(
        forward_kernel,
        grid=(2, DEPTH // block),
        in_specs=[whole((ANGLES, LANES)), sliced],
        out_specs=whole((512, LANES)),
        out_shape=jax.ShapeDtypeStruct((512, LANES), f32),
        scratch_shapes=[pltpu.VMEM((ANGLES, COLS), f32)],
        compiler_params=pltpu.CompilerParams(vmem_limit_bytes=16 << 20),
        cost_estimate=pl.CostEstimate(flops=6 * 64 * DEPTH * COLS, bytes_accessed=4 * 2 * DEPTH * COLS, transcendentals=0),
        name="forward",
    )(sine_wide, volume)

    vmem = pl.BlockSpec(memory_space=pltpu.VMEM)
    dma = pltpu.SemaphoreType.DMA
    back, residual = pl.pallas_call(
        exchange_kernel,
        in_specs=[vmem, vmem, vmem, pl.BlockSpec(memory_space=pl.ANY), pl.BlockSpec(memory_space=pl.ANY)],
        out_specs=(vmem, vmem),
        out_shape=(jax.ShapeDtypeStruct((512, LANES), f32), jax.ShapeDtypeStruct((ROWS * 8, LANES), f32)),
        scratch_shapes=[
            pltpu.VMEM((2048, LANES), f32), pltpu.VMEM((128, 1, LANES), f32),
            pltpu.VMEM((ROWS * 8, LANES), f32), pltpu.VMEM((ROWS * 8, LANES), f32),
            pltpu.VMEM((512, 256), bf16), pltpu.VMEM((ROWS, CELLS), bf16),
            pltpu.VMEM((2, 64, CELLS), f32), pltpu.VMEM((2, 64, CELLS), f32),
            pltpu.VMEM((64, CELLS), f32), pltpu.VMEM((64, CELLS), f32),
            pltpu.VMEM((512, LANES), f32), pltpu.VMEM((512, LANES), f32),
            dma((2,)), dma((32,)), dma((32,)), dma((32,)), dma((32,)), dma((8,)), dma((8,)),
            dma((8,)), dma((8,)), dma((8,)), dma((8,)), dma((3,)), dma((3,)), dma((3,)), dma((3,)),
            dma((32,)), dma((32,)),
        ],
        compiler_params=pltpu.CompilerParams(collective_id=0, has_side_effects=True, vmem_limit_bytes=24 << 20),
        cost_estimate=pl.CostEstimate(flops=2 * 6 * 192 * 256 * 1024, bytes_accessed=4 << 20, transcendentals=0),
        name="exchange",
    )(sino, aux, wanted, measured.reshape(ROWS * 8, LANES), ray_norm.reshape(ROWS * 8, LANES))

    new_volume = pl.pallas_call(
        final_kernel,
        grid=(2, DEPTH // block),
        in_specs=[whole((ANGLES, LANES)), whole((8, LANES)), whole((512, LANES)), sliced, sliced],
        out_specs=sliced,
        out_shape=jax.ShapeDtypeStruct(volume.shape, f32),
        scratch_shapes=[pltpu.VMEM((LANES, COLS), bf16)],
        compiler_params=pltpu.CompilerParams(vmem_limit_bytes=24 << 20),
        cost_estimate=pl.CostEstimate(flops=6 * 64 * DEPTH * COLS, bytes_accessed=4 * 6 * DEPTH * COLS, transcendentals=0),
        name="final",
    )(sine_wide, sine_row, back, volume, voxel_norm)
    return new_volume, residual.reshape(measured.shape)


def solution(mesh):
    placed = (
        P(("grp", "blk"), None, None),
        P(("grp", "blk"), None, None),
        P("grp", "blk", None),
        P("grp", "blk", None),
        P(("grp", "blk"), None, None),
        P(),
        P(),
        P(),
    )
    return jax.shard_map(
        shards,
        mesh=mesh,
        in_specs=placed,
        out_specs=(P(("grp", "blk"), None, None), P("grp", "blk", None)),
        check_vma=False,
    )
```

```python
import math

import jax
import jax.numpy as jnp
from jax import lax
from jax.experimental import pallas as pl
from jax.experimental.pallas import tpu as pltpu
from jax.sharding import PartitionSpec as P

TOTAL_ANG = 1024
MESH = pl.DeviceIdType.MESH
LANES = 128
ANGLES = 32
FOOT = 8
COLS = 768
DEPTH = 768
CELLS = 1024
ROWS = 192
PARTS = 3
STEP = 0.8 * CELLS / COLS


def halves(value):
    high = value.astype(jnp.bfloat16)
    return high, (value - high.astype(jnp.float32)).astype(jnp.bfloat16)


def dot(left, right):
    return jnp.dot(left, right, preferred_element_type=jnp.float32)


def depth_weight(cell, sine):
    middle = (DEPTH - 1) / 2.0 * (1.0 + 0.8 * sine)
    bump = jnp.maximum(0.0, 1.0 - jnp.abs(cell - middle) / (0.1 * DEPTH))
    return (1.0 + 2.0 * bump) / DEPTH


def centre_of(col, shift):
    return ((CELLS - 1) / 2.0 + STEP * (col - (COLS - 1) / 2.0)) + shift


def pick(tiles, first, last, index):
    inside = index & (LANES - 1)
    tile = index >> 7
    value = None
    for number in range(first, last + 1):
        found = jnp.take_along_axis(tiles[number], inside, axis=1, mode="promise_in_bounds")
        value = found if value is None else jnp.where(tile == number, found, value)
    return value


def span(low, high, tiles):
    first = max(0, min(tiles - 1, math.floor(low) // LANES))
    return first, max(first, min(tiles - 1, math.floor(high) // LANES))


def sines(subset_ref, which):
    chosen = jnp.zeros_like(which)
    for angle in range(ANGLES):
        chosen = jnp.where(which == angle, subset_ref[angle], chosen)
    return jnp.sin(2.0 * math.pi / TOTAL_ANG * chosen.astype(jnp.float32))


def ray_sums(tiles, shift, chunk):
    lane = lax.broadcasted_iota(jnp.int32, (ANGLES, LANES), 1).astype(jnp.float32)
    detector = lane + chunk * LANES
    nearest = jnp.floor((detector - (CELLS - 1) / 2.0 - shift) * (1.0 / STEP) + (COLS - 1) / 2.0)
    middle = (chunk * LANES - (CELLS - 1) / 2.0) / STEP + (COLS - 1) / 2.0
    first, last = span(middle - 49.5, middle + 49.5 + 128 / STEP + 1, COLS // LANES)
    values, total = [0.0, 0.0], 0.0
    for near in (0.0, 1.0):
        col = nearest + near
        weight = jnp.maximum(0.0, 1.0 - jnp.abs(detector - centre_of(col, shift)))
        weight = jnp.where((col >= 0.0) & (col <= COLS - 1.0), weight, 0.0)
        index = col.astype(jnp.int32)
        values = [value + weight * pick(tile, first, last, index) for value, tile in zip(values, tiles)]
        total = total + weight
    return values, total


def spread_rows(tiles, shift, chunk):
    lane = lax.broadcasted_iota(jnp.int32, (ANGLES, LANES), 1).astype(jnp.float32)
    centre = centre_of(lane + chunk * LANES, shift)
    left = jnp.floor(centre)
    middle = (CELLS - 1) / 2.0 + STEP * (chunk * LANES - (COLS - 1) / 2.0)
    first, last = span(middle - 52.5, middle + 52.5 + STEP * 128 + 1, CELLS // LANES)
    value = 0.0
    for near in (0.0, 1.0):
        detector = left + near
        weight = jnp.maximum(0.0, 1.0 - jnp.abs(detector - centre))
        value = value + weight * pick(tiles, first, last, detector.astype(jnp.int32))
    return value


def main_kernel(
    subset, row_start, order, axial, volume_hbm, scale_hbm, measured_hbm, norm_hbm,
    back, residual, volume, scale,
    measured, norm, rowsum, straight, sino, aux, every, every_aux, every_wide, weight, wide, mean,
    ratio, ahead, from_far, own, linear, arrived,
    volume_sem, load_sem, send_sem, recv_sem, aux_send, aux_recv, far_send, far_recv,
    near_send, near_recv, pass_send, pass_recv, aux2_send, aux2_recv, ratio_send, ratio_recv,
    sum_send, sum_recv, out_send, out_recv,
):
    f32, bf16 = jnp.float32, jnp.bfloat16
    block = DEPTH // PARTS
    g, m = lax.axis_index("grp"), lax.axis_index("blk")
    core, y_lo = g % 2, g // 2
    y_hi, z, x = m // 16, (m // 4) % 4, m % 4
    sibling = (y_lo * 2 + (1 - core), m)
    far = ((1 - y_lo) * 2 + core, m)
    far_sibling = (1 - y_lo) * 2 + (1 - core)

    def partner(d):
        flip = d // 16
        return ((y_lo + flip) % 2) * 2 + core, ((y_hi + flip) % 2) * 16 + ((z + (d // 4) % 4) % 4) * 4 + (x + d % 4) % 4

    def source(d):
        flip = d // 16
        return ((y_hi + flip) % 2) * 16 + ((z + 4 - (d // 4) % 4) % 4) * 4 + (x + 4 - d % 4) % 4

    def slot(group, member, members=1):
        return pl.ds(pl.multiple_of((group * 32 + member) * 16, 16), members * 16)

    def remote(source_ref, target_ref, send, recv, device):
        return pltpu.make_async_remote_copy(
            src_ref=source_ref, dst_ref=target_ref, send_sem=send, recv_sem=recv,
            device_id=device, device_id_type=MESH,
        )

    bring = []
    for q in range(2):
        for part in range(PARTS):
            here = pl.ds(part * block, block)
            bring.append(pltpu.make_async_copy(volume_hbm.at[q, here], volume.at[q, here], volume_sem.at[q * PARTS + part]))
    for copy in bring:
        copy.start()
    load = [
        pltpu.make_async_copy(measured_hbm, measured, load_sem.at[0]),
        pltpu.make_async_copy(norm_hbm, norm, load_sem.at[1]),
        pltpu.make_async_copy(scale_hbm, scale, load_sem.at[2]),
    ]
    for copy in load:
        copy.start()

    barrier = pltpu.get_barrier_semaphore()

    def greet(d, carry):
        pl.semaphore_signal(barrier, inc=1, device_id=partner(d), device_id_type=MESH)
        return carry

    lax.fori_loop(1, 32, greet, 0)
    for device in (sibling, far):
        pl.semaphore_signal(barrier, inc=1, device_id=device, device_id_type=MESH)

    sine = sines(subset, lax.broadcasted_iota(jnp.int32, (ANGLES, LANES), 0))
    shift = (0.05 * CELLS) * sine
    tiles, means = [], []
    for q in range(2):
        total = 0.0
        for part in range(PARTS):
            cell = (lax.broadcasted_iota(jnp.int32, (ANGLES, block), 1) + part * block).astype(f32)
            high, low = halves(depth_weight(cell, sine[:, :1]))
            bring[q * PARTS + part].wait()
            volume_high, volume_low = halves(volume[q, part * block:(part + 1) * block, :])
            both = dot(jnp.concatenate([high, low], axis=0), volume_high)
            total = total + (both[:ANGLES] + (both[ANGLES:] + dot(high, volume_low)))
        middle = jnp.sum(total, axis=1, keepdims=True) * (1.0 / COLS)
        means.append(middle)
        total = total - middle
        tiles.append([total[:, t * LANES:(t + 1) * LANES] for t in range(COLS // LANES)])
    for chunk in range(CELLS // LANES):
        values, sums = ray_sums(tiles, shift, chunk)
        rowsum[:, chunk * LANES:(chunk + 1) * LANES] = sums
        for q in range(2):
            straight[pl.ds(q * 8 + chunk, ANGLES, stride=16), :] = values[q]
    sino[...] = straight[...].astype(bf16)

    lane = lax.broadcasted_iota(jnp.int32, (ANGLES, LANES), 1)
    first = jnp.sum(jnp.where(lane == g * 32 + m, row_start[...], 0), axis=1, keepdims=True).astype(f32)
    table = jnp.concatenate([axial[...].reshape(16, ANGLES), jnp.zeros((16, LANES - ANGLES), f32)], axis=1)
    table = jnp.concatenate([table, jnp.zeros((LANES - 16, LANES), f32)], axis=0).T[:ANGLES]
    for number, column in ((16, first), (17, means[0]), (18, means[1])):
        table = jnp.where(lane == number, column, table)
    aux[...] = table.reshape(ANGLES, 1, LANES)

    pl.semaphore_wait(barrier, 33)

    def first_copy(d, group, member):
        device = partner(d)
        return remote(sino.at[slot(0, device[1])], every.at[slot(group, member)], send_sem.at[d], recv_sem.at[d], device)

    def first_aux(d, group, member):
        device = partner(d)
        return remote(aux.at[device[1]], every_aux.at[group * 32 + member], aux_send.at[d], aux_recv.at[d], device)

    def send_rows(d, carry):
        first_copy(d, partner(d)[0], m).start()
        return carry

    def send_aux(d, carry):
        first_aux(d, partner(d)[0], m).start()
        return carry

    lax.fori_loop(1, 32, send_rows, 0)
    lax.fori_loop(1, 32, send_aux, 0)
    every[slot(g, m)] = sino[slot(0, m)]
    every_aux[g * 32 + m] = aux[m]

    def run(group, k):
        return slot(group, ((y_hi + k // 4) % 2) * 16 + ((z + 4 - k % 4) % 4) * 4, 4)

    def to_far(k, group):
        return remote(every.at[run(group, k)], every.at[run(group, k)], far_send.at[k], far_recv.at[k], far)

    def to_near(k, group):
        return remote(every.at[run(group, k)], every.at[run(group, k)], near_send.at[k], near_recv.at[k], sibling)

    def pass_on(k, group):
        return remote(every.at[run(group, k)], every.at[run(group, k)], pass_send.at[k], pass_recv.at[k], sibling)

    def hand(k, carry):
        def arrive(d, carry):
            first_copy(d, g, source(d)).wait_recv()
            return carry

        lax.fori_loop(jnp.where(k == 0, 1, 4 * k), 4 * k + 4, arrive, 0)
        to_far(k, g).start()
        to_near(k, g).start()
        return carry

    lax.fori_loop(0, 8, hand, 0)

    def aux_copy(number, group, device):
        rows = pl.ds(group * 32, 32)
        return remote(every_aux.at[rows], every_aux.at[rows], aux2_send.at[number], aux2_recv.at[number], device)

    def arrive_aux(d, carry):
        first_aux(d, g, source(d)).wait_recv()
        return carry

    lax.fori_loop(1, 32, arrive_aux, 0)
    aux_copy(0, g, far).start()
    aux_copy(1, g, sibling).start()

    def forward_on(k, carry):
        to_far(k, far[0]).wait_recv()
        pass_on(k, far[0]).start()
        return carry

    lax.fori_loop(0, 8, forward_on, 0)
    aux_copy(0, far[0], far).wait_recv()
    aux_copy(2, far[0], sibling).start()
    aux_copy(1, sibling[0], sibling).wait_recv()
    aux_copy(2, far_sibling, sibling).wait_recv()

    table = every_aux[...].reshape(4 * ANGLES, LANES)
    rows = order[...].astype(f32)
    lower = jnp.concatenate([rows[i:i + 1] for i in range(3)], axis=1)
    upper = jnp.concatenate([rows[i:i + 1] for i in range(3, 6)], axis=1)
    offset = jnp.where(y_lo == 0, lower, upper) - table[:, 16:17]
    tall, level = [None] * 8, [None] * 8
    for q in range(2):
        value = jnp.zeros_like(offset)
        for r in range(FOOT):
            value = jnp.where(offset == float(r), table[:, q * FOOT + r:q * FOOT + r + 1], value)
        for h in range(4):
            tall[h * 2 + q] = value[h * 32:(h + 1) * 32]
            level[h * 2 + q] = table[h * 32:(h + 1) * 32, 17 + q:18 + q]
    tall, level = jnp.concatenate(tall, axis=0), jnp.concatenate(level, axis=0)
    constant = jnp.sum(tall * level, axis=0, keepdims=True)
    mean[...] = jnp.broadcast_to(constant, (LANES, 2 * ROWS)).T
    tall_high, tall_low = halves(tall)
    for h in range(4):
        weight[h * 128:h * 128 + 64, :] = tall_high[h * 64:(h + 1) * 64]
        weight[h * 128 + 64:(h + 1) * 128, :] = tall_low[h * 64:(h + 1) * 64]
    wide_high, wide_low = halves(tall.T)
    wide[0] = wide_high
    wide[1] = wide_low

    def settle(k, carry):
        to_near(k, sibling[0]).wait_recv()
        pass_on(k, far_sibling).wait_recv()
        return carry

    lax.fori_loop(0, 8, settle, 0)
    for copy in load[:2]:
        copy.wait()
    every_wide[...] = every[...].astype(f32)

    mine = pl.ds(pl.multiple_of(core * ROWS, ROWS), ROWS)
    other = pl.ds(pl.multiple_of((1 - core) * ROWS, ROWS), ROWS)
    place = jnp.concatenate([wide[0, mine, :], wide[1, mine, :]], axis=0)
    own_mean = mean[mine, :]
    own_sum = rowsum[pl.ds(m, 1), :]
    ahead_weight = weight[pl.ds(pl.multiple_of(far[0] * 128, 128), 128), :]
    own_weight = weight[pl.ds(pl.multiple_of(g * 128, 128), 128), :]

    def to_sibling(pair, rows):
        here = pl.ds(pair * 256, 256)
        return remote(ratio.at[rows, here], ratio.at[rows, here], ratio_send.at[pair], ratio_recv.at[pair], sibling)

    def over(pair):
        return remote(ahead.at[pair], from_far.at[pair], sum_send.at[pair], sum_recv.at[pair], far)

    def forward(pair):
        columns = []
        for chunk in (2 * pair, 2 * pair + 1):
            columns.append(jnp.concatenate(
                [every_wide[pl.ds(h * 512 + q * 8 + chunk, 32, stride=16), :] for h in range(4) for q in range(2)], axis=0
            ))
        both = dot(place, jnp.concatenate(columns, axis=1).astype(bf16))
        value = both[:ROWS] + both[ROWS:]
        for side in range(2):
            chunk = 2 * pair + side
            here = slice(chunk * LANES, (chunk + 1) * LANES)
            found = value[:, side * LANES:(side + 1) * LANES] + own_mean * own_sum[:, here]
            rows = pl.ds(chunk, ROWS, stride=8)
            rest = norm[rows, :] * (measured[rows, :] - found)
            residual[rows, :] = rest
            ratio[mine, here] = rest.astype(bf16)
        to_sibling(pair, mine).start()

    def part_of(weights, pair):
        both = dot(weights, ratio[:, pair * 256:(pair + 1) * 256])
        return both[:64] + both[64:]

    def send_over(pair):
        to_sibling(pair, other).wait_recv()
        ahead[pair] = part_of(ahead_weight, pair).astype(bf16)
        over(pair).start()

    forward(0)
    for pair in range(1, 4):
        forward(pair)
        send_over(pair - 1)
    send_over(3)
    for pair in range(4):
        own[:, pair * 256:(pair + 1) * 256] = part_of(own_weight, pair)
    for pair in range(4):
        over(pair).wait_recv()
        value = own[:, pair * 256:(pair + 1) * 256] + from_far[pair].astype(f32)
        for q in range(2):
            for side in range(2):
                straight[pl.ds(q * 8 + 2 * pair + side, 32, stride=16), :] = value[q * 32:(q + 1) * 32, side * LANES:(side + 1) * LANES]
    linear[...] = straight[...].astype(bf16)

    def last_copy(d, member):
        device = partner(d)
        return remote(linear.at[slot(0, device[1])], arrived.at[slot(0, member)], out_send.at[d], out_recv.at[d], device)

    def give(d, carry):
        last_copy(d, m).start()
        return carry

    lax.fori_loop(1, 32, give, 0)
    arrived[slot(0, m)] = linear[slot(0, m)]

    def sent(d, carry):
        first_copy(d, partner(d)[0], m).wait_send()
        first_aux(d, partner(d)[0], m).wait_send()
        return carry

    lax.fori_loop(1, 32, sent, 0)

    def sent_runs(k, carry):
        to_far(k, g).wait_send()
        to_near(k, g).wait_send()
        pass_on(k, far[0]).wait_send()
        return carry

    lax.fori_loop(0, 8, sent_runs, 0)
    aux_copy(0, g, far).wait_send()
    aux_copy(1, g, sibling).wait_send()
    aux_copy(2, far[0], sibling).wait_send()
    for pair in range(4):
        to_sibling(pair, mine).wait_send()
        over(pair).wait_send()
    load[2].wait()

    def take(d, carry):
        last_copy(d, source(d)).wait_recv()
        return carry

    lax.fori_loop(1, 32, take, 0)
    back[...] = arrived[...]

    def given(d, carry):
        last_copy(d, m).wait_send()
        return carry

    lax.fori_loop(1, 32, given, 0)


def final_kernel(subset, back, volume, scale, residual_in, new_volume, residual, straight, spread, staged, sems, rest_sem):
    f32 = jnp.float32
    block = DEPTH // PARTS
    keep = pltpu.make_async_copy(residual_in, residual, rest_sem)
    keep.start()
    straight[...] = back[...].astype(f32)
    shift = (0.05 * CELLS) * sines(subset, lax.broadcasted_iota(jnp.int32, (ANGLES, LANES), 0))
    sine_row = sines(subset, lax.broadcasted_iota(jnp.int32, (8, LANES), 1) % ANGLES)[:1]
    weights = []
    for part in range(PARTS):
        cell = (lax.broadcasted_iota(jnp.int32, (block, LANES), 0) + part * block).astype(f32)
        lane = lax.broadcasted_iota(jnp.int32, (block, LANES), 1)
        weight = depth_weight(cell, sine_row)
        high = weight.astype(jnp.bfloat16).astype(f32)
        weights.append(jnp.where(lane < 2 * ANGLES, high, weight - high).astype(jnp.bfloat16))
    copies = []
    for q in range(2):
        tiles = [straight[pl.ds(q * 8 + chunk, ANGLES, stride=16), :] for chunk in range(CELLS // LANES)]
        for chunk in range(COLS // LANES):
            high, low = halves(spread_rows(tiles, shift, chunk))
            here = slice(chunk * LANES, (chunk + 1) * LANES)
            spread[q, 0:ANGLES, here] = high
            spread[q, ANGLES:2 * ANGLES, here] = low
            spread[q, 2 * ANGLES:3 * ANGLES, here] = high
            spread[q, 3 * ANGLES:4 * ANGLES, here] = jnp.zeros_like(high)
        for part in range(PARTS):
            here = slice(part * block, (part + 1) * block)
            update = dot(weights[part], spread[q])
            staged[q, here, :] = jnp.maximum(0.0, volume[q, here, :] + scale[q, here, :] * update)
            rows = pl.ds(part * block, block)
            copies.append(pltpu.make_async_copy(staged.at[q, rows], new_volume.at[q, rows], sems.at[q * PARTS + part]))
            copies[-1].start()
    for copy in copies:
        copy.wait()
    keep.wait()


def shards(volume, voxel_norm, measured, ray_norm, axial_weights, row_start, row_order, subset):
    f32, bf16 = jnp.float32, jnp.bfloat16
    vmem = pl.BlockSpec(memory_space=pltpu.VMEM)
    smem = pl.BlockSpec(memory_space=pltpu.SMEM)
    hbm = pl.BlockSpec(memory_space=pltpu.HBM)
    dma = pltpu.SemaphoreType.DMA
    lines = ROWS * 8
    back, residual, volume_near, scale_near = pl.pallas_call(
        main_kernel,
        in_specs=[smem, vmem, vmem, vmem, hbm, hbm, hbm, hbm],
        out_specs=(vmem, vmem, vmem, vmem),
        out_shape=(
            jax.ShapeDtypeStruct((512, LANES), bf16), jax.ShapeDtypeStruct((lines, LANES), f32),
            jax.ShapeDtypeStruct(volume.shape, f32), jax.ShapeDtypeStruct(volume.shape, f32),
        ),
        scratch_shapes=[
            pltpu.VMEM((lines, LANES), f32), pltpu.VMEM((lines, LANES), f32),
            pltpu.VMEM((ANGLES, CELLS), f32), pltpu.VMEM((512, LANES), f32), pltpu.VMEM((512, LANES), bf16),
            pltpu.VMEM((ANGLES, 1, LANES), f32), pltpu.VMEM((2048, LANES), bf16), pltpu.VMEM((128, 1, LANES), f32),
            pltpu.VMEM((2048, LANES), f32), pltpu.VMEM((512, 2 * ROWS), bf16), pltpu.VMEM((2, 2 * ROWS, 256), bf16),
            pltpu.VMEM((2 * ROWS, LANES), f32), pltpu.VMEM((2 * ROWS, CELLS), bf16),
            pltpu.VMEM((4, 64, 256), bf16), pltpu.VMEM((4, 64, 256), bf16), pltpu.VMEM((64, CELLS), f32),
            pltpu.VMEM((512, LANES), bf16), pltpu.VMEM((512, LANES), bf16),
            dma((2 * PARTS,)), dma((3,)), dma((32,)), dma((32,)), dma((32,)), dma((32,)), dma((8,)), dma((8,)),
            dma((8,)), dma((8,)), dma((8,)), dma((8,)), dma((3,)), dma((3,)), dma((4,)), dma((4,)),
            dma((4,)), dma((4,)), dma((32,)), dma((32,)),
        ],
        compiler_params=pltpu.CompilerParams(collective_id=0, has_side_effects=True, vmem_limit_bytes=28 << 20),
        cost_estimate=pl.CostEstimate(flops=10 ** 9, bytes_accessed=100 << 20, transcendentals=0),
        name="exchange",
    )(
        subset, row_start, row_order.reshape(6, LANES), jnp.transpose(axial_weights, (0, 2, 1)), volume, voxel_norm,
        measured.reshape(lines, LANES), ray_norm.reshape(lines, LANES),
    )
    new_volume, residual = pl.pallas_call(
        final_kernel,
        in_specs=[smem, vmem, vmem, vmem, pl.BlockSpec(memory_space=pl.ANY)],
        out_specs=(hbm, hbm),
        out_shape=(jax.ShapeDtypeStruct(volume.shape, f32), jax.ShapeDtypeStruct((lines, LANES), f32)),
        scratch_shapes=[
            pltpu.VMEM((512, LANES), f32), pltpu.VMEM((2, LANES, COLS), bf16), pltpu.VMEM(volume.shape, f32),
            dma((2 * PARTS,)), dma,
        ],
        compiler_params=pltpu.CompilerParams(vmem_limit_bytes=28 << 20),
        cost_estimate=pl.CostEstimate(flops=6 * 64 * DEPTH * COLS, bytes_accessed=4 * 6 * DEPTH * COLS, transcendentals=0),
        name="final",
    )(subset, back, volume_near, scale_near, residual)
    return new_volume, residual.reshape(measured.shape)


def solution(mesh):
    placed = (
        P(("grp", "blk"), None, None),
        P(("grp", "blk"), None, None),
        P("grp", "blk", None),
        P("grp", "blk", None),
        P(("grp", "blk"), None, None),
        P(),
        P(),
        P(),
    )
    return jax.shard_map(
        shards,
        mesh=mesh,
        in_specs=placed,
        out_specs=(P(("grp", "blk"), None, None), P("grp", "blk", None)),
        check_vma=False,
    )
```

```python
import math

import jax
import jax.numpy as jnp
from jax import lax
from jax.experimental import pallas as pl
from jax.experimental.pallas import tpu as pltpu
from jax.sharding import PartitionSpec as P

TOTAL_ANG = 1024
MESH = pl.DeviceIdType.MESH
LANES = 128
ANGLES = 32
FOOT = 8
COLS = 768
DEPTH = 768
CELLS = 1024
ROWS = 192
PARTS = 3
STEP = 0.8 * CELLS / COLS


def halves(value):
    high = value.astype(jnp.bfloat16)
    return high, (value - high.astype(jnp.float32)).astype(jnp.bfloat16)


def dot(left, right):
    return jnp.dot(left, right, preferred_element_type=jnp.float32)


def depth_weight(cell, sine):
    middle = (DEPTH - 1) / 2.0 * (1.0 + 0.8 * sine)
    bump = jnp.maximum(0.0, 1.0 - jnp.abs(cell - middle) / (0.1 * DEPTH))
    return (1.0 + 2.0 * bump) / DEPTH


def centre_of(col, shift):
    return ((CELLS - 1) / 2.0 + STEP * (col - (COLS - 1) / 2.0)) + shift


def pick(tiles, first, last, index):
    inside = index & (LANES - 1)
    tile = index >> 7
    value = None
    for number in range(first, last + 1):
        found = jnp.take_along_axis(tiles[number], inside, axis=1, mode="promise_in_bounds")
        value = found if value is None else jnp.where(tile == number, found, value)
    return value


def span(low, high, tiles):
    first = max(0, min(tiles - 1, math.floor(low) // LANES))
    return first, max(first, min(tiles - 1, math.floor(high) // LANES))


def sines(subset_ref, which):
    chosen = jnp.zeros_like(which)
    for angle in range(ANGLES):
        chosen = jnp.where(which == angle, subset_ref[angle], chosen)
    return jnp.sin(2.0 * math.pi / TOTAL_ANG * chosen.astype(jnp.float32))


def ray_sums(tiles, shift, chunk):
    lane = lax.broadcasted_iota(jnp.int32, (ANGLES, LANES), 1).astype(jnp.float32)
    detector = lane + chunk * LANES
    nearest = jnp.floor((detector - (CELLS - 1) / 2.0 - shift) * (1.0 / STEP) + (COLS - 1) / 2.0)
    middle = (chunk * LANES - (CELLS - 1) / 2.0) / STEP + (COLS - 1) / 2.0
    first, last = span(middle - 49.5, middle + 49.5 + 128 / STEP + 1, COLS // LANES)
    values, total = [0.0, 0.0], 0.0
    for near in (0.0, 1.0):
        col = nearest + near
        weight = jnp.maximum(0.0, 1.0 - jnp.abs(detector - centre_of(col, shift)))
        weight = jnp.where((col >= 0.0) & (col <= COLS - 1.0), weight, 0.0)
        index = col.astype(jnp.int32)
        values = [value + weight * pick(tile, first, last, index) for value, tile in zip(values, tiles)]
        total = total + weight
    return values, total


def spread_rows(tiles, shift, chunk):
    lane = lax.broadcasted_iota(jnp.int32, (ANGLES, LANES), 1).astype(jnp.float32)
    centre = centre_of(lane + chunk * LANES, shift)
    left = jnp.floor(centre)
    middle = (CELLS - 1) / 2.0 + STEP * (chunk * LANES - (COLS - 1) / 2.0)
    first, last = span(middle - 52.5, middle + 52.5 + STEP * 128 + 1, CELLS // LANES)
    value = 0.0
    for near in (0.0, 1.0):
        detector = left + near
        weight = jnp.maximum(0.0, 1.0 - jnp.abs(detector - centre))
        value = value + weight * pick(tiles, first, last, detector.astype(jnp.int32))
    return value


def main_kernel(
    subset_hbm, row_start_hbm, order_hbm, axial_hbm, volume_hbm, scale_hbm, measured_hbm, norm_hbm,
    back, residual, volume, scale, moved, depth,
    subset, row_start, order, axial, measured, norm, rowsum, straight, sino, aux, every, every_aux, every_wide, weight, wide, mean,
    ratio, ahead, from_far, own, linear, arrived,
    volume_sem, small_sem, load_sem, send_sem, recv_sem, aux_send, aux_recv, far_send, far_recv,
    near_send, near_recv, pass_send, pass_recv, aux2_send, aux2_recv, ratio_send, ratio_recv,
    sum_send, sum_recv, out_send, out_recv,
):
    f32, bf16 = jnp.float32, jnp.bfloat16
    block = DEPTH // PARTS
    g, m = lax.axis_index("grp"), lax.axis_index("blk")
    core, y_lo = g % 2, g // 2
    y_hi, z, x = m // 16, (m // 4) % 4, m % 4
    sibling = (y_lo * 2 + (1 - core), m)
    far = ((1 - y_lo) * 2 + core, m)
    far_sibling = (1 - y_lo) * 2 + (1 - core)

    def partner(d):
        flip = d // 16
        return ((y_lo + flip) % 2) * 2 + core, ((y_hi + flip) % 2) * 16 + ((z + (d // 4) % 4) % 4) * 4 + (x + d % 4) % 4

    def source(d):
        flip = d // 16
        return ((y_hi + flip) % 2) * 16 + ((z + 4 - (d // 4) % 4) % 4) * 4 + (x + 4 - d % 4) % 4

    def slot(group, member, members=1):
        return pl.ds(pl.multiple_of((group * 32 + member) * 16, 16), members * 16)

    def remote(source_ref, target_ref, send, recv, device):
        return pltpu.make_async_remote_copy(
            src_ref=source_ref, dst_ref=target_ref, send_sem=send, recv_sem=recv,
            device_id=device, device_id_type=MESH,
        )

    small = [
        pltpu.make_async_copy(subset_hbm, subset, small_sem.at[0]),
        pltpu.make_async_copy(row_start_hbm, row_start, small_sem.at[1]),
        pltpu.make_async_copy(axial_hbm, axial, small_sem.at[2]),
        pltpu.make_async_copy(order_hbm, order, small_sem.at[3]),
    ]
    for copy in small:
        copy.start()
    bring = []
    for q in range(2):
        for part in range(PARTS):
            here = pl.ds(part * block, block)
            bring.append(pltpu.make_async_copy(volume_hbm.at[q, here], volume.at[q, here], volume_sem.at[q * PARTS + part]))
    for copy in bring:
        copy.start()
    load = [
        pltpu.make_async_copy(measured_hbm, measured, load_sem.at[0]),
        pltpu.make_async_copy(norm_hbm, norm, load_sem.at[1]),
        pltpu.make_async_copy(scale_hbm, scale, load_sem.at[2]),
    ]
    for copy in load:
        copy.start()

    barrier = pltpu.get_barrier_semaphore()

    def greet(d, carry):
        pl.semaphore_signal(barrier, inc=1, device_id=partner(d), device_id_type=MESH)
        return carry

    lax.fori_loop(1, 32, greet, 0)
    for device in (sibling, far):
        pl.semaphore_signal(barrier, inc=1, device_id=device, device_id_type=MESH)

    for copy in small:
        copy.wait()
    sine = sines(subset, lax.broadcasted_iota(jnp.int32, (ANGLES, LANES), 0))
    shift = (0.05 * CELLS) * sine
    moved[...] = shift
    tiles, means = [], []
    for q in range(2):
        total = 0.0
        for part in range(PARTS):
            cell = (lax.broadcasted_iota(jnp.int32, (ANGLES, block), 1) + part * block).astype(f32)
            high, low = halves(depth_weight(cell, sine[:, :1]))
            bring[q * PARTS + part].wait()
            volume_high, volume_low = halves(volume[q, part * block:(part + 1) * block, :])
            both = dot(jnp.concatenate([high, low], axis=0), volume_high)
            total = total + (both[:ANGLES] + (both[ANGLES:] + dot(high, volume_low)))
        middle = jnp.sum(total, axis=1, keepdims=True) * (1.0 / COLS)
        means.append(middle)
        total = total - middle
        tiles.append([total[:, t * LANES:(t + 1) * LANES] for t in range(COLS // LANES)])
    for chunk in range(CELLS // LANES):
        values, sums = ray_sums(tiles, shift, chunk)
        rowsum[:, chunk * LANES:(chunk + 1) * LANES] = sums
        for q in range(2):
            straight[pl.ds(q * 8 + chunk, ANGLES, stride=16), :] = values[q]
    sino[...] = straight[...].astype(bf16)

    lane = lax.broadcasted_iota(jnp.int32, (ANGLES, LANES), 1)
    first = jnp.sum(jnp.where(lane == g * 32 + m, row_start[...], 0), axis=1, keepdims=True).astype(f32)
    table = jnp.concatenate([axial[...].reshape(16, ANGLES), jnp.zeros((16, LANES - ANGLES), f32)], axis=1)
    table = jnp.concatenate([table, jnp.zeros((LANES - 16, LANES), f32)], axis=0).T[:ANGLES]
    for number, column in ((16, first), (17, means[0]), (18, means[1])):
        table = jnp.where(lane == number, column, table)
    aux[...] = table.reshape(ANGLES, 1, LANES)

    pl.semaphore_wait(barrier, 33)

    def first_copy(d, group, member):
        device = partner(d)
        return remote(sino.at[slot(0, device[1])], every.at[slot(group, member)], send_sem.at[d], recv_sem.at[d], device)

    def first_aux(d, group, member):
        device = partner(d)
        return remote(aux.at[device[1]], every_aux.at[group * 32 + member], aux_send.at[d], aux_recv.at[d], device)

    def send_rows(d, carry):
        first_copy(d, partner(d)[0], m).start()
        return carry

    def send_aux(d, carry):
        first_aux(d, partner(d)[0], m).start()
        return carry

    lax.fori_loop(1, 32, send_rows, 0)
    lax.fori_loop(1, 32, send_aux, 0)
    every[slot(g, m)] = sino[slot(0, m)]
    every_aux[g * 32 + m] = aux[m]

    def run(group, k):
        return slot(group, ((y_hi + k // 4) % 2) * 16 + ((z + 4 - k % 4) % 4) * 4, 4)

    def to_far(k, group):
        return remote(every.at[run(group, k)], every.at[run(group, k)], far_send.at[k], far_recv.at[k], far)

    def to_near(k, group):
        return remote(every.at[run(group, k)], every.at[run(group, k)], near_send.at[k], near_recv.at[k], sibling)

    def pass_on(k, group):
        return remote(every.at[run(group, k)], every.at[run(group, k)], pass_send.at[k], pass_recv.at[k], sibling)

    def hand(k, carry):
        def arrive(d, carry):
            first_copy(d, g, source(d)).wait_recv()
            return carry

        lax.fori_loop(jnp.where(k == 0, 1, 4 * k), 4 * k + 4, arrive, 0)
        to_far(k, g).start()
        to_near(k, g).start()
        return carry

    lax.fori_loop(0, 8, hand, 0)

    def aux_copy(number, group, device):
        rows = pl.ds(group * 32, 32)
        return remote(every_aux.at[rows], every_aux.at[rows], aux2_send.at[number], aux2_recv.at[number], device)

    def arrive_aux(d, carry):
        first_aux(d, g, source(d)).wait_recv()
        return carry

    lax.fori_loop(1, 32, arrive_aux, 0)
    aux_copy(0, g, far).start()
    aux_copy(1, g, sibling).start()

    def forward_on(k, carry):
        to_far(k, far[0]).wait_recv()
        pass_on(k, far[0]).start()
        return carry

    lax.fori_loop(0, 8, forward_on, 0)
    aux_copy(0, far[0], far).wait_recv()
    aux_copy(2, far[0], sibling).start()
    aux_copy(1, sibling[0], sibling).wait_recv()
    aux_copy(2, far_sibling, sibling).wait_recv()

    table = every_aux[...].reshape(4 * ANGLES, LANES)
    rows = order[...].astype(f32)
    lower = jnp.concatenate([rows[i:i + 1] for i in range(3)], axis=1)
    upper = jnp.concatenate([rows[i:i + 1] for i in range(3, 6)], axis=1)
    offset = jnp.where(y_lo == 0, lower, upper) - table[:, 16:17]
    tall, level = [None] * 8, [None] * 8
    for q in range(2):
        value = jnp.zeros_like(offset)
        for r in range(FOOT):
            value = jnp.where(offset == float(r), table[:, q * FOOT + r:q * FOOT + r + 1], value)
        for h in range(4):
            tall[h * 2 + q] = value[h * 32:(h + 1) * 32]
            level[h * 2 + q] = table[h * 32:(h + 1) * 32, 17 + q:18 + q]
    tall, level = jnp.concatenate(tall, axis=0), jnp.concatenate(level, axis=0)
    constant = jnp.sum(tall * level, axis=0, keepdims=True)
    mean[...] = jnp.broadcast_to(constant, (LANES, 2 * ROWS)).T
    tall_high, tall_low = halves(tall)
    for h in range(4):
        weight[h * 128:h * 128 + 64, :] = tall_high[h * 64:(h + 1) * 64]
        weight[h * 128 + 64:(h + 1) * 128, :] = tall_low[h * 64:(h + 1) * 64]
    wide_high, wide_low = halves(tall.T)
    wide[0] = wide_high
    wide[1] = wide_low

    def settle(k, carry):
        to_near(k, sibling[0]).wait_recv()
        pass_on(k, far_sibling).wait_recv()
        return carry

    lax.fori_loop(0, 8, settle, 0)
    for copy in load[:2]:
        copy.wait()
    every_wide[...] = every[...].astype(f32)

    mine = pl.ds(pl.multiple_of(core * ROWS, ROWS), ROWS)
    other = pl.ds(pl.multiple_of((1 - core) * ROWS, ROWS), ROWS)
    place = jnp.concatenate([wide[0, mine, :], wide[1, mine, :]], axis=0)
    own_mean = mean[mine, :]
    own_sum = rowsum[pl.ds(m, 1), :]
    ahead_weight = weight[pl.ds(pl.multiple_of(far[0] * 128, 128), 128), :]
    own_weight = weight[pl.ds(pl.multiple_of(g * 128, 128), 128), :]

    def to_sibling(pair, rows):
        here = pl.ds(pair * 256, 256)
        return remote(ratio.at[rows, here], ratio.at[rows, here], ratio_send.at[pair], ratio_recv.at[pair], sibling)

    def over(pair):
        return remote(ahead.at[pair], from_far.at[pair], sum_send.at[pair], sum_recv.at[pair], far)

    def forward(pair):
        columns = []
        for chunk in (2 * pair, 2 * pair + 1):
            columns.append(jnp.concatenate(
                [every_wide[pl.ds(h * 512 + q * 8 + chunk, 32, stride=16), :] for h in range(4) for q in range(2)], axis=0
            ))
        both = dot(place, jnp.concatenate(columns, axis=1).astype(bf16))
        value = both[:ROWS] + both[ROWS:]
        for side in range(2):
            chunk = 2 * pair + side
            here = slice(chunk * LANES, (chunk + 1) * LANES)
            found = value[:, side * LANES:(side + 1) * LANES] + own_mean * own_sum[:, here]
            rows = pl.ds(chunk, ROWS, stride=8)
            rest = norm[rows, :] * (measured[rows, :] - found)
            residual[rows, :] = rest
            ratio[mine, here] = rest.astype(bf16)
        to_sibling(pair, mine).start()

    def part_of(weights, pair):
        both = dot(weights, ratio[:, pair * 256:(pair + 1) * 256])
        return both[:64] + both[64:]

    def send_over(pair):
        to_sibling(pair, other).wait_recv()
        ahead[pair] = part_of(ahead_weight, pair).astype(bf16)
        over(pair).start()

    forward(0)
    for pair in range(1, 4):
        forward(pair)
        send_over(pair - 1)
    send_over(3)
    for pair in range(4):
        own[:, pair * 256:(pair + 1) * 256] = part_of(own_weight, pair)
    for pair in range(4):
        over(pair).wait_recv()
        value = own[:, pair * 256:(pair + 1) * 256] + from_far[pair].astype(f32)
        for q in range(2):
            for side in range(2):
                straight[pl.ds(q * 8 + 2 * pair + side, 32, stride=16), :] = value[q * 32:(q + 1) * 32, side * LANES:(side + 1) * LANES]
    linear[...] = straight[...].astype(bf16)

    def last_copy(d, member):
        device = partner(d)
        return remote(linear.at[slot(0, device[1])], arrived.at[slot(0, member)], out_send.at[d], out_recv.at[d], device)

    def give(d, carry):
        last_copy(d, m).start()
        return carry

    lax.fori_loop(1, 32, give, 0)
    arrived[slot(0, m)] = linear[slot(0, m)]

    sine_row = sines(subset, lax.broadcasted_iota(jnp.int32, (8, LANES), 1) % ANGLES)[:1]
    for part in range(PARTS):
        cell = (lax.broadcasted_iota(jnp.int32, (block, LANES), 0) + part * block).astype(f32)
        lane = lax.broadcasted_iota(jnp.int32, (block, LANES), 1)
        value = depth_weight(cell, sine_row)
        high = value.astype(bf16).astype(f32)
        depth[part * block:(part + 1) * block, :] = jnp.where(lane < 2 * ANGLES, high, value - high).astype(bf16)

    def sent(d, carry):
        first_copy(d, partner(d)[0], m).wait_send()
        first_aux(d, partner(d)[0], m).wait_send()
        return carry

    lax.fori_loop(1, 32, sent, 0)

    def sent_runs(k, carry):
        to_far(k, g).wait_send()
        to_near(k, g).wait_send()
        pass_on(k, far[0]).wait_send()
        return carry

    lax.fori_loop(0, 8, sent_runs, 0)
    aux_copy(0, g, far).wait_send()
    aux_copy(1, g, sibling).wait_send()
    aux_copy(2, far[0], sibling).wait_send()
    for pair in range(4):
        to_sibling(pair, mine).wait_send()
        over(pair).wait_send()
    load[2].wait()

    def take(d, carry):
        last_copy(d, source(d)).wait_recv()
        return carry

    lax.fori_loop(1, 32, take, 0)
    back[...] = arrived[...]

    def given(d, carry):
        last_copy(d, m).wait_send()
        return carry

    lax.fori_loop(1, 32, given, 0)


def final_kernel(moved, depth, back, volume, scale, residual_in, new_volume, residual, straight, spread, staged, sems, rest_sem):
    f32 = jnp.float32
    block = DEPTH // PARTS
    keep = pltpu.make_async_copy(residual_in, residual, rest_sem)
    keep.start()
    straight[...] = back[...].astype(f32)
    shift = moved[...]
    copies = []
    for q in range(2):
        tiles = [straight[pl.ds(q * 8 + chunk, ANGLES, stride=16), :] for chunk in range(CELLS // LANES)]
        for chunk in range(COLS // LANES):
            high, low = halves(spread_rows(tiles, shift, chunk))
            here = slice(chunk * LANES, (chunk + 1) * LANES)
            spread[q, 0:ANGLES, here] = high
            spread[q, ANGLES:2 * ANGLES, here] = low
            spread[q, 2 * ANGLES:3 * ANGLES, here] = high
            spread[q, 3 * ANGLES:4 * ANGLES, here] = jnp.zeros_like(high)
        for part in range(PARTS):
            here = slice(part * block, (part + 1) * block)
            update = dot(depth[here, :], spread[q])
            staged[q, here, :] = jnp.maximum(0.0, volume[q, here, :] + scale[q, here, :] * update)
            rows = pl.ds(part * block, block)
            copies.append(pltpu.make_async_copy(staged.at[q, rows], new_volume.at[q, rows], sems.at[q * PARTS + part]))
            copies[-1].start()
    for copy in copies:
        copy.wait()
    keep.wait()


def shards(volume, voxel_norm, measured, ray_norm, axial_weights, row_start, row_order, subset):
    f32, bf16 = jnp.float32, jnp.bfloat16
    vmem = pl.BlockSpec(memory_space=pltpu.VMEM)
    hbm = pl.BlockSpec(memory_space=pltpu.HBM)
    dma = pltpu.SemaphoreType.DMA
    lines = ROWS * 8
    back, residual, volume_near, scale_near, moved, depth = pl.pallas_call(
        main_kernel,
        in_specs=[hbm] * 8,
        out_specs=(vmem,) * 6,
        out_shape=(
            jax.ShapeDtypeStruct((512, LANES), bf16), jax.ShapeDtypeStruct((lines, LANES), f32),
            jax.ShapeDtypeStruct(volume.shape, f32), jax.ShapeDtypeStruct(volume.shape, f32),
            jax.ShapeDtypeStruct((ANGLES, LANES), f32), jax.ShapeDtypeStruct((DEPTH, LANES), bf16),
        ),
        scratch_shapes=[
            pltpu.SMEM((ANGLES,), jnp.int32), pltpu.VMEM((ANGLES, 4 * ANGLES), jnp.int32),
            pltpu.VMEM((6, LANES), jnp.int32), pltpu.VMEM((2, FOOT, ANGLES), f32),
            pltpu.VMEM((lines, LANES), f32), pltpu.VMEM((lines, LANES), f32),
            pltpu.VMEM((ANGLES, CELLS), f32), pltpu.VMEM((512, LANES), f32), pltpu.VMEM((512, LANES), bf16),
            pltpu.VMEM((ANGLES, 1, LANES), f32), pltpu.VMEM((2048, LANES), bf16), pltpu.VMEM((128, 1, LANES), f32),
            pltpu.VMEM((2048, LANES), f32), pltpu.VMEM((512, 2 * ROWS), bf16), pltpu.VMEM((2, 2 * ROWS, 256), bf16),
            pltpu.VMEM((2 * ROWS, LANES), f32), pltpu.VMEM((2 * ROWS, CELLS), bf16),
            pltpu.VMEM((4, 64, 256), bf16), pltpu.VMEM((4, 64, 256), bf16), pltpu.VMEM((64, CELLS), f32),
            pltpu.VMEM((512, LANES), bf16), pltpu.VMEM((512, LANES), bf16),
            dma((2 * PARTS,)), dma((4,)), dma((3,)), dma((32,)), dma((32,)), dma((32,)), dma((32,)), dma((8,)), dma((8,)),
            dma((8,)), dma((8,)), dma((8,)), dma((8,)), dma((3,)), dma((3,)), dma((4,)), dma((4,)),
            dma((4,)), dma((4,)), dma((32,)), dma((32,)),
        ],
        compiler_params=pltpu.CompilerParams(collective_id=0, has_side_effects=True, vmem_limit_bytes=28 << 20),
        cost_estimate=pl.CostEstimate(flops=10 ** 9, bytes_accessed=100 << 20, transcendentals=0),
        name="exchange",
    )(
        *[pltpu.with_memory_space_constraint(array, pltpu.HBM) for array in (
            subset, row_start, row_order.reshape(6, LANES), jnp.transpose(axial_weights, (0, 2, 1)), volume, voxel_norm,
            measured.reshape(lines, LANES), ray_norm.reshape(lines, LANES),
        )]
    )
    new_volume, residual = pl.pallas_call(
        final_kernel,
        in_specs=[vmem, vmem, vmem, vmem, vmem, pl.BlockSpec(memory_space=pl.ANY)],
        out_specs=(hbm, hbm),
        out_shape=(jax.ShapeDtypeStruct(volume.shape, f32), jax.ShapeDtypeStruct((lines, LANES), f32)),
        scratch_shapes=[
            pltpu.VMEM((512, LANES), f32), pltpu.VMEM((2, LANES, COLS), bf16), pltpu.VMEM(volume.shape, f32),
            dma((2 * PARTS,)), dma,
        ],
        compiler_params=pltpu.CompilerParams(vmem_limit_bytes=28 << 20),
        cost_estimate=pl.CostEstimate(flops=6 * 64 * DEPTH * COLS, bytes_accessed=4 * 6 * DEPTH * COLS, transcendentals=0),
        name="final",
    )(moved, depth, back, volume_near, scale_near, residual)
    return new_volume, residual.reshape(measured.shape)


def solution(mesh):
    placed = (
        P(("grp", "blk"), None, None),
        P(("grp", "blk"), None, None),
        P("grp", "blk", None),
        P("grp", "blk", None),
        P(("grp", "blk"), None, None),
        P(),
        P(),
        P(),
    )
    return jax.shard_map(
        shards,
        mesh=mesh,
        in_specs=placed,
        out_specs=(P(("grp", "blk"), None, None), P("grp", "blk", None)),
        check_vma=False,
    )
```

```python
import math

import jax
import jax.numpy as jnp
from jax import lax
from jax.experimental import pallas as pl
from jax.experimental.pallas import tpu as pltpu
from jax.sharding import PartitionSpec as P

TOTAL_ANG = 1024
MESH = pl.DeviceIdType.MESH
LANES = 128
ANGLES = 32
FOOT = 8
COLS = 768
DEPTH = 768
CELLS = 1024
ROWS = 192
PARTS = 3
STEP = 0.8 * CELLS / COLS


def halves(value):
    high = value.astype(jnp.bfloat16)
    return high, (value - high.astype(jnp.float32)).astype(jnp.bfloat16)


def dot(left, right):
    return jnp.dot(left, right, preferred_element_type=jnp.float32)


def depth_weight(cell, sine):
    middle = (DEPTH - 1) / 2.0 * (1.0 + 0.8 * sine)
    bump = jnp.maximum(0.0, 1.0 - jnp.abs(cell - middle) / (0.1 * DEPTH))
    return (1.0 + 2.0 * bump) / DEPTH


def centre_of(col, shift):
    return ((CELLS - 1) / 2.0 + STEP * (col - (COLS - 1) / 2.0)) + shift


def pick(tiles, first, last, index):
    inside = index & (LANES - 1)
    tile = index >> 7
    value = None
    for number in range(first, last + 1):
        found = jnp.take_along_axis(tiles[number], inside, axis=1, mode="promise_in_bounds")
        value = found if value is None else jnp.where(tile == number, found, value)
    return value


def span(low, high, tiles):
    first = max(0, min(tiles - 1, math.floor(low) // LANES))
    return first, max(first, min(tiles - 1, math.floor(high) // LANES))


def sines(subset_ref, which):
    chosen = jnp.zeros_like(which)
    for angle in range(ANGLES):
        chosen = jnp.where(which == angle, subset_ref[angle], chosen)
    return jnp.sin(2.0 * math.pi / TOTAL_ANG * chosen.astype(jnp.float32))


def ray_sums(tiles, shift, chunk):
    lane = lax.broadcasted_iota(jnp.int32, (ANGLES, LANES), 1).astype(jnp.float32)
    detector = lane + chunk * LANES
    nearest = jnp.floor((detector - (CELLS - 1) / 2.0 - shift) * (1.0 / STEP) + (COLS - 1) / 2.0)
    middle = (chunk * LANES - (CELLS - 1) / 2.0) / STEP + (COLS - 1) / 2.0
    first, last = span(middle - 49.5, middle + 49.5 + 128 / STEP + 1, COLS // LANES)
    values, total = [0.0, 0.0], 0.0
    for near in (0.0, 1.0):
        col = nearest + near
        weight = jnp.maximum(0.0, 1.0 - jnp.abs(detector - centre_of(col, shift)))
        weight = jnp.where((col >= 0.0) & (col <= COLS - 1.0), weight, 0.0)
        index = col.astype(jnp.int32)
        values = [value + weight * pick(tile, first, last, index) for value, tile in zip(values, tiles)]
        total = total + weight
    return values, total


def spread_rows(tiles, shift, chunk):
    lane = lax.broadcasted_iota(jnp.int32, (ANGLES, LANES), 1).astype(jnp.float32)
    centre = centre_of(lane + chunk * LANES, shift)
    left = jnp.floor(centre)
    middle = (CELLS - 1) / 2.0 + STEP * (chunk * LANES - (COLS - 1) / 2.0)
    first, last = span(middle - 52.5, middle + 52.5 + STEP * 128 + 1, CELLS // LANES)
    value = 0.0
    for near in (0.0, 1.0):
        detector = left + near
        weight = jnp.maximum(0.0, 1.0 - jnp.abs(detector - centre))
        value = value + weight * pick(tiles, first, last, detector.astype(jnp.int32))
    return value


def main_kernel(
    subset_hbm, row_start_hbm, order_hbm, axial_hbm, volume_hbm, scale_hbm, measured_hbm, norm_hbm,
    back, residual, volume, scale, moved, depth,
    subset, row_start, order, axial, measured, norm, rowsum, straight, sino, aux, every, every_aux, every_wide, weight, wide, mean,
    ratio, linear, arrived,
    volume_sem, small_sem, load_sem, send_sem, recv_sem, aux_send, aux_recv,
    near_send, near_recv, aux2_send, aux2_recv, ratio_send, ratio_recv, out_send, out_recv,
):
    f32, bf16 = jnp.float32, jnp.bfloat16
    block = DEPTH // PARTS
    g, m = lax.axis_index("grp"), lax.axis_index("blk")
    core = g % 2
    y, z, x = (m // 16) * 2 + g // 2, (m // 4) % 4, m % 4
    sibling = (g - core + (1 - core), m)

    def chip(y, z, x):
        return (y % 2) * 2 + core, (y // 2) * 16 + z * 4 + x

    def spread_out(i):
        far_first = lambda j: jnp.where(j == 0, 2, jnp.where(j == 1, 1, jnp.where(j == 2, 3, 0)))
        return far_first(i // 16), far_first((i // 4) % 4), far_first(i % 4)

    def partner(i):
        dy, dz, dx = spread_out(i)
        return chip((y + dy) % 4, (z + dz) % 4, (x + dx) % 4)

    def source(i):
        dy, dz, dx = spread_out(i)
        return ((y + 4 - dy) % 4) * 16 + ((z + 4 - dz) % 4) * 4 + (x + 4 - dx) % 4

    here_chip = y * 16 + z * 4 + x

    def slot(number, members=1):
        return pl.ds(pl.multiple_of(number * 16, 16), members * 16)

    def remote(source_ref, target_ref, send, recv, device):
        return pltpu.make_async_remote_copy(
            src_ref=source_ref, dst_ref=target_ref, send_sem=send, recv_sem=recv,
            device_id=device, device_id_type=MESH,
        )

    small = [
        pltpu.make_async_copy(subset_hbm, subset, small_sem.at[0]),
        pltpu.make_async_copy(row_start_hbm, row_start, small_sem.at[1]),
        pltpu.make_async_copy(axial_hbm, axial, small_sem.at[2]),
        pltpu.make_async_copy(order_hbm, order, small_sem.at[3]),
    ]
    for copy in small:
        copy.start()
    bring = []
    for q in range(2):
        for part in range(PARTS):
            here = pl.ds(part * block, block)
            bring.append(pltpu.make_async_copy(volume_hbm.at[q, here], volume.at[q, here], volume_sem.at[q * PARTS + part]))
    for copy in bring:
        copy.start()
    load = [
        pltpu.make_async_copy(measured_hbm, measured, load_sem.at[0]),
        pltpu.make_async_copy(norm_hbm, norm, load_sem.at[1]),
        pltpu.make_async_copy(scale_hbm, scale, load_sem.at[2]),
    ]
    barrier = pltpu.get_barrier_semaphore()

    def greet(d, carry):
        pl.semaphore_signal(barrier, inc=1, device_id=partner(d), device_id_type=MESH)
        return carry

    lax.fori_loop(0, 63, greet, 0)
    pl.semaphore_signal(barrier, inc=1, device_id=sibling, device_id_type=MESH)

    for copy in small:
        copy.wait()
    sine = sines(subset, lax.broadcasted_iota(jnp.int32, (ANGLES, LANES), 0))
    shift = (0.05 * CELLS) * sine
    moved[...] = shift
    tiles, means = [], []
    for q in range(2):
        total = 0.0
        for part in range(PARTS):
            cell = (lax.broadcasted_iota(jnp.int32, (ANGLES, block), 1) + part * block).astype(f32)
            high, low = halves(depth_weight(cell, sine[:, :1]))
            bring[q * PARTS + part].wait()
            volume_high, volume_low = halves(volume[q, part * block:(part + 1) * block, :])
            both = dot(jnp.concatenate([high, low], axis=0), volume_high)
            total = total + (both[:ANGLES] + (both[ANGLES:] + dot(high, volume_low)))
        middle = jnp.sum(total, axis=1, keepdims=True) * (1.0 / COLS)
        means.append(middle)
        total = total - middle
        tiles.append([total[:, t * LANES:(t + 1) * LANES] for t in range(COLS // LANES)])
    for copy in load:
        copy.start()
    for chunk in range(CELLS // LANES):
        values, sums = ray_sums(tiles, shift, chunk)
        rowsum[:, chunk * LANES:(chunk + 1) * LANES] = sums
        for q in range(2):
            straight[pl.ds(q * 8 + chunk, ANGLES, stride=16), :] = values[q]
    sino[...] = straight[:512].astype(bf16)

    lane = lax.broadcasted_iota(jnp.int32, (ANGLES, LANES), 1)
    first = jnp.sum(jnp.where(lane == g * 32 + m, row_start[...], 0), axis=1, keepdims=True).astype(f32)
    table = jnp.concatenate([axial[...].reshape(16, ANGLES), jnp.zeros((16, LANES - ANGLES), f32)], axis=1)
    table = jnp.concatenate([table, jnp.zeros((LANES - 16, LANES), f32)], axis=0).T[:ANGLES]
    for number, column in ((16, first), (17, means[0]), (18, means[1])):
        table = jnp.where(lane == number, column, table)
    aux[...] = table.reshape(ANGLES, 1, LANES)

    pl.semaphore_wait(barrier, 64)

    def first_copy(i, number):
        device = partner(i)
        return remote(sino.at[slot(device[1])], every.at[slot(core * 64 + number)], send_sem.at[i], recv_sem.at[i], device)

    def first_aux(i, number):
        device = partner(i)
        return remote(aux.at[device[1]], every_aux.at[core * 64 + number], aux_send.at[i], aux_recv.at[i], device)

    def send(i, carry):
        first_aux(i, here_chip).start()
        first_copy(i, here_chip).start()
        return carry

    lax.fori_loop(0, 63, send, 0)
    every[slot(core * 64 + here_chip)] = sino[slot(m)]
    every_aux[core * 64 + here_chip] = aux[m]

    def near_rows(number, side):
        rows = slot(side * 64 + ((y + 4 - number) % 4) * 16, 16)
        return remote(every.at[rows], every.at[rows], near_send.at[number], near_recv.at[number], sibling)

    def near_aux(side):
        rows = pl.ds(side * 64, 64)
        return remote(every_aux.at[rows], every_aux.at[rows], aux2_send.at[0], aux2_recv.at[0], sibling)

    def arrive_aux(i, carry):
        first_aux(i, source(i)).wait_recv()
        return carry

    def arrive(i, carry):
        first_copy(i, source(i)).wait_recv()
        return carry

    lax.fori_loop(0, 63, arrive_aux, 0)
    near_aux(core).start()
    for number, order_of in ((0, 3), (1, 1), (3, 2), (2, 0)):
        lax.fori_loop(order_of * 16, order_of * 16 + (15 if number == 0 else 16), arrive, 0)
        near_rows(number, core).start()
    near_aux(1 - core).wait_recv()

    table = every_aux[...].reshape(4 * ANGLES, LANES)
    rows = order[...].astype(f32)
    lower = jnp.concatenate([rows[i:i + 1] for i in range(3)], axis=1)
    upper = jnp.concatenate([rows[i:i + 1] for i in range(3, 6)], axis=1)
    offset = jnp.where(y % 2 == 0, lower, upper) - table[:, 16:17]
    tall, level = [None] * 4, [None] * 4
    for q in range(2):
        value = jnp.zeros_like(offset)
        for r in range(FOOT):
            value = jnp.where(offset == float(r), table[:, q * FOOT + r:q * FOOT + r + 1], value)
        for side in range(2):
            tall[side * 2 + q] = value[side * 64:(side + 1) * 64]
            level[side * 2 + q] = table[side * 64:(side + 1) * 64, 17 + q:18 + q]
    tall, level = jnp.concatenate(tall, axis=0), jnp.concatenate(level, axis=0)
    constant = jnp.sum(tall * level, axis=0, keepdims=True)
    mean[...] = jnp.broadcast_to(constant, (LANES, 2 * ROWS)).T
    tall_high, tall_low = halves(tall)
    for side in range(2):
        weight[side * 256:side * 256 + 128, :] = tall_high[side * 128:(side + 1) * 128]
        weight[side * 256 + 128:(side + 1) * 256, :] = tall_low[side * 128:(side + 1) * 128]
    wide_high, wide_low = halves(tall.T)
    wide[0] = wide_high
    wide[1] = wide_low

    for number in range(4):
        near_rows(number, 1 - core).wait_recv()
    for copy in load[:2]:
        copy.wait()
    every_wide[...] = every[...].astype(f32)

    mine = pl.ds(pl.multiple_of(core * ROWS, ROWS), ROWS)
    other = pl.ds(pl.multiple_of((1 - core) * ROWS, ROWS), ROWS)
    place = jnp.concatenate([wide[0, mine, :], wide[1, mine, :]], axis=0)
    own_mean = mean[mine, :]
    own_sum = rowsum[pl.ds(m, 1), :]
    own_weight = weight[pl.ds(pl.multiple_of(core * 256, 256), 256), :]

    def to_sibling(pair, rows):
        here = pl.ds(pair * 256, 256)
        return remote(ratio.at[rows, here], ratio.at[rows, here], ratio_send.at[pair], ratio_recv.at[pair], sibling)

    def forward(pair):
        columns = []
        for chunk in (2 * pair, 2 * pair + 1):
            columns.append(jnp.concatenate(
                [every_wide[pl.ds(side * 1024 + q * 8 + chunk, 64, stride=16), :] for side in range(2) for q in range(2)], axis=0
            ))
        both = dot(place, jnp.concatenate(columns, axis=1).astype(bf16))
        value = both[:ROWS] + both[ROWS:]
        for side in range(2):
            chunk = 2 * pair + side
            here = slice(chunk * LANES, (chunk + 1) * LANES)
            found = value[:, side * LANES:(side + 1) * LANES] + own_mean * own_sum[:, here]
            rows = pl.ds(chunk, ROWS, stride=8)
            rest = norm[rows, :] * (measured[rows, :] - found)
            residual[rows, :] = rest
            ratio[mine, here] = rest.astype(bf16)
        to_sibling(pair, mine).start()

    def collect(pair):
        to_sibling(pair, other).wait_recv()
        both = dot(own_weight, ratio[:, pair * 256:(pair + 1) * 256])
        value = both[:128] + both[128:]
        for q in range(2):
            for side in range(2):
                straight[pl.ds(q * 8 + 2 * pair + side, 64, stride=16), :] = value[q * 64:(q + 1) * 64, side * LANES:(side + 1) * LANES]

    forward(0)
    for pair in range(1, 4):
        forward(pair)
        collect(pair - 1)
    collect(3)

    def slot_of(i):
        dy, dz, dx = spread_out(i)
        return ((y + dy) % 4) * 16 + ((z + dz) % 4) * 4 + (x + dx) % 4

    def last_copy(i, number):
        return remote(
            linear.at[slot(slot_of(i))], arrived.at[slot(number)], out_send.at[i], out_recv.at[i], partner(i)
        )

    arrival = (y % 2) * 32 + m

    def give(i, carry):
        rows = slot(slot_of(i))
        linear[rows] = straight[rows].astype(bf16)
        last_copy(i, arrival).start()
        return carry

    lax.fori_loop(0, 63, give, 0)
    arrived[slot(arrival)] = straight[slot(here_chip)].astype(bf16)

    sine_row = sines(subset, lax.broadcasted_iota(jnp.int32, (8, LANES), 1) % ANGLES)[:1]
    for part in range(PARTS):
        cell = (lax.broadcasted_iota(jnp.int32, (block, LANES), 0) + part * block).astype(f32)
        lane = lax.broadcasted_iota(jnp.int32, (block, LANES), 1)
        value = depth_weight(cell, sine_row)
        high = value.astype(bf16).astype(f32)
        depth[part * block:(part + 1) * block, :] = jnp.where(lane < 2 * ANGLES, high, value - high).astype(bf16)

    def sent(i, carry):
        first_copy(i, here_chip).wait_send()
        first_aux(i, here_chip).wait_send()
        return carry

    lax.fori_loop(0, 63, sent, 0)
    near_aux(core).wait_send()
    for number in range(4):
        near_rows(number, core).wait_send()
        to_sibling(number, mine).wait_send()
    load[2].wait()

    def take(i, carry):
        dy, dz, dx = spread_out(i)
        y2, z2, x2 = (y + 4 - dy) % 4, (z + 4 - dz) % 4, (x + 4 - dx) % 4
        last_copy(i, (y2 % 2) * 32 + (y2 // 2) * 16 + z2 * 4 + x2).wait_recv()
        return carry

    lax.fori_loop(0, 63, take, 0)
    back[...] = arrived[...]

    def given(i, carry):
        last_copy(i, arrival).wait_send()
        return carry

    lax.fori_loop(0, 63, given, 0)


def final_kernel(moved, depth, back, volume, scale, residual_in, new_volume, residual, straight, spread, staged, sems, rest_sem):
    f32 = jnp.float32
    block = DEPTH // PARTS
    keep = pltpu.make_async_copy(residual_in, residual, rest_sem)
    keep.start()
    straight[...] = back[:512].astype(f32) + back[512:].astype(f32)
    shift = moved[...]
    copies = []
    for q in range(2):
        tiles = [straight[pl.ds(q * 8 + chunk, ANGLES, stride=16), :] for chunk in range(CELLS // LANES)]
        for chunk in range(COLS // LANES):
            high, low = halves(spread_rows(tiles, shift, chunk))
            here = slice(chunk * LANES, (chunk + 1) * LANES)
            spread[q, 0:ANGLES, here] = high
            spread[q, ANGLES:2 * ANGLES, here] = low
            spread[q, 2 * ANGLES:3 * ANGLES, here] = high
            spread[q, 3 * ANGLES:4 * ANGLES, here] = jnp.zeros_like(high)
        for part in range(PARTS):
            here = slice(part * block, (part + 1) * block)
            update = dot(depth[here, :], spread[q])
            staged[q, here, :] = jnp.maximum(0.0, volume[q, here, :] + scale[q, here, :] * update)
            rows = pl.ds(part * block, block)
            copies.append(pltpu.make_async_copy(staged.at[q, rows], new_volume.at[q, rows], sems.at[q * PARTS + part]))
            copies[-1].start()
    for copy in copies:
        copy.wait()
    keep.wait()


def shards(volume, voxel_norm, measured, ray_norm, axial_weights, row_start, row_order, subset):
    f32, bf16 = jnp.float32, jnp.bfloat16
    vmem = pl.BlockSpec(memory_space=pltpu.VMEM)
    hbm = pl.BlockSpec(memory_space=pltpu.HBM)
    dma = pltpu.SemaphoreType.DMA
    lines = ROWS * 8
    back, residual, volume_near, scale_near, moved, depth = pl.pallas_call(
        main_kernel,
        in_specs=[hbm] * 8,
        out_specs=(vmem,) * 6,
        out_shape=(
            jax.ShapeDtypeStruct((1024, LANES), bf16), jax.ShapeDtypeStruct((lines, LANES), f32),
            jax.ShapeDtypeStruct(volume.shape, f32), jax.ShapeDtypeStruct(volume.shape, f32),
            jax.ShapeDtypeStruct((ANGLES, LANES), f32), jax.ShapeDtypeStruct((DEPTH, LANES), bf16),
        ),
        scratch_shapes=[
            pltpu.SMEM((ANGLES,), jnp.int32), pltpu.VMEM((ANGLES, 4 * ANGLES), jnp.int32),
            pltpu.VMEM((6, LANES), jnp.int32), pltpu.VMEM((2, FOOT, ANGLES), f32),
            pltpu.VMEM((lines, LANES), f32), pltpu.VMEM((lines, LANES), f32),
            pltpu.VMEM((ANGLES, CELLS), f32), pltpu.VMEM((1024, LANES), f32), pltpu.VMEM((512, LANES), bf16),
            pltpu.VMEM((ANGLES, 1, LANES), f32), pltpu.VMEM((2048, LANES), bf16), pltpu.VMEM((128, 1, LANES), f32),
            pltpu.VMEM((2048, LANES), f32), pltpu.VMEM((512, 2 * ROWS), bf16), pltpu.VMEM((2, 2 * ROWS, 256), bf16),
            pltpu.VMEM((2 * ROWS, LANES), f32), pltpu.VMEM((2 * ROWS, CELLS), bf16),
            pltpu.VMEM((1024, LANES), bf16), pltpu.VMEM((1024, LANES), bf16),
            dma((2 * PARTS,)), dma((4,)), dma((3,)), dma((63,)), dma((63,)), dma((63,)), dma((63,)),
            dma((4,)), dma((4,)), dma((1,)), dma((1,)), dma((4,)), dma((4,)), dma((63,)), dma((63,)),
        ],
        compiler_params=pltpu.CompilerParams(collective_id=0, has_side_effects=True, vmem_limit_bytes=28 << 20),
        cost_estimate=pl.CostEstimate(flops=10 ** 9, bytes_accessed=100 << 20, transcendentals=0),
        name="exchange",
    )(
        *[pltpu.with_memory_space_constraint(array, pltpu.HBM) for array in (
            subset, row_start, row_order.reshape(6, LANES), jnp.transpose(axial_weights, (0, 2, 1)), volume, voxel_norm,
            measured.reshape(lines, LANES), ray_norm.reshape(lines, LANES),
        )]
    )
    new_volume, residual = pl.pallas_call(
        final_kernel,
        in_specs=[vmem, vmem, vmem, vmem, vmem, pl.BlockSpec(memory_space=pl.ANY)],
        out_specs=(hbm, hbm),
        out_shape=(jax.ShapeDtypeStruct(volume.shape, f32), jax.ShapeDtypeStruct((lines, LANES), f32)),
        scratch_shapes=[
            pltpu.VMEM((512, LANES), f32), pltpu.VMEM((2, LANES, COLS), bf16), pltpu.VMEM(volume.shape, f32),
            dma((2 * PARTS,)), dma,
        ],
        compiler_params=pltpu.CompilerParams(vmem_limit_bytes=28 << 20),
        cost_estimate=pl.CostEstimate(flops=6 * 64 * DEPTH * COLS, bytes_accessed=4 * 6 * DEPTH * COLS, transcendentals=0),
        name="final",
    )(moved, depth, back, volume_near, scale_near, residual)
    return new_volume, residual.reshape(measured.shape)


def solution(mesh):
    placed = (
        P(("grp", "blk"), None, None),
        P(("grp", "blk"), None, None),
        P("grp", "blk", None),
        P("grp", "blk", None),
        P(("grp", "blk"), None, None),
        P(),
        P(),
        P(),
    )
    return jax.shard_map(
        shards,
        mesh=mesh,
        in_specs=placed,
        out_specs=(P(("grp", "blk"), None, None), P("grp", "blk", None)),
        check_vma=False,
    )
```

```python
import itertools
import math

import jax
import jax.numpy as jnp
from jax import lax
from jax.experimental import pallas as pl
from jax.experimental.pallas import tpu as pltpu
from jax.sharding import PartitionSpec as P

TOTAL_ANG = 1024
MESH = pl.DeviceIdType.MESH
LANES = 128
ANGLES = 32
FOOT = 8
COLS = 768
DEPTH = 768
CELLS = 1024
ROWS = 192
PARTS = 3
OFFSETS = sorted(
    itertools.product(range(4), repeat=3), key=lambda offset: -sum(min(step, 4 - step) for step in offset)
)[:-1]
STEP = 0.8 * CELLS / COLS


def halves(value):
    high = value.astype(jnp.bfloat16)
    return high, (value - high.astype(jnp.float32)).astype(jnp.bfloat16)


def dot(left, right):
    return jnp.dot(left, right, preferred_element_type=jnp.float32)


def depth_weight(cell, sine):
    middle = (DEPTH - 1) / 2.0 * (1.0 + 0.8 * sine)
    bump = jnp.maximum(0.0, 1.0 - jnp.abs(cell - middle) / (0.1 * DEPTH))
    return (1.0 + 2.0 * bump) / DEPTH


def centre_of(col, shift):
    return ((CELLS - 1) / 2.0 + STEP * (col - (COLS - 1) / 2.0)) + shift


def pick(tiles, first, last, index):
    inside = index & (LANES - 1)
    tile = index >> 7
    value = None
    for number in range(first, last + 1):
        found = jnp.take_along_axis(tiles[number], inside, axis=1, mode="promise_in_bounds")
        value = found if value is None else jnp.where(tile == number, found, value)
    return value


def span(low, high, tiles):
    first = max(0, min(tiles - 1, math.floor(low) // LANES))
    return first, max(first, min(tiles - 1, math.floor(high) // LANES))


def sines(subset_ref, which):
    chosen = jnp.zeros_like(which)
    for angle in range(ANGLES):
        chosen = jnp.where(which == angle, subset_ref[angle], chosen)
    return jnp.sin(2.0 * math.pi / TOTAL_ANG * chosen.astype(jnp.float32))


def ray_sums(tiles, shift, chunk):
    lane = lax.broadcasted_iota(jnp.int32, (ANGLES, LANES), 1).astype(jnp.float32)
    detector = lane + chunk * LANES
    nearest = jnp.floor((detector - (CELLS - 1) / 2.0 - shift) * (1.0 / STEP) + (COLS - 1) / 2.0)
    middle = (chunk * LANES - (CELLS - 1) / 2.0) / STEP + (COLS - 1) / 2.0
    first, last = span(middle - 49.5, middle + 49.5 + 128 / STEP + 1, COLS // LANES)
    values, total = [0.0, 0.0], 0.0
    for near in (0.0, 1.0):
        col = nearest + near
        weight = jnp.maximum(0.0, 1.0 - jnp.abs(detector - centre_of(col, shift)))
        weight = jnp.where((col >= 0.0) & (col <= COLS - 1.0), weight, 0.0)
        index = col.astype(jnp.int32)
        values = [value + weight * pick(tile, first, last, index) for value, tile in zip(values, tiles)]
        total = total + weight
    return values, total


def spread_rows(tiles, shift, chunk):
    lane = lax.broadcasted_iota(jnp.int32, (ANGLES, LANES), 1).astype(jnp.float32)
    centre = centre_of(lane + chunk * LANES, shift)
    left = jnp.floor(centre)
    middle = (CELLS - 1) / 2.0 + STEP * (chunk * LANES - (COLS - 1) / 2.0)
    first, last = span(middle - 52.5, middle + 52.5 + STEP * 128 + 1, CELLS // LANES)
    value = 0.0
    for near in (0.0, 1.0):
        detector = left + near
        weight = jnp.maximum(0.0, 1.0 - jnp.abs(detector - centre))
        value = value + weight * pick(tiles, first, last, detector.astype(jnp.int32))
    return value


def main_kernel(
    subset_hbm, row_start_hbm, order_hbm, axial_hbm, volume_hbm, scale_hbm, measured_hbm, norm_hbm,
    back, residual, volume, scale, moved, depth,
    subset, row_start, order, axial, measured, norm, rowsum, straight, sino, aux, every, every_aux, every_wide, weight, wide, mean,
    ratio, linear, arrived,
    volume_sem, small_sem, load_sem, send_sem, recv_sem, aux_send, aux_recv,
    near_send, near_recv, aux2_send, aux2_recv, ratio_send, ratio_recv, out_send, out_recv,
):
    f32, bf16 = jnp.float32, jnp.bfloat16
    block = DEPTH // PARTS
    g, m = lax.axis_index("grp"), lax.axis_index("blk")
    core = g % 2
    y, z, x = (m // 16) * 2 + g // 2, (m // 4) % 4, m % 4
    sibling = (g - core + (1 - core), m)

    ys, zs, xs = ([(place + step) % 4 for step in range(4)] for place in (y, z, x))
    group_of = [place % 2 * 2 + core for place in ys]
    plane_of = [place // 2 * 16 for place in ys]
    line_of = [[row * 4 + col for col in xs] for row in zs]

    def partner(offset):
        return group_of[offset[0]], plane_of[offset[0]] + line_of[offset[1]][offset[2]]

    def partner_slot(offset):
        return ys[offset[0]] * 16 + line_of[offset[1]][offset[2]]

    def arrived_all(ref, sem):
        return pltpu.make_async_copy(ref, ref, sem)

    here_chip = y * 16 + z * 4 + x

    def slot(number, members=1):
        return pl.ds(pl.multiple_of(number * 16, 16), members * 16)

    def remote(source_ref, target_ref, send, recv, device):
        return pltpu.make_async_remote_copy(
            src_ref=source_ref, dst_ref=target_ref, send_sem=send, recv_sem=recv,
            device_id=device, device_id_type=MESH,
        )

    small = [
        pltpu.make_async_copy(subset_hbm, subset, small_sem.at[0]),
        pltpu.make_async_copy(row_start_hbm, row_start, small_sem.at[1]),
        pltpu.make_async_copy(axial_hbm, axial, small_sem.at[2]),
        pltpu.make_async_copy(order_hbm, order, small_sem.at[3]),
    ]
    for copy in small:
        copy.start()
    bring = []
    for q in range(2):
        for part in range(PARTS):
            here = pl.ds(part * block, block)
            bring.append(pltpu.make_async_copy(volume_hbm.at[q, here], volume.at[q, here], volume_sem.at[q * PARTS + part]))
    for copy in bring:
        copy.start()
    load = [
        pltpu.make_async_copy(measured_hbm, measured, load_sem.at[0]),
        pltpu.make_async_copy(norm_hbm, norm, load_sem.at[1]),
        pltpu.make_async_copy(scale_hbm, scale, load_sem.at[2]),
    ]
    barrier = pltpu.get_barrier_semaphore()

    for offset in OFFSETS:
        pl.semaphore_signal(barrier, inc=1, device_id=partner(offset), device_id_type=MESH)
    pl.semaphore_signal(barrier, inc=1, device_id=sibling, device_id_type=MESH)

    for copy in small:
        copy.wait()
    sine = sines(subset, lax.broadcasted_iota(jnp.int32, (ANGLES, LANES), 0))
    shift = (0.05 * CELLS) * sine
    moved[...] = shift
    tiles, means = [], []
    for q in range(2):
        total = 0.0
        for part in range(PARTS):
            cell = (lax.broadcasted_iota(jnp.int32, (ANGLES, block), 1) + part * block).astype(f32)
            high, low = halves(depth_weight(cell, sine[:, :1]))
            bring[q * PARTS + part].wait()
            volume_high, volume_low = halves(volume[q, part * block:(part + 1) * block, :])
            both = dot(jnp.concatenate([high, low], axis=0), volume_high)
            total = total + (both[:ANGLES] + (both[ANGLES:] + dot(high, volume_low)))
        middle = jnp.sum(total, axis=1, keepdims=True) * (1.0 / COLS)
        means.append(middle)
        total = total - middle
        tiles.append([total[:, t * LANES:(t + 1) * LANES] for t in range(COLS // LANES)])
    for copy in load:
        copy.start()
    for chunk in range(CELLS // LANES):
        values, sums = ray_sums(tiles, shift, chunk)
        rowsum[:, chunk * LANES:(chunk + 1) * LANES] = sums
        for q in range(2):
            straight[pl.ds(q * 8 + chunk, ANGLES, stride=16), :] = values[q]
    sino[...] = straight[:512].astype(bf16)

    lane = lax.broadcasted_iota(jnp.int32, (ANGLES, LANES), 1)
    first = jnp.sum(jnp.where(lane == g * 32 + m, row_start[...], 0), axis=1, keepdims=True).astype(f32)
    table = jnp.concatenate([axial[...].reshape(16, ANGLES), jnp.zeros((16, LANES - ANGLES), f32)], axis=1)
    table = jnp.concatenate([table, jnp.zeros((LANES - 16, LANES), f32)], axis=0).T[:ANGLES]
    for number, column in ((16, first), (17, means[0]), (18, means[1])):
        table = jnp.where(lane == number, column, table)
    aux[...] = table.reshape(ANGLES, 1, LANES)

    pl.semaphore_wait(barrier, 64)

    for offset in OFFSETS:
        device = partner(offset)
        remote(
            aux.at[device[1]], every_aux.at[core * 64 + here_chip], aux_send.at[0], aux_recv.at[0], device
        ).start()
        remote(
            sino.at[slot(device[1])], every.at[slot(core * 64 + here_chip)], send_sem.at[0], recv_sem.at[offset[0]], device
        ).start()
    every[slot(core * 64 + here_chip)] = sino[slot(m)]
    every_aux[core * 64 + here_chip] = aux[m]

    def near_rows(number, side):
        rows = slot(side * 64 + ys[(4 - number) % 4] * 16, 16)
        return remote(every.at[rows], every.at[rows], near_send.at[number], near_recv.at[number], sibling)

    def near_aux(side):
        rows = pl.ds(side * 64, 64)
        return remote(every_aux.at[rows], every_aux.at[rows], aux2_send.at[0], aux2_recv.at[0], sibling)

    arrived_all(every_aux.at[pl.ds(core * 64, 63)], aux_recv.at[0]).wait()
    near_aux(core).start()
    for number in (0, 1, 3, 2):
        rows = slot(core * 64 + ys[(4 - number) % 4] * 16, 15 if number == 0 else 16)
        arrived_all(every.at[rows], recv_sem.at[number]).wait()
        near_rows(number, core).start()
    near_aux(1 - core).wait_recv()

    table = every_aux[...].reshape(4 * ANGLES, LANES)
    rows = order[...].astype(f32)
    lower = jnp.concatenate([rows[i:i + 1] for i in range(3)], axis=1)
    upper = jnp.concatenate([rows[i:i + 1] for i in range(3, 6)], axis=1)
    offset = jnp.where(y % 2 == 0, lower, upper) - table[:, 16:17]
    tall, level = [None] * 4, [None] * 4
    for q in range(2):
        value = jnp.zeros_like(offset)
        for r in range(FOOT):
            value = jnp.where(offset == float(r), table[:, q * FOOT + r:q * FOOT + r + 1], value)
        for side in range(2):
            tall[side * 2 + q] = value[side * 64:(side + 1) * 64]
            level[side * 2 + q] = table[side * 64:(side + 1) * 64, 17 + q:18 + q]
    tall, level = jnp.concatenate(tall, axis=0), jnp.concatenate(level, axis=0)
    constant = jnp.sum(tall * level, axis=0, keepdims=True)
    mean[...] = jnp.broadcast_to(constant, (LANES, 2 * ROWS)).T
    tall_high, tall_low = halves(tall)
    for side in range(2):
        weight[side * 256:side * 256 + 128, :] = tall_high[side * 128:(side + 1) * 128]
        weight[side * 256 + 128:(side + 1) * 256, :] = tall_low[side * 128:(side + 1) * 128]
    wide_high, wide_low = halves(tall.T)
    wide[0] = wide_high
    wide[1] = wide_low

    for number in range(4):
        near_rows(number, 1 - core).wait_recv()
    for copy in load[:2]:
        copy.wait()
    every_wide[...] = every[...].astype(f32)

    mine = pl.ds(pl.multiple_of(core * ROWS, ROWS), ROWS)
    other = pl.ds(pl.multiple_of((1 - core) * ROWS, ROWS), ROWS)
    place = jnp.concatenate([wide[0, mine, :], wide[1, mine, :]], axis=0)
    own_mean = mean[mine, :]
    own_sum = rowsum[pl.ds(m, 1), :]
    own_weight = weight[pl.ds(pl.multiple_of(core * 256, 256), 256), :]

    def to_sibling(pair, rows):
        here = pl.ds(pair * 256, 256)
        return remote(ratio.at[rows, here], ratio.at[rows, here], ratio_send.at[pair], ratio_recv.at[pair], sibling)

    def forward(pair):
        columns = []
        for chunk in (2 * pair, 2 * pair + 1):
            columns.append(jnp.concatenate(
                [every_wide[pl.ds(side * 1024 + q * 8 + chunk, 64, stride=16), :] for side in range(2) for q in range(2)], axis=0
            ))
        both = dot(place, jnp.concatenate(columns, axis=1).astype(bf16))
        value = both[:ROWS] + both[ROWS:]
        for side in range(2):
            chunk = 2 * pair + side
            here = slice(chunk * LANES, (chunk + 1) * LANES)
            found = value[:, side * LANES:(side + 1) * LANES] + own_mean * own_sum[:, here]
            rows = pl.ds(chunk, ROWS, stride=8)
            rest = norm[rows, :] * (measured[rows, :] - found)
            residual[rows, :] = rest
            ratio[mine, here] = rest.astype(bf16)
        to_sibling(pair, mine).start()

    def collect(pair):
        to_sibling(pair, other).wait_recv()
        both = dot(own_weight, ratio[:, pair * 256:(pair + 1) * 256])
        value = both[:128] + both[128:]
        for q in range(2):
            for side in range(2):
                straight[pl.ds(q * 8 + 2 * pair + side, 64, stride=16), :] = value[q * 64:(q + 1) * 64, side * LANES:(side + 1) * LANES]

    forward(0)
    for pair in range(1, 4):
        forward(pair)
        collect(pair - 1)
    collect(3)

    arrival = (y % 2) * 32 + m
    for offset in OFFSETS:
        rows = slot(partner_slot(offset))
        linear[rows] = straight[rows].astype(bf16)
        remote(linear.at[rows], arrived.at[slot(arrival)], out_send.at[0], out_recv.at[0], partner(offset)).start()
    arrived[slot(arrival)] = straight[slot(here_chip)].astype(bf16)

    sine_row = sines(subset, lax.broadcasted_iota(jnp.int32, (8, LANES), 1) % ANGLES)[:1]
    for part in range(PARTS):
        cell = (lax.broadcasted_iota(jnp.int32, (block, LANES), 0) + part * block).astype(f32)
        lane = lax.broadcasted_iota(jnp.int32, (block, LANES), 1)
        value = depth_weight(cell, sine_row)
        high = value.astype(bf16).astype(f32)
        depth[part * block:(part + 1) * block, :] = jnp.where(lane < 2 * ANGLES, high, value - high).astype(bf16)

    arrived_all(every.at[slot(0, 63)], send_sem.at[0]).wait()
    arrived_all(every_aux.at[pl.ds(0, 63)], aux_send.at[0]).wait()
    near_aux(core).wait_send()
    for number in range(4):
        near_rows(number, core).wait_send()
        to_sibling(number, mine).wait_send()
    load[2].wait()

    arrived_all(arrived.at[slot(0, 63)], out_recv.at[0]).wait()
    back[...] = arrived[...]
    arrived_all(linear.at[slot(0, 63)], out_send.at[0]).wait()


def final_kernel(moved, depth, back, volume, scale, residual_in, new_volume, residual, straight, spread, staged, sems, rest_sem):
    f32 = jnp.float32
    block = DEPTH // PARTS
    keep = pltpu.make_async_copy(residual_in, residual, rest_sem)
    keep.start()
    straight[...] = back[:512].astype(f32) + back[512:].astype(f32)
    shift = moved[...]
    copies = []
    for q in range(2):
        tiles = [straight[pl.ds(q * 8 + chunk, ANGLES, stride=16), :] for chunk in range(CELLS // LANES)]
        for chunk in range(COLS // LANES):
            high, low = halves(spread_rows(tiles, shift, chunk))
            here = slice(chunk * LANES, (chunk + 1) * LANES)
            spread[q, 0:ANGLES, here] = high
            spread[q, ANGLES:2 * ANGLES, here] = low
            spread[q, 2 * ANGLES:3 * ANGLES, here] = high
            spread[q, 3 * ANGLES:4 * ANGLES, here] = jnp.zeros_like(high)
        for part in range(PARTS):
            here = slice(part * block, (part + 1) * block)
            update = dot(depth[here, :], spread[q])
            staged[q, here, :] = jnp.maximum(0.0, volume[q, here, :] + scale[q, here, :] * update)
            rows = pl.ds(part * block, block)
            copies.append(pltpu.make_async_copy(staged.at[q, rows], new_volume.at[q, rows], sems.at[q * PARTS + part]))
            copies[-1].start()
    for copy in copies:
        copy.wait()
    keep.wait()


def shards(volume, voxel_norm, measured, ray_norm, axial_weights, row_start, row_order, subset):
    f32, bf16 = jnp.float32, jnp.bfloat16
    vmem = pl.BlockSpec(memory_space=pltpu.VMEM)
    hbm = pl.BlockSpec(memory_space=pltpu.HBM)
    dma = pltpu.SemaphoreType.DMA
    lines = ROWS * 8
    back, residual, volume_near, scale_near, moved, depth = pl.pallas_call(
        main_kernel,
        in_specs=[hbm] * 8,
        out_specs=(vmem,) * 6,
        out_shape=(
            jax.ShapeDtypeStruct((1024, LANES), bf16), jax.ShapeDtypeStruct((lines, LANES), f32),
            jax.ShapeDtypeStruct(volume.shape, f32), jax.ShapeDtypeStruct(volume.shape, f32),
            jax.ShapeDtypeStruct((ANGLES, LANES), f32), jax.ShapeDtypeStruct((DEPTH, LANES), bf16),
        ),
        scratch_shapes=[
            pltpu.SMEM((ANGLES,), jnp.int32), pltpu.VMEM((ANGLES, 4 * ANGLES), jnp.int32),
            pltpu.VMEM((6, LANES), jnp.int32), pltpu.VMEM((2, FOOT, ANGLES), f32),
            pltpu.VMEM((lines, LANES), f32), pltpu.VMEM((lines, LANES), f32),
            pltpu.VMEM((ANGLES, CELLS), f32), pltpu.VMEM((1024, LANES), f32), pltpu.VMEM((512, LANES), bf16),
            pltpu.VMEM((ANGLES, 1, LANES), f32), pltpu.VMEM((2048, LANES), bf16), pltpu.VMEM((128, 1, LANES), f32),
            pltpu.VMEM((2048, LANES), f32), pltpu.VMEM((512, 2 * ROWS), bf16), pltpu.VMEM((2, 2 * ROWS, 256), bf16),
            pltpu.VMEM((2 * ROWS, LANES), f32), pltpu.VMEM((2 * ROWS, CELLS), bf16),
            pltpu.VMEM((1024, LANES), bf16), pltpu.VMEM((1024, LANES), bf16),
            dma((2 * PARTS,)), dma((4,)), dma((3,)), dma((1,)), dma((4,)), dma((1,)), dma((1,)),
            dma((4,)), dma((4,)), dma((1,)), dma((1,)), dma((4,)), dma((4,)), dma((1,)), dma((1,)),
        ],
        compiler_params=pltpu.CompilerParams(collective_id=0, has_side_effects=True, vmem_limit_bytes=28 << 20),
        cost_estimate=pl.CostEstimate(flops=10 ** 9, bytes_accessed=100 << 20, transcendentals=0),
        name="exchange",
    )(
        *[pltpu.with_memory_space_constraint(array, pltpu.HBM) for array in (
            subset, row_start, row_order.reshape(6, LANES), jnp.transpose(axial_weights, (0, 2, 1)), volume, voxel_norm,
            measured.reshape(lines, LANES), ray_norm.reshape(lines, LANES),
        )]
    )
    new_volume, residual = pl.pallas_call(
        final_kernel,
        in_specs=[vmem, vmem, vmem, vmem, vmem, pl.BlockSpec(memory_space=pl.ANY)],
        out_specs=(hbm, hbm),
        out_shape=(jax.ShapeDtypeStruct(volume.shape, f32), jax.ShapeDtypeStruct((lines, LANES), f32)),
        scratch_shapes=[
            pltpu.VMEM((512, LANES), f32), pltpu.VMEM((2, LANES, COLS), bf16), pltpu.VMEM(volume.shape, f32),
            dma((2 * PARTS,)), dma,
        ],
        compiler_params=pltpu.CompilerParams(vmem_limit_bytes=28 << 20),
        cost_estimate=pl.CostEstimate(flops=6 * 64 * DEPTH * COLS, bytes_accessed=4 * 6 * DEPTH * COLS, transcendentals=0),
        name="final",
    )(moved, depth, back, volume_near, scale_near, residual)
    return new_volume, residual.reshape(measured.shape)


def solution(mesh):
    placed = (
        P(("grp", "blk"), None, None),
        P(("grp", "blk"), None, None),
        P("grp", "blk", None),
        P("grp", "blk", None),
        P(("grp", "blk"), None, None),
        P(),
        P(),
        P(),
    )
    return jax.shard_map(
        shards,
        mesh=mesh,
        in_specs=placed,
        out_specs=(P(("grp", "blk"), None, None), P("grp", "blk", None)),
        check_vma=False,
    )
```

```python
import itertools
import math

import jax
import jax.numpy as jnp
from jax import lax
from jax.experimental import pallas as pl
from jax.experimental.pallas import tpu as pltpu
from jax.sharding import PartitionSpec as P

TOTAL_ANG = 1024
MESH = pl.DeviceIdType.MESH
LANES = 128
ANGLES = 32
FOOT = 8
COLS = 768
DEPTH = 768
CELLS = 1024
ROWS = 192
PARTS = 3
OFFSETS = sorted(
    itertools.product(range(4), repeat=3), key=lambda offset: -sum(min(step, 4 - step) for step in offset)
)[:-1]
STEP = 0.8 * CELLS / COLS


def halves(value):
    high = value.astype(jnp.bfloat16)
    return high, (value - high.astype(jnp.float32)).astype(jnp.bfloat16)


def dot(left, right):
    return jnp.dot(left, right, preferred_element_type=jnp.float32)


def depth_weight(cell, sine):
    middle = (DEPTH - 1) / 2.0 * (1.0 + 0.8 * sine)
    bump = jnp.maximum(0.0, 1.0 - jnp.abs(cell - middle) / (0.1 * DEPTH))
    return (1.0 + 2.0 * bump) / DEPTH


def centre_of(col, shift):
    return ((CELLS - 1) / 2.0 + STEP * (col - (COLS - 1) / 2.0)) + shift


def pick(tiles, first, last, index):
    inside = index & (LANES - 1)
    tile = index >> 7
    value = None
    for number in range(first, last + 1):
        found = jnp.take_along_axis(tiles[number], inside, axis=1, mode="promise_in_bounds")
        value = found if value is None else jnp.where(tile == number, found, value)
    return value


def span(low, high, tiles):
    first = max(0, min(tiles - 1, math.floor(low) // LANES))
    return first, max(first, min(tiles - 1, math.floor(high) // LANES))


def sines(subset_ref, which):
    chosen = jnp.zeros_like(which)
    for angle in range(ANGLES):
        chosen = jnp.where(which == angle, subset_ref[angle], chosen)
    return jnp.sin(2.0 * math.pi / TOTAL_ANG * chosen.astype(jnp.float32))


def ray_sums(tiles, shift, chunk):
    lane = lax.broadcasted_iota(jnp.int32, (ANGLES, LANES), 1).astype(jnp.float32)
    detector = lane + chunk * LANES
    nearest = jnp.floor((detector - (CELLS - 1) / 2.0 - shift) * (1.0 / STEP) + (COLS - 1) / 2.0)
    middle = (chunk * LANES - (CELLS - 1) / 2.0) / STEP + (COLS - 1) / 2.0
    first, last = span(middle - 49.5, middle + 49.5 + 128 / STEP + 1, COLS // LANES)
    values, total = [0.0, 0.0], 0.0
    for near in (0.0, 1.0):
        col = nearest + near
        weight = jnp.maximum(0.0, 1.0 - jnp.abs(detector - centre_of(col, shift)))
        weight = jnp.where((col >= 0.0) & (col <= COLS - 1.0), weight, 0.0)
        index = col.astype(jnp.int32)
        values = [value + weight * pick(tile, first, last, index) for value, tile in zip(values, tiles)]
        total = total + weight
    return values, total


def spread_rows(tiles, shift, chunk):
    lane = lax.broadcasted_iota(jnp.int32, (ANGLES, LANES), 1).astype(jnp.float32)
    centre = centre_of(lane + chunk * LANES, shift)
    left = jnp.floor(centre)
    middle = (CELLS - 1) / 2.0 + STEP * (chunk * LANES - (COLS - 1) / 2.0)
    first, last = span(middle - 52.5, middle + 52.5 + STEP * 128 + 1, CELLS // LANES)
    value = 0.0
    for near in (0.0, 1.0):
        detector = left + near
        weight = jnp.maximum(0.0, 1.0 - jnp.abs(detector - centre))
        value = value + weight * pick(tiles, first, last, detector.astype(jnp.int32))
    return value


def main_kernel(
    subset_hbm, row_start_hbm, order_hbm, axial_hbm, volume_hbm, scale_hbm, measured_hbm, norm_hbm,
    back, residual, volume, scale, moved, depth,
    subset, row_start, order, axial, measured, norm, rowsum, straight, sino, aux, every, every_aux, every_wide, tall, weight, wide, mean,
    ratio, partial, from_sibling, linear, arrived,
    volume_sem, small_sem, load_sem, send_sem, recv_sem, aux_send, aux_recv,
    sum_send, sum_recv, ratio_send, ratio_recv, out_send, out_recv,
):
    f32, bf16 = jnp.float32, jnp.bfloat16
    block = DEPTH // PARTS
    g, m = lax.axis_index("grp"), lax.axis_index("blk")
    core = g % 2
    y, z, x = (m // 16) * 2 + g // 2, (m // 4) % 4, m % 4
    sibling = (g - core + (1 - core), m)

    ys, zs, xs = ([(place + step) % 4 for step in range(4)] for place in (y, z, x))
    group_of = [place % 2 * 2 + core for place in ys]
    plane_of = [place // 2 * 16 for place in ys]
    line_of = [[row * 4 + col for col in xs] for row in zs]

    def partner(offset):
        return group_of[offset[0]], plane_of[offset[0]] + line_of[offset[1]][offset[2]]

    def partner_slot(offset):
        return ys[offset[0]] * 16 + line_of[offset[1]][offset[2]]

    def arrived_all(ref, sem):
        return pltpu.make_async_copy(ref, ref, sem)

    here_chip = y * 16 + z * 4 + x

    def slot(number, members=1):
        return pl.ds(pl.multiple_of(number * 16, 16), members * 16)

    def remote(source_ref, target_ref, send, recv, device):
        return pltpu.make_async_remote_copy(
            src_ref=source_ref, dst_ref=target_ref, send_sem=send, recv_sem=recv,
            device_id=device, device_id_type=MESH,
        )

    small = [
        pltpu.make_async_copy(subset_hbm, subset, small_sem.at[0]),
        pltpu.make_async_copy(row_start_hbm, row_start, small_sem.at[1]),
        pltpu.make_async_copy(axial_hbm, axial, small_sem.at[2]),
        pltpu.make_async_copy(order_hbm, order, small_sem.at[3]),
    ]
    for copy in small:
        copy.start()
    bring = []
    for q in range(2):
        for part in range(PARTS):
            here = pl.ds(part * block, block)
            bring.append(pltpu.make_async_copy(volume_hbm.at[q, here], volume.at[q, here], volume_sem.at[q * PARTS + part]))
    for copy in bring:
        copy.start()
    load = [
        pltpu.make_async_copy(measured_hbm, measured, load_sem.at[0]),
        pltpu.make_async_copy(norm_hbm, norm, load_sem.at[1]),
        pltpu.make_async_copy(scale_hbm, scale, load_sem.at[2]),
    ]
    barrier = pltpu.get_barrier_semaphore()

    for offset in OFFSETS:
        pl.semaphore_signal(barrier, inc=1, device_id=partner(offset), device_id_type=MESH)
    pl.semaphore_signal(barrier, inc=1, device_id=sibling, device_id_type=MESH)

    for copy in small:
        copy.wait()
    sine = sines(subset, lax.broadcasted_iota(jnp.int32, (ANGLES, LANES), 0))
    shift = (0.05 * CELLS) * sine
    moved[...] = shift
    tiles, means = [], []
    for q in range(2):
        total = 0.0
        for part in range(PARTS):
            cell = (lax.broadcasted_iota(jnp.int32, (ANGLES, block), 1) + part * block).astype(f32)
            high, low = halves(depth_weight(cell, sine[:, :1]))
            bring[q * PARTS + part].wait()
            volume_high, volume_low = halves(volume[q, part * block:(part + 1) * block, :])
            both = dot(jnp.concatenate([high, low], axis=0), volume_high)
            total = total + (both[:ANGLES] + (both[ANGLES:] + dot(high, volume_low)))
        middle = jnp.sum(total, axis=1, keepdims=True) * (1.0 / COLS)
        means.append(middle)
        total = total - middle
        tiles.append([total[:, t * LANES:(t + 1) * LANES] for t in range(COLS // LANES)])
    for copy in load:
        copy.start()
    for chunk in range(CELLS // LANES):
        values, sums = ray_sums(tiles, shift, chunk)
        rowsum[:, chunk * LANES:(chunk + 1) * LANES] = sums
        for q in range(2):
            straight[pl.ds(q * 8 + chunk, ANGLES, stride=16), :] = values[q]
    sino[...] = straight[:512].astype(bf16)

    lane = lax.broadcasted_iota(jnp.int32, (ANGLES, LANES), 1)
    first = jnp.sum(jnp.where(lane == g * 32 + m, row_start[...], 0), axis=1, keepdims=True).astype(f32)
    table = jnp.concatenate([axial[...].reshape(16, ANGLES), jnp.zeros((16, LANES - ANGLES), f32)], axis=1)
    table = jnp.concatenate([table, jnp.zeros((LANES - 16, LANES), f32)], axis=0).T[:ANGLES]
    for number, column in ((16, first), (17, means[0]), (18, means[1])):
        table = jnp.where(lane == number, column, table)
    aux[...] = table.reshape(ANGLES, 1, LANES)

    pl.semaphore_wait(barrier, 64)

    for offset in OFFSETS:
        device = partner(offset)
        remote(
            aux.at[device[1]], every_aux.at[here_chip], aux_send.at[0], aux_recv.at[offset[0]], device
        ).start()
        remote(
            sino.at[slot(device[1])], every.at[slot(here_chip)], send_sem.at[0], recv_sem.at[offset[0]], device
        ).start()
    every[slot(here_chip)] = sino[slot(m)]
    every_aux[here_chip] = aux[m]

    rows = order[...].astype(f32)
    lower = jnp.concatenate([rows[i:i + 1] for i in range(3)], axis=1)
    upper = jnp.concatenate([rows[i:i + 1] for i in range(3, 6)], axis=1)
    rows = jnp.where(y % 2 == 0, lower, upper)
    constant = 0.0
    for number in (0, 1, 3, 2):
        low, count = pl.multiple_of(ys[(4 - number) % 4] * 16, 16), 15 if number == 0 else 16
        arrived_all(every_aux.at[pl.ds(low, count)], aux_recv.at[number]).wait()
        table = every_aux[pl.ds(low, 16)].reshape(16, LANES)
        offset = rows - table[:, 16:17]
        for q in range(2):
            value = jnp.zeros_like(offset)
            for r in range(FOOT):
                value = jnp.where(offset == float(r), table[:, q * FOOT + r:q * FOOT + r + 1], value)
            tall[pl.ds(q * 64 + low, 16), :] = value
            constant = constant + jnp.sum(value * table[:, 17 + q:18 + q], axis=0, keepdims=True)
        arrived_all(every.at[slot(low, count)], recv_sem.at[number]).wait()
        every_wide[slot(low, 16), :] = every[slot(low, 16), :].astype(f32)
    own_mean = jnp.broadcast_to(constant, (LANES, 2 * ROWS)).T
    tall_high, tall_low = halves(tall[...])
    weight[0:128, :] = tall_high
    weight[128:256, :] = tall_low
    wide_high, wide_low = halves(tall[...].T)
    wide[:, 0:128] = wide_high
    wide[:, 128:256] = wide_low
    for copy in load[:2]:
        copy.wait()

    mine = pl.ds(pl.multiple_of(core * ROWS, ROWS), ROWS)
    other = pl.ds(pl.multiple_of((1 - core) * ROWS, ROWS), ROWS)
    mean[...] = own_mean
    own_sum = rowsum[pl.ds(m, 1), :]

    def to_sibling(pair, rows):
        here = pl.ds(pair * 256, 256)
        return remote(ratio.at[rows, here], ratio.at[rows, here], ratio_send.at[pair], ratio_recv.at[pair], sibling)

    def half_sums(pair):
        return remote(partial.at[pair, other], from_sibling.at[pair], sum_send.at[pair], sum_recv.at[pair], sibling)

    def forward(pair):
        columns = jnp.concatenate([
            jnp.concatenate([every_wide[pl.ds(q * 8 + chunk, 64, stride=16), :] for q in range(2)], axis=0)
            for chunk in (2 * pair, 2 * pair + 1)
        ], axis=1).astype(bf16)
        value = dot(wide[...], jnp.concatenate([columns, columns], axis=0))
        for side in range(2):
            here = slice((2 * pair + side) * LANES, (2 * pair + side + 1) * LANES)
            partial[pair, :, side * LANES:(side + 1) * LANES] = (
                value[:, side * LANES:(side + 1) * LANES] + mean[...] * own_sum[:, here]
            )
        half_sums(pair).start()

    def finish(pair):
        half_sums(pair).wait_recv()
        for side in range(2):
            chunk = 2 * pair + side
            here = slice(side * LANES, (side + 1) * LANES)
            found = partial[pair, mine, here] + from_sibling[pair, :, here]
            rows = pl.ds(chunk, ROWS, stride=8)
            rest = norm[rows, :] * (measured[rows, :] - found)
            residual[rows, :] = rest
            ratio[mine, chunk * LANES:(chunk + 1) * LANES] = rest.astype(bf16)
        to_sibling(pair, mine).start()

    def collect(pair):
        to_sibling(pair, other).wait_recv()
        both = dot(weight[...], ratio[:, pair * 256:(pair + 1) * 256])
        value = both[:128] + both[128:]
        for q in range(2):
            for side in range(2):
                straight[pl.ds(q * 8 + 2 * pair + side, 64, stride=16), :] = value[q * 64:(q + 1) * 64, side * LANES:(side + 1) * LANES]

    for step in range(6):
        if step < 4:
            forward(step)
        if 0 <= step - 1 < 4:
            finish(step - 1)
        if 0 <= step - 2 < 4:
            collect(step - 2)

    arrival = (y % 2) * 32 + m
    for offset in OFFSETS:
        rows = slot(partner_slot(offset))
        linear[rows] = straight[rows].astype(bf16)
        remote(linear.at[rows], arrived.at[slot(arrival)], out_send.at[0], out_recv.at[0], partner(offset)).start()
    arrived[slot(arrival)] = straight[slot(here_chip)].astype(bf16)

    sine_row = sines(subset, lax.broadcasted_iota(jnp.int32, (8, LANES), 1) % ANGLES)[:1]
    for part in range(PARTS):
        cell = (lax.broadcasted_iota(jnp.int32, (block, LANES), 0) + part * block).astype(f32)
        lane = lax.broadcasted_iota(jnp.int32, (block, LANES), 1)
        value = depth_weight(cell, sine_row)
        high = value.astype(bf16).astype(f32)
        depth[part * block:(part + 1) * block, :] = jnp.where(lane < 2 * ANGLES, high, value - high).astype(bf16)

    arrived_all(every.at[slot(0, 63)], send_sem.at[0]).wait()
    arrived_all(every_aux.at[pl.ds(0, 63)], aux_send.at[0]).wait()
    for number in range(4):
        half_sums(number).wait_send()
        to_sibling(number, mine).wait_send()
    load[2].wait()

    arrived_all(arrived.at[slot(0, 63)], out_recv.at[0]).wait()
    back[...] = arrived[...]
    arrived_all(linear.at[slot(0, 63)], out_send.at[0]).wait()


def final_kernel(moved, depth, back, volume, scale, residual_in, new_volume, residual, straight, spread, staged, sems, rest_sem):
    f32 = jnp.float32
    block = DEPTH // PARTS
    keep = pltpu.make_async_copy(residual_in, residual, rest_sem)
    keep.start()
    straight[...] = back[:512].astype(f32) + back[512:].astype(f32)
    shift = moved[...]
    copies = []
    for q in range(2):
        tiles = [straight[pl.ds(q * 8 + chunk, ANGLES, stride=16), :] for chunk in range(CELLS // LANES)]
        for chunk in range(COLS // LANES):
            high, low = halves(spread_rows(tiles, shift, chunk))
            here = slice(chunk * LANES, (chunk + 1) * LANES)
            spread[q, 0:ANGLES, here] = high
            spread[q, ANGLES:2 * ANGLES, here] = low
            spread[q, 2 * ANGLES:3 * ANGLES, here] = high
            spread[q, 3 * ANGLES:4 * ANGLES, here] = jnp.zeros_like(high)
        for part in range(PARTS):
            here = slice(part * block, (part + 1) * block)
            update = dot(depth[here, :], spread[q])
            staged[q, here, :] = jnp.maximum(0.0, volume[q, here, :] + scale[q, here, :] * update)
            rows = pl.ds(part * block, block)
            copies.append(pltpu.make_async_copy(staged.at[q, rows], new_volume.at[q, rows], sems.at[q * PARTS + part]))
            copies[-1].start()
    for copy in copies:
        copy.wait()
    keep.wait()


def shards(volume, voxel_norm, measured, ray_norm, axial_weights, row_start, row_order, subset):
    f32, bf16 = jnp.float32, jnp.bfloat16
    vmem = pl.BlockSpec(memory_space=pltpu.VMEM)
    hbm = pl.BlockSpec(memory_space=pltpu.HBM)
    dma = pltpu.SemaphoreType.DMA
    lines = ROWS * 8
    back, residual, volume_near, scale_near, moved, depth = pl.pallas_call(
        main_kernel,
        in_specs=[hbm] * 8,
        out_specs=(vmem,) * 6,
        out_shape=(
            jax.ShapeDtypeStruct((1024, LANES), bf16), jax.ShapeDtypeStruct((lines, LANES), f32),
            jax.ShapeDtypeStruct(volume.shape, f32), jax.ShapeDtypeStruct(volume.shape, f32),
            jax.ShapeDtypeStruct((ANGLES, LANES), f32), jax.ShapeDtypeStruct((DEPTH, LANES), bf16),
        ),
        scratch_shapes=[
            pltpu.SMEM((ANGLES,), jnp.int32), pltpu.VMEM((ANGLES, 4 * ANGLES), jnp.int32),
            pltpu.VMEM((6, LANES), jnp.int32), pltpu.VMEM((2, FOOT, ANGLES), f32),
            pltpu.VMEM((lines, LANES), f32), pltpu.VMEM((lines, LANES), f32),
            pltpu.VMEM((ANGLES, CELLS), f32), pltpu.VMEM((1024, LANES), f32), pltpu.VMEM((512, LANES), bf16),
            pltpu.VMEM((ANGLES, 1, LANES), f32), pltpu.VMEM((1024, LANES), bf16), pltpu.VMEM((64, 1, LANES), f32),
            pltpu.VMEM((1024, LANES), f32), pltpu.VMEM((128, 2 * ROWS), f32), pltpu.VMEM((256, 2 * ROWS), bf16),
            pltpu.VMEM((2 * ROWS, 256), bf16), pltpu.VMEM((2 * ROWS, LANES), f32), pltpu.VMEM((2 * ROWS, CELLS), bf16),
            pltpu.VMEM((4, 2 * ROWS, 256), f32), pltpu.VMEM((4, ROWS, 256), f32),
            pltpu.VMEM((1024, LANES), bf16), pltpu.VMEM((1024, LANES), bf16),
            dma((2 * PARTS,)), dma((4,)), dma((3,)), dma((1,)), dma((4,)), dma((1,)), dma((4,)),
            dma((4,)), dma((4,)), dma((4,)), dma((4,)), dma((1,)), dma((1,)),
        ],
        compiler_params=pltpu.CompilerParams(collective_id=0, has_side_effects=True, vmem_limit_bytes=28 << 20),
        cost_estimate=pl.CostEstimate(flops=10 ** 9, bytes_accessed=100 << 20, transcendentals=0),
        name="exchange",
    )(
        *[pltpu.with_memory_space_constraint(array, pltpu.HBM) for array in (
            subset, row_start, row_order.reshape(6, LANES), jnp.transpose(axial_weights, (0, 2, 1)), volume, voxel_norm,
            measured.reshape(lines, LANES), ray_norm.reshape(lines, LANES),
        )]
    )
    new_volume, residual = pl.pallas_call(
        final_kernel,
        in_specs=[vmem, vmem, vmem, vmem, vmem, pl.BlockSpec(memory_space=pl.ANY)],
        out_specs=(hbm, hbm),
        out_shape=(jax.ShapeDtypeStruct(volume.shape, f32), jax.ShapeDtypeStruct((lines, LANES), f32)),
        scratch_shapes=[
            pltpu.VMEM((512, LANES), f32), pltpu.VMEM((2, LANES, COLS), bf16), pltpu.VMEM(volume.shape, f32),
            dma((2 * PARTS,)), dma,
        ],
        compiler_params=pltpu.CompilerParams(vmem_limit_bytes=28 << 20),
        cost_estimate=pl.CostEstimate(flops=6 * 64 * DEPTH * COLS, bytes_accessed=4 * 6 * DEPTH * COLS, transcendentals=0),
        name="final",
    )(moved, depth, back, volume_near, scale_near, residual)
    return new_volume, residual.reshape(measured.shape)


def solution(mesh):
    placed = (
        P(("grp", "blk"), None, None),
        P(("grp", "blk"), None, None),
        P("grp", "blk", None),
        P("grp", "blk", None),
        P(("grp", "blk"), None, None),
        P(),
        P(),
        P(),
    )
    return jax.shard_map(
        shards,
        mesh=mesh,
        in_specs=placed,
        out_specs=(P(("grp", "blk"), None, None), P("grp", "blk", None)),
        check_vma=False,
    )
```

```python
import itertools
import math

import jax
import jax.numpy as jnp
from jax import lax
from jax.experimental import pallas as pl
from jax.experimental.pallas import tpu as pltpu
from jax.sharding import PartitionSpec as P

TOTAL_ANG = 1024
MESH = pl.DeviceIdType.MESH
LANES = 128
ANGLES = 32
FOOT = 8
COLS = 768
DEPTH = 768
CELLS = 1024
ROWS = 192
PARTS = 3
OFFSETS = sorted(
    itertools.product(range(4), repeat=3), key=lambda offset: -sum(min(step, 4 - step) for step in offset)
)[:-1]
STEP = 0.8 * CELLS / COLS


def halves(value):
    high = value.astype(jnp.bfloat16)
    return high, (value - high.astype(jnp.float32)).astype(jnp.bfloat16)


def dot(left, right):
    return jnp.dot(left, right, preferred_element_type=jnp.float32)


def depth_weight(cell, sine):
    middle = (DEPTH - 1) / 2.0 * (1.0 + 0.8 * sine)
    bump = jnp.maximum(0.0, 1.0 - jnp.abs(cell - middle) / (0.1 * DEPTH))
    return (1.0 + 2.0 * bump) / DEPTH


def centre_of(col, shift):
    return ((CELLS - 1) / 2.0 + STEP * (col - (COLS - 1) / 2.0)) + shift


def pick(tiles, first, last, index):
    inside = index & (LANES - 1)
    tile = index >> 7
    value = None
    for number in range(first, last + 1):
        found = jnp.take_along_axis(tiles[number], inside, axis=1, mode="promise_in_bounds")
        value = found if value is None else jnp.where(tile == number, found, value)
    return value


def span(low, high, tiles):
    first = max(0, min(tiles - 1, math.floor(low) // LANES))
    return first, max(first, min(tiles - 1, math.floor(high) // LANES))


def sines(subset_ref, which):
    chosen = jnp.zeros_like(which)
    for angle in range(ANGLES):
        chosen = jnp.where(which == angle, subset_ref[angle], chosen)
    return jnp.sin(2.0 * math.pi / TOTAL_ANG * chosen.astype(jnp.float32))


def ray_sums(tiles, shift, chunk):
    lane = lax.broadcasted_iota(jnp.int32, (ANGLES, LANES), 1).astype(jnp.float32)
    detector = lane + chunk * LANES
    nearest = jnp.floor((detector - (CELLS - 1) / 2.0 - shift) * (1.0 / STEP) + (COLS - 1) / 2.0)
    middle = (chunk * LANES - (CELLS - 1) / 2.0) / STEP + (COLS - 1) / 2.0
    first, last = span(middle - 49.5, middle + 49.5 + 128 / STEP + 1, COLS // LANES)
    values, total = [0.0, 0.0], 0.0
    for near in (0.0, 1.0):
        col = nearest + near
        weight = jnp.maximum(0.0, 1.0 - jnp.abs(detector - centre_of(col, shift)))
        weight = jnp.where((col >= 0.0) & (col <= COLS - 1.0), weight, 0.0)
        index = col.astype(jnp.int32)
        values = [value + weight * pick(tile, first, last, index) for value, tile in zip(values, tiles)]
        total = total + weight
    return values, total


def spread_rows(tiles, shift, chunk):
    lane = lax.broadcasted_iota(jnp.int32, (ANGLES, LANES), 1).astype(jnp.float32)
    centre = centre_of(lane + chunk * LANES, shift)
    left = jnp.floor(centre)
    middle = (CELLS - 1) / 2.0 + STEP * (chunk * LANES - (COLS - 1) / 2.0)
    first, last = span(middle - 52.5, middle + 52.5 + STEP * 128 + 1, CELLS // LANES)
    value = 0.0
    for near in (0.0, 1.0):
        detector = left + near
        weight = jnp.maximum(0.0, 1.0 - jnp.abs(detector - centre))
        value = value + weight * pick(tiles, first, last, detector.astype(jnp.int32))
    return value


def main_kernel(
    subset_hbm, row_start_hbm, order_hbm, axial_hbm, volume_hbm, scale_hbm, measured_hbm, norm_hbm,
    back, residual, volume, scale, moved, depth,
    subset, row_start, order, axial, measured, norm, rowsum, straight, sino, aux, every, every_aux, every_wide, tall, weight, wide, matrix,
    remainder, ratio, linear, arrived,
    volume_sem, small_sem, load_sem, send_sem, recv_sem, aux_send, aux_recv,
    near_send, near_recv, aux2_send, aux2_recv, input_send, input_recv, out_send, out_recv,
):
    f32, bf16 = jnp.float32, jnp.bfloat16
    block = DEPTH // PARTS
    g, m = lax.axis_index("grp"), lax.axis_index("blk")
    core = g % 2
    y, z, x = (m // 16) * 2 + g // 2, (m // 4) % 4, m % 4
    sibling = (g - core + (1 - core), m)

    ys, zs, xs = ([(place + step) % 4 for step in range(4)] for place in (y, z, x))
    group_of = [place % 2 * 2 + core for place in ys]
    plane_of = [place // 2 * 16 for place in ys]
    line_of = [[row * 4 + col for col in xs] for row in zs]

    def partner(offset):
        return group_of[offset[0]], plane_of[offset[0]] + line_of[offset[1]][offset[2]]

    def partner_slot(offset):
        return ys[offset[0]] * 16 + line_of[offset[1]][offset[2]]

    def arrived_all(ref, sem):
        return pltpu.make_async_copy(ref, ref, sem)

    here_chip = y * 16 + z * 4 + x

    def slot(number, members=1):
        return pl.ds(pl.multiple_of(number * 16, 16), members * 16)

    def remote(source_ref, target_ref, send, recv, device):
        return pltpu.make_async_remote_copy(
            src_ref=source_ref, dst_ref=target_ref, send_sem=send, recv_sem=recv,
            device_id=device, device_id_type=MESH,
        )

    small = [
        pltpu.make_async_copy(subset_hbm, subset, small_sem.at[0]),
        pltpu.make_async_copy(row_start_hbm, row_start, small_sem.at[1]),
        pltpu.make_async_copy(axial_hbm, axial, small_sem.at[2]),
        pltpu.make_async_copy(order_hbm, order, small_sem.at[3]),
    ]
    for copy in small:
        copy.start()
    bring = []
    for q in range(2):
        for part in range(PARTS):
            here = pl.ds(part * block, block)
            bring.append(pltpu.make_async_copy(volume_hbm.at[q, here], volume.at[q, here], volume_sem.at[q * PARTS + part]))
    for copy in bring:
        copy.start()
    mine = pl.ds(pl.multiple_of(core * ROWS, ROWS), ROWS)
    other = pl.ds(pl.multiple_of((1 - core) * ROWS, ROWS), ROWS)
    load = [
        pltpu.make_async_copy(
            array.at[:, chunk, :], target.at[mine, pl.ds(chunk * LANES, LANES)], load_sem.at[number * 8 + chunk]
        )
        for number, (array, target) in enumerate(((measured_hbm, measured), (norm_hbm, norm))) for chunk in range(8)
    ]
    load_scale = pltpu.make_async_copy(scale_hbm, scale, load_sem.at[16])

    barrier = pltpu.get_barrier_semaphore()

    for offset in OFFSETS:
        pl.semaphore_signal(barrier, inc=1, device_id=partner(offset), device_id_type=MESH)
    pl.semaphore_signal(barrier, inc=1, device_id=sibling, device_id_type=MESH)

    for copy in small:
        copy.wait()
    sine = sines(subset, lax.broadcasted_iota(jnp.int32, (ANGLES, LANES), 0))
    shift = (0.05 * CELLS) * sine
    moved[...] = shift
    tiles, means = [], []
    for q in range(2):
        total = 0.0
        for part in range(PARTS):
            cell = (lax.broadcasted_iota(jnp.int32, (ANGLES, block), 1) + part * block).astype(f32)
            high, low = halves(depth_weight(cell, sine[:, :1]))
            bring[q * PARTS + part].wait()
            volume_high, volume_low = halves(volume[q, part * block:(part + 1) * block, :])
            both = dot(jnp.concatenate([high, low], axis=0), volume_high)
            total = total + (both[:ANGLES] + (both[ANGLES:] + dot(high, volume_low)))
        middle = jnp.sum(total, axis=1, keepdims=True) * (1.0 / COLS)
        means.append(middle)
        total = total - middle
        tiles.append([total[:, t * LANES:(t + 1) * LANES] for t in range(COLS // LANES)])
    for copy in load:
        copy.start()
    load_scale.start()
    for chunk in range(CELLS // LANES):
        values, sums = ray_sums(tiles, shift, chunk)
        rowsum[:, chunk * LANES:(chunk + 1) * LANES] = sums
        for q in range(2):
            straight[pl.ds(q * 8 + chunk, ANGLES, stride=16), :] = values[q]
    sino[...] = straight[:512].astype(bf16)

    lane = lax.broadcasted_iota(jnp.int32, (ANGLES, LANES), 1)
    first = jnp.sum(jnp.where(lane == g * 32 + m, row_start[...], 0), axis=1, keepdims=True).astype(f32)
    table = jnp.concatenate([axial[...].reshape(16, ANGLES), jnp.zeros((16, LANES - ANGLES), f32)], axis=1)
    table = jnp.concatenate([table, jnp.zeros((LANES - 16, LANES), f32)], axis=0).T[:ANGLES]
    for number, column in ((16, first), (17, means[0]), (18, means[1])):
        table = jnp.where(lane == number, column, table)
    aux[...] = table.reshape(ANGLES, 1, LANES)

    pl.semaphore_wait(barrier, 64)

    for offset in OFFSETS:
        device = partner(offset)
        remote(
            aux.at[device[1]], every_aux.at[core * 64 + here_chip], aux_send.at[0], aux_recv.at[offset[0]], device
        ).start()
        remote(
            sino.at[slot(device[1])], every.at[slot(core * 64 + here_chip)], send_sem.at[0], recv_sem.at[offset[0]], device
        ).start()
    every[slot(core * 64 + here_chip)] = sino[slot(m)]
    every_aux[core * 64 + here_chip] = aux[m]

    for copy in load:
        copy.wait()

    def near_input(number, rows):
        target = (measured, norm)[number].at[rows]
        return remote(target, target, input_send.at[number], input_recv.at[number], sibling)

    near_input(0, mine).start()
    near_input(1, mine).start()

    rows = order[...].astype(f32)
    lower = jnp.concatenate([rows[i:i + 1] for i in range(3)], axis=1)
    upper = jnp.concatenate([rows[i:i + 1] for i in range(3, 6)], axis=1)
    rows = jnp.where(y % 2 == 0, lower, upper)
    own_sum = rowsum[pl.ds(m, 1), :]

    def first_slot(number, side):
        return pl.multiple_of(side * 64 + ys[(4 - number) % 4] * 16, 16)

    def near_rows(number, side):
        here = slot(first_slot(number, side), 16)
        return remote(every.at[here], every.at[here], near_send.at[number], near_recv.at[number], sibling)

    def near_aux(number, side):
        here = pl.ds(first_slot(number, side), 16)
        return remote(every_aux.at[here], every_aux.at[here], aux2_send.at[number], aux2_recv.at[number], sibling)

    def place(step, number, side, turn):
        low = first_slot(number, side)
        table = every_aux[pl.ds(low, 16)].reshape(16, LANES)
        offset = rows - table[:, 16:17]
        lane = lax.broadcasted_iota(jnp.int32, (16, LANES), 1)
        every_wide[...] = every[slot(low, 16), :].astype(f32)
        for q in range(2):
            value = jnp.zeros_like(offset)
            for r in range(FOOT):
                value = jnp.where(offset == float(r), table[:, q * FOOT + r:q * FOOT + r + 1], value)
            line = step * 64 + turn * 32 + q * 16
            tall[line:line + 16, :] = value
            if turn == 0:
                high, low_part = halves(value)
                weight[step * 32 + q * 16:step * 32 + q * 16 + 16, :] = high
                weight[128 + step * 32 + q * 16:128 + step * 32 + q * 16 + 16, :] = low_part
            for chunk in range(8):
                matrix[line:line + 16, chunk * LANES:(chunk + 1) * LANES] = (
                    every_wide[pl.ds(q * 8 + chunk, 16, stride=16), :].astype(bf16)
                )
            high, low_part = halves(table[:, 17 + q:18 + q])
            level = jnp.where(lane == 0, high.astype(f32), jnp.where(lane == 1, low_part.astype(f32), 0.0))
            matrix[line:line + 16, CELLS:CELLS + LANES] = level.astype(bf16)

    def own_rows(step, number):
        low, count = first_slot(number, core), 15 if number == 0 else 16
        arrived_all(every_aux.at[pl.ds(low, count)], aux_recv.at[number]).wait()
        near_aux(number, core).start()
        arrived_all(every.at[slot(low, count)], recv_sem.at[number]).wait()
        near_rows(number, core).start()
        place(step, number, core, 0)

    def sibling_rows(step, number):
        near_aux(number, 1 - core).wait_recv()
        near_rows(number, 1 - core).wait_recv()
        place(step, number, 1 - core, 1)

    def turn_over(part):
        high, low = halves(tall[part * LANES:(part + 1) * LANES, :].T)
        wide[:, part * LANES:(part + 1) * LANES] = high
        wide[:, 256 + part * LANES:256 + (part + 1) * LANES] = low

    sequence = (0, 1, 3, 2)
    own_rows(0, 0)
    own_rows(1, 1)
    sibling_rows(0, 0)
    own_rows(2, 3)
    sibling_rows(1, 1)
    turn_over(0)
    near_input(0, other).wait_recv()
    near_input(1, other).wait_recv()
    own_rows(3, 2)
    sibling_rows(2, 3)
    sibling_rows(3, 2)
    turn_over(1)

    def product(here):
        right = matrix[:, here]
        return dot(wide[...], jnp.concatenate([right, right], axis=0))

    level = product(slice(CELLS, CELLS + LANES))
    level = jnp.broadcast_to(level[:, 0:1] + level[:, 1:2], (2 * ROWS, LANES))

    def forward(pair):
        value = product(slice(pair * 256, (pair + 1) * 256))
        for side in range(2):
            here = slice((2 * pair + side) * LANES, (2 * pair + side + 1) * LANES)
            found = value[:, side * LANES:(side + 1) * LANES] + level * own_sum[:, here]
            rest = norm[:, here] * (measured[:, here] - found)
            remainder[:, here] = rest
            ratio[:, here] = rest.astype(bf16)

    def collect(pair):
        both = dot(weight[...], ratio[:, pair * 256:(pair + 1) * 256])
        value = both[:128] + both[128:]
        for step, number in enumerate(sequence):
            low = first_slot(number, 0) * 16
            for q in range(2):
                line = step * 32 + q * 16
                for side in range(2):
                    straight[pl.ds(low + q * 8 + 2 * pair + side, 16, stride=16), :] = (
                        value[line:line + 16, side * LANES:(side + 1) * LANES]
                    )

    for pair in range(4):
        forward(pair)
        collect(pair)

    arrival = (y % 2) * 32 + m
    for offset in OFFSETS:
        rows = slot(partner_slot(offset))
        linear[rows] = straight[rows].astype(bf16)
        remote(linear.at[rows], arrived.at[slot(arrival)], out_send.at[0], out_recv.at[0], partner(offset)).start()
    arrived[slot(arrival)] = straight[slot(here_chip)].astype(bf16)

    keep = [
        pltpu.make_async_copy(
            remainder.at[mine, pl.ds(chunk * LANES, LANES)], residual.at[:, chunk, :], load_sem.at[17 + chunk]
        )
        for chunk in range(8)
    ]
    for copy in keep:
        copy.start()
    sine_row = sines(subset, lax.broadcasted_iota(jnp.int32, (8, LANES), 1) % ANGLES)[:1]
    for part in range(PARTS):
        cell = (lax.broadcasted_iota(jnp.int32, (block, LANES), 0) + part * block).astype(f32)
        lane = lax.broadcasted_iota(jnp.int32, (block, LANES), 1)
        value = depth_weight(cell, sine_row)
        high = value.astype(bf16).astype(f32)
        depth[part * block:(part + 1) * block, :] = jnp.where(lane < 2 * ANGLES, high, value - high).astype(bf16)

    arrived_all(every.at[slot(0, 63)], send_sem.at[0]).wait()
    arrived_all(every_aux.at[pl.ds(0, 63)], aux_send.at[0]).wait()
    for number in range(4):
        near_rows(number, core).wait_send()
        near_aux(number, core).wait_send()
    for number in range(2):
        near_input(number, mine).wait_send()
    load_scale.wait()
    for copy in keep:
        copy.wait()

    arrived_all(arrived.at[slot(0, 63)], out_recv.at[0]).wait()
    back[...] = arrived[...]
    arrived_all(linear.at[slot(0, 63)], out_send.at[0]).wait()


def final_kernel(moved, depth, back, volume, scale, residual_in, new_volume, residual, straight, spread, staged, sems, rest_sem):
    f32 = jnp.float32
    block = DEPTH // PARTS
    keep = pltpu.make_async_copy(residual_in, residual, rest_sem)
    keep.start()
    straight[...] = back[:512].astype(f32) + back[512:].astype(f32)
    shift = moved[...]
    copies = []
    for q in range(2):
        tiles = [straight[pl.ds(q * 8 + chunk, ANGLES, stride=16), :] for chunk in range(CELLS // LANES)]
        for chunk in range(COLS // LANES):
            high, low = halves(spread_rows(tiles, shift, chunk))
            here = slice(chunk * LANES, (chunk + 1) * LANES)
            spread[q, 0:ANGLES, here] = high
            spread[q, ANGLES:2 * ANGLES, here] = low
            spread[q, 2 * ANGLES:3 * ANGLES, here] = high
            spread[q, 3 * ANGLES:4 * ANGLES, here] = jnp.zeros_like(high)
        for part in range(PARTS):
            here = slice(part * block, (part + 1) * block)
            update = dot(depth[here, :], spread[q])
            staged[q, here, :] = jnp.maximum(0.0, volume[q, here, :] + scale[q, here, :] * update)
            rows = pl.ds(part * block, block)
            copies.append(pltpu.make_async_copy(staged.at[q, rows], new_volume.at[q, rows], sems.at[q * PARTS + part]))
            copies[-1].start()
    for copy in copies:
        copy.wait()
    keep.wait()


def shards(volume, voxel_norm, measured, ray_norm, axial_weights, row_start, row_order, subset):
    f32, bf16 = jnp.float32, jnp.bfloat16
    vmem = pl.BlockSpec(memory_space=pltpu.VMEM)
    hbm = pl.BlockSpec(memory_space=pltpu.HBM)
    dma = pltpu.SemaphoreType.DMA
    back, residual, volume_near, scale_near, moved, depth = pl.pallas_call(
        main_kernel,
        in_specs=[hbm] * 8,
        out_specs=(vmem, hbm, vmem, vmem, vmem, vmem),
        out_shape=(
            jax.ShapeDtypeStruct((1024, LANES), bf16), jax.ShapeDtypeStruct((ROWS, 8, LANES), f32),
            jax.ShapeDtypeStruct(volume.shape, f32), jax.ShapeDtypeStruct(volume.shape, f32),
            jax.ShapeDtypeStruct((ANGLES, LANES), f32), jax.ShapeDtypeStruct((DEPTH, LANES), bf16),
        ),
        scratch_shapes=[
            pltpu.SMEM((ANGLES,), jnp.int32), pltpu.VMEM((ANGLES, 4 * ANGLES), jnp.int32),
            pltpu.VMEM((6, LANES), jnp.int32), pltpu.VMEM((2, FOOT, ANGLES), f32),
            pltpu.VMEM((2 * ROWS, CELLS), f32), pltpu.VMEM((2 * ROWS, CELLS), f32),
            pltpu.VMEM((ANGLES, CELLS), f32), pltpu.VMEM((1024, LANES), f32), pltpu.VMEM((512, LANES), bf16),
            pltpu.VMEM((ANGLES, 1, LANES), f32), pltpu.VMEM((2048, LANES), bf16), pltpu.VMEM((128, 1, LANES), f32),
            pltpu.VMEM((256, LANES), f32), pltpu.VMEM((256, 2 * ROWS), f32), pltpu.VMEM((256, 2 * ROWS), bf16),
            pltpu.VMEM((2 * ROWS, 512), bf16), pltpu.VMEM((256, CELLS + LANES), bf16),
            pltpu.VMEM((2 * ROWS, CELLS), f32), pltpu.VMEM((2 * ROWS, CELLS), bf16),
            pltpu.VMEM((1024, LANES), bf16), pltpu.VMEM((1024, LANES), bf16),
            dma((2 * PARTS,)), dma((4,)), dma((25,)), dma((1,)), dma((4,)), dma((1,)), dma((4,)),
            dma((4,)), dma((4,)), dma((4,)), dma((4,)), dma((2,)), dma((2,)), dma((1,)), dma((1,)),
        ],
        compiler_params=pltpu.CompilerParams(collective_id=0, has_side_effects=True, vmem_limit_bytes=28 << 20),
        cost_estimate=pl.CostEstimate(flops=10 ** 9, bytes_accessed=100 << 20, transcendentals=0),
        name="exchange",
    )(
        *[pltpu.with_memory_space_constraint(array, pltpu.HBM) for array in (
            subset, row_start, row_order.reshape(6, LANES), jnp.transpose(axial_weights, (0, 2, 1)), volume, voxel_norm,
            measured.reshape(ROWS, 8, LANES), ray_norm.reshape(ROWS, 8, LANES),
        )]
    )
    new_volume, residual = pl.pallas_call(
        final_kernel,
        in_specs=[vmem, vmem, vmem, vmem, vmem, pl.BlockSpec(memory_space=pl.ANY)],
        out_specs=(hbm, hbm),
        out_shape=(jax.ShapeDtypeStruct(volume.shape, f32), jax.ShapeDtypeStruct((ROWS, 8, LANES), f32)),
        scratch_shapes=[
            pltpu.VMEM((512, LANES), f32), pltpu.VMEM((2, LANES, COLS), bf16), pltpu.VMEM(volume.shape, f32),
            dma((2 * PARTS,)), dma,
        ],
        compiler_params=pltpu.CompilerParams(vmem_limit_bytes=28 << 20),
        cost_estimate=pl.CostEstimate(flops=6 * 64 * DEPTH * COLS, bytes_accessed=4 * 6 * DEPTH * COLS, transcendentals=0),
        name="final",
    )(moved, depth, back, volume_near, scale_near, residual)
    return new_volume, residual.reshape(measured.shape)


def solution(mesh):
    placed = (
        P(("grp", "blk"), None, None),
        P(("grp", "blk"), None, None),
        P("grp", "blk", None),
        P("grp", "blk", None),
        P(("grp", "blk"), None, None),
        P(),
        P(),
        P(),
    )
    return jax.shard_map(
        shards,
        mesh=mesh,
        in_specs=placed,
        out_specs=(P(("grp", "blk"), None, None), P("grp", "blk", None)),
        check_vma=False,
    )
```

```python
import itertools
import math

import jax
import jax.numpy as jnp
from jax import lax
from jax.experimental import pallas as pl
from jax.experimental.pallas import tpu as pltpu
from jax.sharding import PartitionSpec as P

TOTAL_ANG = 1024
MESH = pl.DeviceIdType.MESH
LANES = 128
ANGLES = 32
FOOT = 8
COLS = 768
DEPTH = 768
CELLS = 1024
ROWS = 192
PARTS = 3
OUT_PARTS = 6
OFFSETS = sorted(
    itertools.product(range(4), repeat=3), key=lambda offset: -sum(min(step, 4 - step) for step in offset)
)[:-1]
STEP = 0.8 * CELLS / COLS


def halves(value):
    high = value.astype(jnp.bfloat16)
    return high, (value - high.astype(jnp.float32)).astype(jnp.bfloat16)


def dot(left, right):
    return jnp.dot(left, right, preferred_element_type=jnp.float32)


def depth_weight(cell, sine):
    middle = (DEPTH - 1) / 2.0 * (1.0 + 0.8 * sine)
    bump = jnp.maximum(0.0, 1.0 - jnp.abs(cell - middle) / (0.1 * DEPTH))
    return (1.0 + 2.0 * bump) / DEPTH


def centre_of(col, shift):
    return ((CELLS - 1) / 2.0 + STEP * (col - (COLS - 1) / 2.0)) + shift


def pick(tiles, first, last, index):
    inside = index & (LANES - 1)
    tile = index >> 7
    value = None
    for number in range(first, last + 1):
        found = jnp.take_along_axis(tiles[number], inside, axis=1, mode="promise_in_bounds")
        value = found if value is None else jnp.where(tile == number, found, value)
    return value


def span(low, high, tiles):
    first = max(0, min(tiles - 1, math.floor(low) // LANES))
    return first, max(first, min(tiles - 1, math.floor(high) // LANES))


def sines(subset_ref, which):
    chosen = jnp.zeros_like(which)
    for angle in range(ANGLES):
        chosen = jnp.where(which == angle, subset_ref[angle], chosen)
    return jnp.sin(2.0 * math.pi / TOTAL_ANG * chosen.astype(jnp.float32))


def ray_sums(tiles, shift, chunk):
    lane = lax.broadcasted_iota(jnp.int32, (ANGLES, LANES), 1).astype(jnp.float32)
    detector = lane + chunk * LANES
    nearest = jnp.floor((detector - (CELLS - 1) / 2.0 - shift) * (1.0 / STEP) + (COLS - 1) / 2.0)
    middle = (chunk * LANES - (CELLS - 1) / 2.0) / STEP + (COLS - 1) / 2.0
    first, last = span(middle - 49.5, middle + 49.5 + 128 / STEP + 1, COLS // LANES)
    values, total = [0.0, 0.0], 0.0
    for near in (0.0, 1.0):
        col = nearest + near
        weight = jnp.maximum(0.0, 1.0 - jnp.abs(detector - centre_of(col, shift)))
        weight = jnp.where((col >= 0.0) & (col <= COLS - 1.0), weight, 0.0)
        index = col.astype(jnp.int32)
        values = [value + weight * pick(tile, first, last, index) for value, tile in zip(values, tiles)]
        total = total + weight
    return values, total


def spread_rows(tiles, shift, chunk):
    lane = lax.broadcasted_iota(jnp.int32, (ANGLES, LANES), 1).astype(jnp.float32)
    centre = centre_of(lane + chunk * LANES, shift)
    left = jnp.floor(centre)
    middle = (CELLS - 1) / 2.0 + STEP * (chunk * LANES - (COLS - 1) / 2.0)
    first, last = span(middle - 52.5, middle + 52.5 + STEP * 128 + 1, CELLS // LANES)
    value = 0.0
    for near in (0.0, 1.0):
        detector = left + near
        weight = jnp.maximum(0.0, 1.0 - jnp.abs(detector - centre))
        value = value + weight * pick(tiles, first, last, detector.astype(jnp.int32))
    return value


def main_kernel(
    subset_hbm, row_start_hbm, order_hbm, axial_hbm, volume_hbm, scale_hbm, measured_hbm, norm_hbm,
    back, residual, volume, scale, moved, depth,
    subset, row_start, order, axial, measured, norm, rowsum, straight, sino, aux, every, every_aux, every_wide, tall, weight, wide, matrix,
    remainder, ratio, linear, arrived,
    volume_sem, small_sem, load_sem, send_sem, recv_sem, aux_send, aux_recv,
    near_send, near_recv, aux2_send, aux2_recv, input_send, input_recv, out_send, out_recv,
):
    f32, bf16 = jnp.float32, jnp.bfloat16
    block = DEPTH // PARTS
    g, m = lax.axis_index("grp"), lax.axis_index("blk")
    core = g % 2
    y, z, x = (m // 16) * 2 + g // 2, (m // 4) % 4, m % 4
    sibling = (g - core + (1 - core), m)

    ys, zs, xs = ([(place + step) % 4 for step in range(4)] for place in (y, z, x))
    group_of = [place % 2 * 2 + core for place in ys]
    plane_of = [place // 2 * 16 for place in ys]
    line_of = [[row * 4 + col for col in xs] for row in zs]

    def partner(offset):
        return group_of[offset[0]], plane_of[offset[0]] + line_of[offset[1]][offset[2]]

    def partner_slot(offset):
        return ys[offset[0]] * 16 + line_of[offset[1]][offset[2]]

    def arrived_all(ref, sem):
        return pltpu.make_async_copy(ref, ref, sem)

    here_chip = y * 16 + z * 4 + x

    def slot(number, members=1):
        return pl.ds(pl.multiple_of(number * 16, 16), members * 16)

    def remote(source_ref, target_ref, send, recv, device):
        return pltpu.make_async_remote_copy(
            src_ref=source_ref, dst_ref=target_ref, send_sem=send, recv_sem=recv,
            device_id=device, device_id_type=MESH,
        )

    small = [
        pltpu.make_async_copy(subset_hbm, subset, small_sem.at[0]),
        pltpu.make_async_copy(row_start_hbm, row_start, small_sem.at[1]),
        pltpu.make_async_copy(axial_hbm, axial, small_sem.at[2]),
        pltpu.make_async_copy(order_hbm, order, small_sem.at[3]),
    ]
    for copy in small:
        copy.start()
    bring = []
    for q in range(2):
        for part in range(PARTS):
            here = pl.ds(part * block, block)
            bring.append(pltpu.make_async_copy(volume_hbm.at[q, here], volume.at[q, here], volume_sem.at[q * PARTS + part]))
    for copy in bring:
        copy.start()
    mine = pl.ds(pl.multiple_of(core * ROWS, ROWS), ROWS)
    other = pl.ds(pl.multiple_of((1 - core) * ROWS, ROWS), ROWS)
    load = [
        pltpu.make_async_copy(
            array.at[:, chunk, :], target.at[mine, pl.ds(chunk * LANES, LANES)], load_sem.at[number * 8 + chunk]
        )
        for number, (array, target) in enumerate(((measured_hbm, measured), (norm_hbm, norm))) for chunk in range(8)
    ]
    load_scale = pltpu.make_async_copy(scale_hbm, scale, load_sem.at[16])

    barrier = pltpu.get_barrier_semaphore()

    for offset in OFFSETS:
        pl.semaphore_signal(barrier, inc=1, device_id=partner(offset), device_id_type=MESH)
    pl.semaphore_signal(barrier, inc=1, device_id=sibling, device_id_type=MESH)

    for copy in small:
        copy.wait()
    sine = sines(subset, lax.broadcasted_iota(jnp.int32, (ANGLES, LANES), 0))
    shift = (0.05 * CELLS) * sine
    moved[...] = shift
    tiles, means = [], []
    for q in range(2):
        total = 0.0
        for part in range(PARTS):
            cell = (lax.broadcasted_iota(jnp.int32, (ANGLES, block), 1) + part * block).astype(f32)
            high, low = halves(depth_weight(cell, sine[:, :1]))
            bring[q * PARTS + part].wait()
            volume_high, volume_low = halves(volume[q, part * block:(part + 1) * block, :])
            both = dot(jnp.concatenate([high, low], axis=0), volume_high)
            total = total + (both[:ANGLES] + (both[ANGLES:] + dot(high, volume_low)))
        middle = jnp.sum(total, axis=1, keepdims=True) * (1.0 / COLS)
        means.append(middle)
        total = total - middle
        tiles.append([total[:, t * LANES:(t + 1) * LANES] for t in range(COLS // LANES)])
    for copy in load:
        copy.start()
    load_scale.start()
    for chunk in range(CELLS // LANES):
        values, sums = ray_sums(tiles, shift, chunk)
        rowsum[:, chunk * LANES:(chunk + 1) * LANES] = sums
        for q in range(2):
            straight[pl.ds(q * 8 + chunk, ANGLES, stride=16), :] = values[q]
    sino[...] = straight[:512].astype(bf16)

    lane = lax.broadcasted_iota(jnp.int32, (ANGLES, LANES), 1)
    first = jnp.sum(jnp.where(lane == g * 32 + m, row_start[...], 0), axis=1, keepdims=True).astype(f32)
    table = jnp.concatenate([axial[...].reshape(16, ANGLES), jnp.zeros((16, LANES - ANGLES), f32)], axis=1)
    table = jnp.concatenate([table, jnp.zeros((LANES - 16, LANES), f32)], axis=0).T[:ANGLES]
    for number, column in ((16, first), (17, means[0]), (18, means[1])):
        table = jnp.where(lane == number, column, table)
    aux[...] = table.reshape(ANGLES, 1, LANES)

    pl.semaphore_wait(barrier, 64)

    for offset in OFFSETS:
        device = partner(offset)
        remote(
            aux.at[device[1]], every_aux.at[core * 64 + here_chip], aux_send.at[0], aux_recv.at[offset[0]], device
        ).start()
        remote(
            sino.at[slot(device[1])], every.at[slot(core * 64 + here_chip)], send_sem.at[0], recv_sem.at[offset[0]], device
        ).start()
    every[slot(core * 64 + here_chip)] = sino[slot(m)]
    every_aux[core * 64 + here_chip] = aux[m]

    for copy in load:
        copy.wait()

    def near_input(number, rows):
        target = (measured, norm)[number].at[rows]
        return remote(target, target, input_send.at[number], input_recv.at[number], sibling)

    near_input(0, mine).start()
    near_input(1, mine).start()

    rows = order[...].astype(f32)
    lower = jnp.concatenate([rows[i:i + 1] for i in range(3)], axis=1)
    upper = jnp.concatenate([rows[i:i + 1] for i in range(3, 6)], axis=1)
    rows = jnp.where(y % 2 == 0, lower, upper)
    own_sum = rowsum[pl.ds(m, 1), :]

    def first_slot(number, side):
        return pl.multiple_of(side * 64 + ys[(4 - number) % 4] * 16, 16)

    def near_rows(number, side):
        here = slot(first_slot(number, side), 16)
        return remote(every.at[here], every.at[here], near_send.at[number], near_recv.at[number], sibling)

    def near_aux(number, side):
        here = pl.ds(first_slot(number, side), 16)
        return remote(every_aux.at[here], every_aux.at[here], aux2_send.at[number], aux2_recv.at[number], sibling)

    def place(step, number, side, turn):
        low = first_slot(number, side)
        table = every_aux[pl.ds(low, 16)].reshape(16, LANES)
        offset = (rows - table[:, 16:17]).astype(jnp.int32)
        inside, entry = (offset >= 0) & (offset < FOOT), offset & (FOOT - 1)
        lane = lax.broadcasted_iota(jnp.int32, (16, LANES), 1)
        every_wide[...] = every[slot(low, 16), :].astype(f32)
        for q in range(2):
            value = jnp.where(inside, jnp.concatenate([
                jnp.take_along_axis(
                    table, entry[:, part * LANES:(part + 1) * LANES] + q * FOOT, axis=1, mode="promise_in_bounds"
                )
                for part in range(3)
            ], axis=1), 0.0)
            line = step * 64 + turn * 32 + q * 16
            tall[line:line + 16, :] = value
            if turn == 0:
                high, low_part = halves(value)
                weight[step * 32 + q * 16:step * 32 + q * 16 + 16, :] = high
                weight[128 + step * 32 + q * 16:128 + step * 32 + q * 16 + 16, :] = low_part
            for chunk in range(8):
                matrix[line:line + 16, chunk * LANES:(chunk + 1) * LANES] = (
                    every_wide[pl.ds(q * 8 + chunk, 16, stride=16), :].astype(bf16)
                )
            high, low_part = halves(table[:, 17 + q:18 + q])
            level = jnp.where(lane == 0, high.astype(f32), jnp.where(lane == 1, low_part.astype(f32), 0.0))
            matrix[line:line + 16, CELLS:CELLS + LANES] = level.astype(bf16)

    def own_rows(step, number):
        low, count = first_slot(number, core), 15 if number == 0 else 16
        arrived_all(every_aux.at[pl.ds(low, count)], aux_recv.at[number]).wait()
        near_aux(number, core).start()
        arrived_all(every.at[slot(low, count)], recv_sem.at[number]).wait()
        near_rows(number, core).start()
        place(step, number, core, 0)

    def sibling_rows(step, number):
        near_aux(number, 1 - core).wait_recv()
        near_rows(number, 1 - core).wait_recv()
        place(step, number, 1 - core, 1)

    def turn_over(part):
        high, low = halves(tall[part * LANES:(part + 1) * LANES, :].T)
        wide[:, part * LANES:(part + 1) * LANES] = high
        wide[:, 256 + part * LANES:256 + (part + 1) * LANES] = low

    sequence = (0, 1, 3, 2)
    own_rows(0, 0)
    own_rows(1, 1)
    sibling_rows(0, 0)
    own_rows(2, 3)
    sibling_rows(1, 1)
    turn_over(0)
    near_input(0, other).wait_recv()
    near_input(1, other).wait_recv()
    own_rows(3, 2)
    sibling_rows(2, 3)
    sibling_rows(3, 2)
    turn_over(1)

    def product(here):
        right = matrix[:, here]
        return dot(wide[...], jnp.concatenate([right, right], axis=0))

    level = product(slice(CELLS, CELLS + LANES))
    level = jnp.broadcast_to(level[:, 0:1] + level[:, 1:2], (2 * ROWS, LANES))

    def forward(pair):
        value = product(slice(pair * 256, (pair + 1) * 256))
        for side in range(2):
            here = slice((2 * pair + side) * LANES, (2 * pair + side + 1) * LANES)
            found = value[:, side * LANES:(side + 1) * LANES] + level * own_sum[:, here]
            rest = norm[:, here] * (measured[:, here] - found)
            remainder[:, here] = rest
            ratio[:, here] = rest.astype(bf16)

    def collect(pair):
        both = dot(weight[...], ratio[:, pair * 256:(pair + 1) * 256])
        value = both[:128] + both[128:]
        for step, number in enumerate(sequence):
            low = first_slot(number, 0) * 16
            for q in range(2):
                line = step * 32 + q * 16
                for side in range(2):
                    straight[pl.ds(low + q * 8 + 2 * pair + side, 16, stride=16), :] = (
                        value[line:line + 16, side * LANES:(side + 1) * LANES]
                    )

    for pair in range(4):
        forward(pair)
        collect(pair)

    arrival = (y % 2) * 32 + m
    for offset in OFFSETS:
        rows = slot(partner_slot(offset))
        linear[rows] = straight[rows].astype(bf16)
        remote(linear.at[rows], arrived.at[slot(arrival)], out_send.at[0], out_recv.at[0], partner(offset)).start()
    arrived[slot(arrival)] = straight[slot(here_chip)].astype(bf16)

    keep = [
        pltpu.make_async_copy(
            remainder.at[mine, pl.ds(chunk * LANES, LANES)], residual.at[:, chunk, :], load_sem.at[17 + chunk]
        )
        for chunk in range(8)
    ]
    for copy in keep:
        copy.start()
    sine_row = sines(subset, lax.broadcasted_iota(jnp.int32, (8, LANES), 1) % ANGLES)[:1]
    for part in range(PARTS):
        cell = (lax.broadcasted_iota(jnp.int32, (block, LANES), 0) + part * block).astype(f32)
        lane = lax.broadcasted_iota(jnp.int32, (block, LANES), 1)
        value = depth_weight(cell, sine_row)
        high = value.astype(bf16).astype(f32)
        depth[part * block:(part + 1) * block, :] = jnp.where(lane < 2 * ANGLES, high, value - high).astype(bf16)

    arrived_all(every.at[slot(0, 63)], send_sem.at[0]).wait()
    arrived_all(every_aux.at[pl.ds(0, 63)], aux_send.at[0]).wait()
    for number in range(4):
        near_rows(number, core).wait_send()
        near_aux(number, core).wait_send()
    for number in range(2):
        near_input(number, mine).wait_send()
    load_scale.wait()
    for copy in keep:
        copy.wait()

    arrived_all(arrived.at[slot(0, 63)], out_recv.at[0]).wait()
    back[...] = arrived[...]
    arrived_all(linear.at[slot(0, 63)], out_send.at[0]).wait()


def final_kernel(moved, depth, back, volume, scale, residual_in, new_volume, residual, straight, spread, staged, sems, rest_sem):
    f32 = jnp.float32
    block = DEPTH // OUT_PARTS
    keep = pltpu.make_async_copy(residual_in, residual, rest_sem)
    keep.start()
    straight[...] = back[:512].astype(f32) + back[512:].astype(f32)
    shift = moved[...]
    copies = []
    for q in range(2):
        tiles = [straight[pl.ds(q * 8 + chunk, ANGLES, stride=16), :] for chunk in range(CELLS // LANES)]
        for chunk in range(COLS // LANES):
            high, low = halves(spread_rows(tiles, shift, chunk))
            here = slice(chunk * LANES, (chunk + 1) * LANES)
            spread[q, 0:ANGLES, here] = high
            spread[q, ANGLES:2 * ANGLES, here] = low
            spread[q, 2 * ANGLES:3 * ANGLES, here] = high
            spread[q, 3 * ANGLES:4 * ANGLES, here] = jnp.zeros_like(high)
        for part in range(OUT_PARTS):
            here = slice(part * block, (part + 1) * block)
            update = dot(depth[here, :], spread[q])
            staged[q, here, :] = jnp.maximum(0.0, volume[q, here, :] + scale[q, here, :] * update)
            rows = pl.ds(part * block, block)
            copies.append(pltpu.make_async_copy(staged.at[q, rows], new_volume.at[q, rows], sems.at[q * OUT_PARTS + part]))
            copies[-1].start()
    for copy in copies:
        copy.wait()
    keep.wait()


def shards(volume, voxel_norm, measured, ray_norm, axial_weights, row_start, row_order, subset):
    f32, bf16 = jnp.float32, jnp.bfloat16
    vmem = pl.BlockSpec(memory_space=pltpu.VMEM)
    hbm = pl.BlockSpec(memory_space=pltpu.HBM)
    dma = pltpu.SemaphoreType.DMA
    back, residual, volume_near, scale_near, moved, depth = pl.pallas_call(
        main_kernel,
        in_specs=[hbm] * 8,
        out_specs=(vmem, hbm, vmem, vmem, vmem, vmem),
        out_shape=(
            jax.ShapeDtypeStruct((1024, LANES), bf16), jax.ShapeDtypeStruct((ROWS, 8, LANES), f32),
            jax.ShapeDtypeStruct(volume.shape, f32), jax.ShapeDtypeStruct(volume.shape, f32),
            jax.ShapeDtypeStruct((ANGLES, LANES), f32), jax.ShapeDtypeStruct((DEPTH, LANES), bf16),
        ),
        scratch_shapes=[
            pltpu.SMEM((ANGLES,), jnp.int32), pltpu.VMEM((ANGLES, 4 * ANGLES), jnp.int32),
            pltpu.VMEM((6, LANES), jnp.int32), pltpu.VMEM((2, FOOT, ANGLES), f32),
            pltpu.VMEM((2 * ROWS, CELLS), f32), pltpu.VMEM((2 * ROWS, CELLS), f32),
            pltpu.VMEM((ANGLES, CELLS), f32), pltpu.VMEM((1024, LANES), f32), pltpu.VMEM((512, LANES), bf16),
            pltpu.VMEM((ANGLES, 1, LANES), f32), pltpu.VMEM((2048, LANES), bf16), pltpu.VMEM((128, 1, LANES), f32),
            pltpu.VMEM((256, LANES), f32), pltpu.VMEM((256, 2 * ROWS), f32), pltpu.VMEM((256, 2 * ROWS), bf16),
            pltpu.VMEM((2 * ROWS, 512), bf16), pltpu.VMEM((256, CELLS + LANES), bf16),
            pltpu.VMEM((2 * ROWS, CELLS), f32), pltpu.VMEM((2 * ROWS, CELLS), bf16),
            pltpu.VMEM((1024, LANES), bf16), pltpu.VMEM((1024, LANES), bf16),
            dma((2 * PARTS,)), dma((4,)), dma((25,)), dma((1,)), dma((4,)), dma((1,)), dma((4,)),
            dma((4,)), dma((4,)), dma((4,)), dma((4,)), dma((2,)), dma((2,)), dma((1,)), dma((1,)),
        ],
        compiler_params=pltpu.CompilerParams(collective_id=0, has_side_effects=True, vmem_limit_bytes=28 << 20),
        cost_estimate=pl.CostEstimate(flops=10 ** 9, bytes_accessed=100 << 20, transcendentals=0),
        name="exchange",
    )(
        *[pltpu.with_memory_space_constraint(array, pltpu.HBM) for array in (
            subset, row_start, row_order.reshape(6, LANES), jnp.transpose(axial_weights, (0, 2, 1)), volume, voxel_norm,
            measured.reshape(ROWS, 8, LANES), ray_norm.reshape(ROWS, 8, LANES),
        )]
    )
    new_volume, residual = pl.pallas_call(
        final_kernel,
        in_specs=[vmem, vmem, vmem, vmem, vmem, pl.BlockSpec(memory_space=pl.ANY)],
        out_specs=(hbm, hbm),
        out_shape=(jax.ShapeDtypeStruct(volume.shape, f32), jax.ShapeDtypeStruct((ROWS, 8, LANES), f32)),
        scratch_shapes=[
            pltpu.VMEM((512, LANES), f32), pltpu.VMEM((2, LANES, COLS), bf16), pltpu.VMEM(volume.shape, f32),
            dma((2 * OUT_PARTS,)), dma,
        ],
        compiler_params=pltpu.CompilerParams(vmem_limit_bytes=28 << 20),
        cost_estimate=pl.CostEstimate(flops=6 * 64 * DEPTH * COLS, bytes_accessed=4 * 6 * DEPTH * COLS, transcendentals=0),
        name="final",
    )(moved, depth, back, volume_near, scale_near, residual)
    return new_volume, residual.reshape(measured.shape)


def solution(mesh):
    placed = (
        P(("grp", "blk"), None, None),
        P(("grp", "blk"), None, None),
        P("grp", "blk", None),
        P("grp", "blk", None),
        P(("grp", "blk"), None, None),
        P(),
        P(),
        P(),
    )
    return jax.shard_map(
        shards,
        mesh=mesh,
        in_specs=placed,
        out_specs=(P(("grp", "blk"), None, None), P("grp", "blk", None)),
        check_vma=False,
    )
```

```python
import itertools
import math

import jax
import jax.numpy as jnp
from jax import lax
from jax.experimental import pallas as pl
from jax.experimental.pallas import tpu as pltpu
from jax.sharding import PartitionSpec as P

TOTAL_ANG = 1024
MESH = pl.DeviceIdType.MESH
LANES = 128
ANGLES = 32
FOOT = 8
COLS = 768
DEPTH = 768
CELLS = 1024
ROWS = 192
PARTS = 3
OUT_PARTS = 6
OFFSETS = sorted(
    itertools.product(range(4), repeat=3), key=lambda offset: -sum(min(step, 4 - step) for step in offset)
)[:-1]
STEP = 0.8 * CELLS / COLS


def halves(value):
    high = value.astype(jnp.bfloat16)
    return high, (value - high.astype(jnp.float32)).astype(jnp.bfloat16)


def dot(left, right):
    return jnp.dot(left, right, preferred_element_type=jnp.float32)


def depth_weight(cell, sine):
    middle = (DEPTH - 1) / 2.0 * (1.0 + 0.8 * sine)
    bump = jnp.maximum(0.0, 1.0 - jnp.abs(cell - middle) / (0.1 * DEPTH))
    return (1.0 + 2.0 * bump) / DEPTH


def centre_of(col, shift):
    return ((CELLS - 1) / 2.0 + STEP * (col - (COLS - 1) / 2.0)) + shift


def pick(tiles, first, last, index):
    inside = index & (LANES - 1)
    tile = index >> 7
    value = None
    for number in range(first, last + 1):
        found = jnp.take_along_axis(tiles[number], inside, axis=1, mode="promise_in_bounds")
        value = found if value is None else jnp.where(tile == number, found, value)
    return value


def span(low, high, tiles):
    first = max(0, min(tiles - 1, math.floor(low) // LANES))
    return first, max(first, min(tiles - 1, math.floor(high) // LANES))


def sines(subset_ref, which):
    chosen = jnp.zeros_like(which)
    for angle in range(ANGLES):
        chosen = jnp.where(which == angle, subset_ref[angle], chosen)
    return jnp.sin(2.0 * math.pi / TOTAL_ANG * chosen.astype(jnp.float32))


def ray_sums(tiles, shift, chunk):
    lane = lax.broadcasted_iota(jnp.int32, (ANGLES, LANES), 1).astype(jnp.float32)
    detector = lane + chunk * LANES
    nearest = jnp.floor((detector - (CELLS - 1) / 2.0 - shift) * (1.0 / STEP) + (COLS - 1) / 2.0)
    middle = (chunk * LANES - (CELLS - 1) / 2.0) / STEP + (COLS - 1) / 2.0
    first, last = span(middle - 49.5, middle + 49.5 + 128 / STEP + 1, COLS // LANES)
    values, total = [0.0, 0.0], 0.0
    for near in (0.0, 1.0):
        col = nearest + near
        weight = jnp.maximum(0.0, 1.0 - jnp.abs(detector - centre_of(col, shift)))
        weight = jnp.where((col >= 0.0) & (col <= COLS - 1.0), weight, 0.0)
        index = col.astype(jnp.int32)
        values = [value + weight * pick(tile, first, last, index) for value, tile in zip(values, tiles)]
        total = total + weight
    return values, total


def spread_rows(tiles, shift, chunk):
    lane = lax.broadcasted_iota(jnp.int32, (ANGLES, LANES), 1).astype(jnp.float32)
    centre = centre_of(lane + chunk * LANES, shift)
    left = jnp.floor(centre)
    middle = (CELLS - 1) / 2.0 + STEP * (chunk * LANES - (COLS - 1) / 2.0)
    first, last = span(middle - 52.5, middle + 52.5 + STEP * 128 + 1, CELLS // LANES)
    value = 0.0
    for near in (0.0, 1.0):
        detector = left + near
        weight = jnp.maximum(0.0, 1.0 - jnp.abs(detector - centre))
        value = value + weight * pick(tiles, first, last, detector.astype(jnp.int32))
    return value


def main_kernel(
    subset_hbm, row_start_hbm, order_hbm, axial_hbm, volume_hbm, scale_hbm, measured_hbm, norm_hbm,
    back, residual, volume, scale, moved, depth,
    subset, row_start, order, axial, measured, norm, rowsum, straight, sino, aux, every, every_aux, every_wide, tall, weight, wide, matrix,
    remainder, ratio, linear, arrived,
    volume_sem, small_sem, load_sem, send_sem, recv_sem, aux_send, aux_recv,
    near_send, near_recv, aux2_send, aux2_recv, input_send, input_recv, out_send, out_recv,
):
    f32, bf16 = jnp.float32, jnp.bfloat16
    block = DEPTH // PARTS
    g, m = lax.axis_index("grp"), lax.axis_index("blk")
    core = g % 2
    y, z, x = (m // 16) * 2 + g // 2, (m // 4) % 4, m % 4
    sibling = (g - core + (1 - core), m)

    ys, zs, xs = ([(place + step) % 4 for step in range(4)] for place in (y, z, x))
    group_of = [place % 2 * 2 + core for place in ys]
    plane_of = [place // 2 * 16 for place in ys]
    line_of = [[row * 4 + col for col in xs] for row in zs]

    def partner(offset):
        return group_of[offset[0]], plane_of[offset[0]] + line_of[offset[1]][offset[2]]

    def partner_slot(offset):
        return ys[offset[0]] * 16 + line_of[offset[1]][offset[2]]

    def arrived_all(ref, sem):
        return pltpu.make_async_copy(ref, ref, sem)

    here_chip = y * 16 + z * 4 + x

    def slot(number, members=1):
        return pl.ds(pl.multiple_of(number * 16, 16), members * 16)

    def remote(source_ref, target_ref, send, recv, device):
        return pltpu.make_async_remote_copy(
            src_ref=source_ref, dst_ref=target_ref, send_sem=send, recv_sem=recv,
            device_id=device, device_id_type=MESH,
        )

    small = [
        pltpu.make_async_copy(subset_hbm, subset, small_sem.at[0]),
        pltpu.make_async_copy(row_start_hbm, row_start, small_sem.at[1]),
        pltpu.make_async_copy(axial_hbm, axial, small_sem.at[2]),
        pltpu.make_async_copy(order_hbm, order, small_sem.at[3]),
    ]
    for copy in small:
        copy.start()
    bring = []
    for q in range(2):
        for part in range(PARTS):
            here = pl.ds(part * block, block)
            bring.append(pltpu.make_async_copy(volume_hbm.at[q, here], volume.at[q, here], volume_sem.at[q * PARTS + part]))
    for copy in bring:
        copy.start()
    mine = pl.ds(pl.multiple_of(core * ROWS, ROWS), ROWS)
    other = pl.ds(pl.multiple_of((1 - core) * ROWS, ROWS), ROWS)
    load = [
        pltpu.make_async_copy(
            array.at[:, chunk, :], target.at[mine, pl.ds(chunk * LANES, LANES)], load_sem.at[number * 8 + chunk]
        )
        for number, (array, target) in enumerate(((measured_hbm, measured), (norm_hbm, norm))) for chunk in range(8)
    ]
    load_scale = pltpu.make_async_copy(scale_hbm, scale, load_sem.at[16])

    barrier = pltpu.get_barrier_semaphore()

    for offset in OFFSETS:
        pl.semaphore_signal(barrier, inc=1, device_id=partner(offset), device_id_type=MESH)
    pl.semaphore_signal(barrier, inc=1, device_id=sibling, device_id_type=MESH)

    for copy in small:
        copy.wait()
    sine = sines(subset, lax.broadcasted_iota(jnp.int32, (ANGLES, LANES), 0))
    shift = (0.05 * CELLS) * sine
    moved[...] = shift
    tiles, means = [], []
    for q in range(2):
        total = 0.0
        for part in range(PARTS):
            cell = (lax.broadcasted_iota(jnp.int32, (ANGLES, block), 1) + part * block).astype(f32)
            high, low = halves(depth_weight(cell, sine[:, :1]))
            bring[q * PARTS + part].wait()
            volume_high, volume_low = halves(volume[q, part * block:(part + 1) * block, :])
            both = dot(jnp.concatenate([high, low], axis=0), volume_high)
            total = total + (both[:ANGLES] + (both[ANGLES:] + dot(high, volume_low)))
        middle = jnp.sum(total, axis=1, keepdims=True) * (1.0 / COLS)
        means.append(middle)
        total = total - middle
        tiles.append([total[:, t * LANES:(t + 1) * LANES] for t in range(COLS // LANES)])
    for copy in load:
        copy.start()
    load_scale.start()
    for chunk in range(CELLS // LANES):
        values, sums = ray_sums(tiles, shift, chunk)
        rowsum[:, chunk * LANES:(chunk + 1) * LANES] = sums
        for q in range(2):
            straight[pl.ds(q * 8 + chunk, ANGLES, stride=16), :] = values[q]
    sino[...] = straight[:512].astype(bf16)

    lane = lax.broadcasted_iota(jnp.int32, (ANGLES, LANES), 1)
    first = jnp.sum(jnp.where(lane == g * 32 + m, row_start[...], 0), axis=1, keepdims=True).astype(f32)
    table = jnp.concatenate([axial[...].reshape(16, ANGLES), jnp.zeros((16, LANES - ANGLES), f32)], axis=1)
    table = jnp.concatenate([table, jnp.zeros((LANES - 16, LANES), f32)], axis=0).T[:ANGLES]
    for number, column in ((16, first), (17, means[0]), (18, means[1])):
        table = jnp.where(lane == number, column, table)
    aux[...] = table.reshape(ANGLES, 1, LANES)

    pl.semaphore_wait(barrier, 64)

    for offset in OFFSETS:
        device = partner(offset)
        remote(
            aux.at[device[1]], every_aux.at[core * 64 + here_chip], aux_send.at[0], aux_recv.at[offset[0]], device
        ).start()
        remote(
            sino.at[slot(device[1])], every.at[slot(core * 64 + here_chip)], send_sem.at[0], recv_sem.at[offset[0]], device
        ).start()
    every[slot(core * 64 + here_chip)] = sino[slot(m)]
    every_aux[core * 64 + here_chip] = aux[m]

    for copy in load:
        copy.wait()

    def near_input(number, rows):
        target = (measured, norm)[number].at[rows]
        return remote(target, target, input_send.at[number], input_recv.at[number], sibling)

    near_input(0, mine).start()
    near_input(1, mine).start()

    rows = order[...].astype(f32)
    lower = jnp.concatenate([rows[i:i + 1] for i in range(3)], axis=1)
    upper = jnp.concatenate([rows[i:i + 1] for i in range(3, 6)], axis=1)
    rows = jnp.where(y % 2 == 0, lower, upper)
    own_sum = rowsum[pl.ds(m, 1), :]

    def first_slot(number, side):
        return pl.multiple_of(side * 64 + ys[(4 - number) % 4] * 16, 16)

    def near_rows(number, side):
        here = slot(first_slot(number, side), 16)
        return remote(every.at[here], every.at[here], near_send.at[number], near_recv.at[number], sibling)

    def near_aux(number, side):
        here = pl.ds(first_slot(number, side), 16)
        return remote(every_aux.at[here], every_aux.at[here], aux2_send.at[number], aux2_recv.at[number], sibling)

    def place(step, number, side, turn):
        low = first_slot(number, side)
        table = every_aux[pl.ds(low, 16)].reshape(16, LANES)
        offset = (rows - table[:, 16:17]).astype(jnp.int32)
        inside, entry = (offset >= 0) & (offset < FOOT), offset & (FOOT - 1)
        lane = lax.broadcasted_iota(jnp.int32, (16, LANES), 1)
        every_wide[...] = every[slot(low, 16), :].astype(f32)
        for q in range(2):
            value = jnp.where(inside, jnp.concatenate([
                jnp.take_along_axis(
                    table, entry[:, part * LANES:(part + 1) * LANES] + q * FOOT, axis=1, mode="promise_in_bounds"
                )
                for part in range(3)
            ], axis=1), 0.0)
            line = step * 64 + turn * 32 + q * 16
            tall[line:line + 16, :] = value
            if turn == 0:
                high, low_part = halves(value)
                weight[step * 32 + q * 16:step * 32 + q * 16 + 16, :] = high
                weight[128 + step * 32 + q * 16:128 + step * 32 + q * 16 + 16, :] = low_part
            for chunk in range(8):
                matrix[line:line + 16, chunk * LANES:(chunk + 1) * LANES] = (
                    every_wide[pl.ds(q * 8 + chunk, 16, stride=16), :].astype(bf16)
                )
            high, low_part = halves(table[:, 17 + q:18 + q])
            level = jnp.where(lane == 0, high.astype(f32), jnp.where(lane == 1, low_part.astype(f32), 0.0))
            matrix[line:line + 16, CELLS:CELLS + LANES] = level.astype(bf16)

    def own_rows(step, number):
        low, count = first_slot(number, core), 15 if number == 0 else 16
        arrived_all(every_aux.at[pl.ds(low, count)], aux_recv.at[number]).wait()
        near_aux(number, core).start()
        arrived_all(every.at[slot(low, count)], recv_sem.at[number]).wait()
        near_rows(number, core).start()
        place(step, number, core, 0)

    def sibling_rows(step, number):
        near_aux(number, 1 - core).wait_recv()
        near_rows(number, 1 - core).wait_recv()
        place(step, number, 1 - core, 1)

    def turn_over(part):
        high, low = halves(tall[part * LANES:(part + 1) * LANES, :].T)
        wide[part, :, 0:LANES] = high
        wide[part, :, LANES:2 * LANES] = low

    def product(part, here):
        right = matrix[part * LANES:(part + 1) * LANES, here]
        return dot(wide[part], jnp.concatenate([right, right], axis=0))

    def level_of(part):
        value = product(part, slice(CELLS, CELLS + LANES))
        return jnp.broadcast_to(value[:, 0:1] + value[:, 1:2], (2 * ROWS, LANES))

    def sums(part, pair, level):
        value = product(part, slice(pair * 256, (pair + 1) * 256))
        for side in range(2):
            here = slice((2 * pair + side) * LANES, (2 * pair + side + 1) * LANES)
            yield here, value[:, side * LANES:(side + 1) * LANES] + level * own_sum[:, here]

    sequence = (0, 1, 3, 2)
    own_rows(0, 0)
    own_rows(1, 1)
    sibling_rows(0, 0)
    own_rows(2, 3)
    sibling_rows(1, 1)
    turn_over(0)
    near_input(0, other).wait_recv()
    near_input(1, other).wait_recv()
    own_rows(3, 2)
    near_input(0, mine).wait_send()
    level = level_of(0)
    for pair in range(4):
        for here, found in sums(0, pair, level):
            measured[:, here] = measured[:, here] - found
    sibling_rows(2, 3)
    sibling_rows(3, 2)
    turn_over(1)

    level = level_of(1)

    def forward(pair):
        for here, found in sums(1, pair, level):
            rest = norm[:, here] * (measured[:, here] - found)
            remainder[:, here] = rest
            ratio[:, here] = rest.astype(bf16)

    def collect(pair):
        both = dot(weight[...], ratio[:, pair * 256:(pair + 1) * 256])
        value = both[:128] + both[128:]
        for step, number in enumerate(sequence):
            low = first_slot(number, 0) * 16
            for q in range(2):
                line = step * 32 + q * 16
                for side in range(2):
                    straight[pl.ds(low + q * 8 + 2 * pair + side, 16, stride=16), :] = (
                        value[line:line + 16, side * LANES:(side + 1) * LANES]
                    )

    for pair in range(4):
        forward(pair)
        collect(pair)

    arrival = (y % 2) * 32 + m
    for offset in OFFSETS:
        rows = slot(partner_slot(offset))
        linear[rows] = straight[rows].astype(bf16)
        remote(linear.at[rows], arrived.at[slot(arrival)], out_send.at[0], out_recv.at[0], partner(offset)).start()
    arrived[slot(arrival)] = straight[slot(here_chip)].astype(bf16)

    keep = [
        pltpu.make_async_copy(
            remainder.at[mine, pl.ds(chunk * LANES, LANES)], residual.at[:, chunk, :], load_sem.at[17 + chunk]
        )
        for chunk in range(8)
    ]
    for copy in keep:
        copy.start()
    sine_row = sines(subset, lax.broadcasted_iota(jnp.int32, (8, LANES), 1) % ANGLES)[:1]
    for part in range(PARTS):
        cell = (lax.broadcasted_iota(jnp.int32, (block, LANES), 0) + part * block).astype(f32)
        lane = lax.broadcasted_iota(jnp.int32, (block, LANES), 1)
        value = depth_weight(cell, sine_row)
        high = value.astype(bf16).astype(f32)
        depth[part * block:(part + 1) * block, :] = jnp.where(lane < 2 * ANGLES, high, value - high).astype(bf16)

    arrived_all(every.at[slot(0, 63)], send_sem.at[0]).wait()
    arrived_all(every_aux.at[pl.ds(0, 63)], aux_send.at[0]).wait()
    for number in range(4):
        near_rows(number, core).wait_send()
        near_aux(number, core).wait_send()
    near_input(1, mine).wait_send()
    load_scale.wait()
    for copy in keep:
        copy.wait()

    arrived_all(arrived.at[slot(0, 63)], out_recv.at[0]).wait()
    back[...] = arrived[...]
    arrived_all(linear.at[slot(0, 63)], out_send.at[0]).wait()


def final_kernel(moved, depth, back, volume, scale, residual_in, new_volume, residual, straight, spread, staged, sems, rest_sem):
    f32 = jnp.float32
    block = DEPTH // OUT_PARTS
    keep = pltpu.make_async_copy(residual_in, residual, rest_sem)
    keep.start()
    straight[...] = back[:512].astype(f32) + back[512:].astype(f32)
    shift = moved[...]
    copies = []
    for q in range(2):
        tiles = [straight[pl.ds(q * 8 + chunk, ANGLES, stride=16), :] for chunk in range(CELLS // LANES)]
        for chunk in range(COLS // LANES):
            high, low = halves(spread_rows(tiles, shift, chunk))
            here = slice(chunk * LANES, (chunk + 1) * LANES)
            spread[q, 0:ANGLES, here] = high
            spread[q, ANGLES:2 * ANGLES, here] = low
            spread[q, 2 * ANGLES:3 * ANGLES, here] = high
            spread[q, 3 * ANGLES:4 * ANGLES, here] = jnp.zeros_like(high)
        for part in range(OUT_PARTS):
            here = slice(part * block, (part + 1) * block)
            update = dot(depth[here, :], spread[q])
            staged[q, here, :] = jnp.maximum(0.0, volume[q, here, :] + scale[q, here, :] * update)
            rows = pl.ds(part * block, block)
            copies.append(pltpu.make_async_copy(staged.at[q, rows], new_volume.at[q, rows], sems.at[q * OUT_PARTS + part]))
            copies[-1].start()
    for copy in copies:
        copy.wait()
    keep.wait()


def shards(volume, voxel_norm, measured, ray_norm, axial_weights, row_start, row_order, subset):
    f32, bf16 = jnp.float32, jnp.bfloat16
    vmem = pl.BlockSpec(memory_space=pltpu.VMEM)
    hbm = pl.BlockSpec(memory_space=pltpu.HBM)
    dma = pltpu.SemaphoreType.DMA
    back, residual, volume_near, scale_near, moved, depth = pl.pallas_call(
        main_kernel,
        in_specs=[hbm] * 8,
        out_specs=(vmem, hbm, vmem, vmem, vmem, vmem),
        out_shape=(
            jax.ShapeDtypeStruct((1024, LANES), bf16), jax.ShapeDtypeStruct((ROWS, 8, LANES), f32),
            jax.ShapeDtypeStruct(volume.shape, f32), jax.ShapeDtypeStruct(volume.shape, f32),
            jax.ShapeDtypeStruct((ANGLES, LANES), f32), jax.ShapeDtypeStruct((DEPTH, LANES), bf16),
        ),
        scratch_shapes=[
            pltpu.SMEM((ANGLES,), jnp.int32), pltpu.VMEM((ANGLES, 4 * ANGLES), jnp.int32),
            pltpu.VMEM((6, LANES), jnp.int32), pltpu.VMEM((2, FOOT, ANGLES), f32),
            pltpu.VMEM((2 * ROWS, CELLS), f32), pltpu.VMEM((2 * ROWS, CELLS), f32),
            pltpu.VMEM((ANGLES, CELLS), f32), pltpu.VMEM((1024, LANES), f32), pltpu.VMEM((512, LANES), bf16),
            pltpu.VMEM((ANGLES, 1, LANES), f32), pltpu.VMEM((2048, LANES), bf16), pltpu.VMEM((128, 1, LANES), f32),
            pltpu.VMEM((256, LANES), f32), pltpu.VMEM((256, 2 * ROWS), f32), pltpu.VMEM((256, 2 * ROWS), bf16),
            pltpu.VMEM((2, 2 * ROWS, 256), bf16), pltpu.VMEM((256, CELLS + LANES), bf16),
            pltpu.VMEM((2 * ROWS, CELLS), f32), pltpu.VMEM((2 * ROWS, CELLS), bf16),
            pltpu.VMEM((1024, LANES), bf16), pltpu.VMEM((1024, LANES), bf16),
            dma((2 * PARTS,)), dma((4,)), dma((25,)), dma((1,)), dma((4,)), dma((1,)), dma((4,)),
            dma((4,)), dma((4,)), dma((4,)), dma((4,)), dma((2,)), dma((2,)), dma((1,)), dma((1,)),
        ],
        compiler_params=pltpu.CompilerParams(collective_id=0, has_side_effects=True, vmem_limit_bytes=28 << 20),
        cost_estimate=pl.CostEstimate(flops=10 ** 9, bytes_accessed=100 << 20, transcendentals=0),
        name="exchange",
    )(
        *[pltpu.with_memory_space_constraint(array, pltpu.HBM) for array in (
            subset, row_start, row_order.reshape(6, LANES), jnp.transpose(axial_weights, (0, 2, 1)), volume, voxel_norm,
            measured.reshape(ROWS, 8, LANES), ray_norm.reshape(ROWS, 8, LANES),
        )]
    )
    new_volume, residual = pl.pallas_call(
        final_kernel,
        in_specs=[vmem, vmem, vmem, vmem, vmem, pl.BlockSpec(memory_space=pl.ANY)],
        out_specs=(hbm, hbm),
        out_shape=(jax.ShapeDtypeStruct(volume.shape, f32), jax.ShapeDtypeStruct((ROWS, 8, LANES), f32)),
        scratch_shapes=[
            pltpu.VMEM((512, LANES), f32), pltpu.VMEM((2, LANES, COLS), bf16), pltpu.VMEM(volume.shape, f32),
            dma((2 * OUT_PARTS,)), dma,
        ],
        compiler_params=pltpu.CompilerParams(vmem_limit_bytes=28 << 20),
        cost_estimate=pl.CostEstimate(flops=6 * 64 * DEPTH * COLS, bytes_accessed=4 * 6 * DEPTH * COLS, transcendentals=0),
        name="final",
    )(moved, depth, back, volume_near, scale_near, residual)
    return new_volume, residual.reshape(measured.shape)


def solution(mesh):
    placed = (
        P(("grp", "blk"), None, None),
        P(("grp", "blk"), None, None),
        P("grp", "blk", None),
        P("grp", "blk", None),
        P(("grp", "blk"), None, None),
        P(),
        P(),
        P(),
    )
    return jax.shard_map(
        shards,
        mesh=mesh,
        in_specs=placed,
        out_specs=(P(("grp", "blk"), None, None), P("grp", "blk", None)),
        check_vma=False,
    )
```

```python
import itertools
import math

import jax
import jax.numpy as jnp
from jax import lax
from jax.experimental import pallas as pl
from jax.experimental.pallas import tpu as pltpu
from jax.sharding import PartitionSpec as P

TOTAL_ANG = 1024
MESH = pl.DeviceIdType.MESH
LANES = 128
ANGLES = 32
FOOT = 8
COLS = 768
DEPTH = 768
CELLS = 1024
ROWS = 192
PARTS = 3
OUT_PARTS = 6
OFFSETS = sorted(
    itertools.product(range(4), repeat=3), key=lambda offset: -sum(min(step, 4 - step) for step in offset)
)[:-1]
STEP = 0.8 * CELLS / COLS


def halves(value):
    high = value.astype(jnp.bfloat16)
    return high, (value - high.astype(jnp.float32)).astype(jnp.bfloat16)


def dot(left, right):
    return jnp.dot(left, right, preferred_element_type=jnp.float32)


def depth_weight(cell, sine):
    middle = (DEPTH - 1) / 2.0 * (1.0 + 0.8 * sine)
    bump = jnp.maximum(0.0, 1.0 - jnp.abs(cell - middle) / (0.1 * DEPTH))
    return (1.0 + 2.0 * bump) / DEPTH


def centre_of(col, shift):
    return ((CELLS - 1) / 2.0 + STEP * (col - (COLS - 1) / 2.0)) + shift


def pick(tiles, first, last, index):
    inside = index & (LANES - 1)
    tile = index >> 7
    value = None
    for number in range(first, last + 1):
        found = jnp.take_along_axis(tiles[number], inside, axis=1, mode="promise_in_bounds")
        value = found if value is None else jnp.where(tile == number, found, value)
    return value


def span(low, high, tiles):
    first = max(0, min(tiles - 1, math.floor(low) // LANES))
    return first, max(first, min(tiles - 1, math.floor(high) // LANES))


def sines(subset_ref, which):
    chosen = jnp.zeros_like(which)
    for angle in range(ANGLES):
        chosen = jnp.where(which == angle, subset_ref[angle], chosen)
    return jnp.sin(2.0 * math.pi / TOTAL_ANG * chosen.astype(jnp.float32))


def ray_sums(tiles, shift, chunk):
    lane = lax.broadcasted_iota(jnp.int32, (ANGLES, LANES), 1).astype(jnp.float32)
    detector = lane + chunk * LANES
    nearest = jnp.floor((detector - (CELLS - 1) / 2.0 - shift) * (1.0 / STEP) + (COLS - 1) / 2.0)
    middle = (chunk * LANES - (CELLS - 1) / 2.0) / STEP + (COLS - 1) / 2.0
    first, last = span(middle - 49.5, middle + 49.5 + 128 / STEP + 1, COLS // LANES)
    values, total = [0.0, 0.0], 0.0
    for near in (0.0, 1.0):
        col = nearest + near
        weight = jnp.maximum(0.0, 1.0 - jnp.abs(detector - centre_of(col, shift)))
        weight = jnp.where((col >= 0.0) & (col <= COLS - 1.0), weight, 0.0)
        index = col.astype(jnp.int32)
        values = [value + weight * pick(tile, first, last, index) for value, tile in zip(values, tiles)]
        total = total + weight
    return values, total


def spread_rows(tiles, shift, chunk):
    lane = lax.broadcasted_iota(jnp.int32, (ANGLES, LANES), 1).astype(jnp.float32)
    centre = centre_of(lane + chunk * LANES, shift)
    left = jnp.floor(centre)
    middle = (CELLS - 1) / 2.0 + STEP * (chunk * LANES - (COLS - 1) / 2.0)
    first, last = span(middle - 52.5, middle + 52.5 + STEP * 128 + 1, CELLS // LANES)
    value = 0.0
    for near in (0.0, 1.0):
        detector = left + near
        weight = jnp.maximum(0.0, 1.0 - jnp.abs(detector - centre))
        value = value + weight * pick(tiles, first, last, detector.astype(jnp.int32))
    return value


def main_kernel(
    subset_hbm, row_start_hbm, order_hbm, axial_hbm, volume_hbm, scale_hbm, measured_hbm, norm_hbm,
    back, residual, volume, scale, moved, depth,
    subset, row_start, order, axial, measured, norm, rowsum, straight, sino, aux, every, every_aux, every_wide, tall, weight, wide, matrix,
    remainder, ratio, linear, arrived,
    volume_sem, small_sem, load_sem, send_sem, recv_sem, aux_send, aux_recv,
    near_send, near_recv, aux2_send, aux2_recv, input_send, input_recv, out_send, out_recv,
):
    f32, bf16 = jnp.float32, jnp.bfloat16
    block = DEPTH // PARTS
    g, m = lax.axis_index("grp"), lax.axis_index("blk")
    core = g % 2
    y, z, x = (m // 16) * 2 + g // 2, (m // 4) % 4, m % 4
    sibling = (g - core + (1 - core), m)

    ys, zs, xs = ([(place + step) % 4 for step in range(4)] for place in (y, z, x))
    group_of = [place % 2 * 2 + core for place in ys]
    plane_of = [place // 2 * 16 for place in ys]
    line_of = [[row * 4 + col for col in xs] for row in zs]

    def partner(offset):
        return group_of[offset[0]], plane_of[offset[0]] + line_of[offset[1]][offset[2]]

    def partner_slot(offset):
        return ys[offset[0]] * 16 + line_of[offset[1]][offset[2]]

    def arrived_all(ref, sem):
        return pltpu.make_async_copy(ref, ref, sem)

    here_chip = y * 16 + z * 4 + x

    def slot(number, members=1):
        return pl.ds(pl.multiple_of(number * 16, 16), members * 16)

    def remote(source_ref, target_ref, send, recv, device):
        return pltpu.make_async_remote_copy(
            src_ref=source_ref, dst_ref=target_ref, send_sem=send, recv_sem=recv,
            device_id=device, device_id_type=MESH,
        )

    small = [
        pltpu.make_async_copy(subset_hbm, subset, small_sem.at[0]),
        pltpu.make_async_copy(row_start_hbm, row_start, small_sem.at[1]),
        pltpu.make_async_copy(axial_hbm, axial, small_sem.at[2]),
        pltpu.make_async_copy(order_hbm, order, small_sem.at[3]),
    ]
    for copy in small:
        copy.start()
    bring = []
    for q in range(2):
        for part in range(PARTS):
            here = pl.ds(part * block, block)
            bring.append(pltpu.make_async_copy(volume_hbm.at[q, here], volume.at[q, here], volume_sem.at[q * PARTS + part]))
    for copy in bring:
        copy.start()
    mine = pl.ds(pl.multiple_of(core * ROWS, ROWS), ROWS)
    other = pl.ds(pl.multiple_of((1 - core) * ROWS, ROWS), ROWS)
    load = [
        pltpu.make_async_copy(
            array.at[:, chunk, :], target.at[mine, pl.ds(chunk * LANES, LANES)], load_sem.at[number * 8 + chunk]
        )
        for number, (array, target) in enumerate(((measured_hbm, measured), (norm_hbm, norm))) for chunk in range(8)
    ]
    load_scale = pltpu.make_async_copy(scale_hbm, scale, load_sem.at[16])

    barrier = pltpu.get_barrier_semaphore()

    for offset in OFFSETS:
        pl.semaphore_signal(barrier, inc=1, device_id=partner(offset), device_id_type=MESH)
    pl.semaphore_signal(barrier, inc=1, device_id=sibling, device_id_type=MESH)

    for copy in small:
        copy.wait()
    sine = sines(subset, lax.broadcasted_iota(jnp.int32, (ANGLES, LANES), 0))
    shift = (0.05 * CELLS) * sine
    moved[...] = shift
    tiles, means = [], []
    for q in range(2):
        total = 0.0
        for part in range(PARTS):
            cell = (lax.broadcasted_iota(jnp.int32, (ANGLES, block), 1) + part * block).astype(f32)
            high, low = halves(depth_weight(cell, sine[:, :1]))
            bring[q * PARTS + part].wait()
            volume_high, volume_low = halves(volume[q, part * block:(part + 1) * block, :])
            both = dot(jnp.concatenate([high, low], axis=0), volume_high)
            total = total + (both[:ANGLES] + (both[ANGLES:] + dot(high, volume_low)))
        middle = jnp.sum(total, axis=1, keepdims=True) * (1.0 / COLS)
        means.append(middle)
        total = total - middle
        tiles.append([total[:, t * LANES:(t + 1) * LANES] for t in range(COLS // LANES)])
    for copy in load:
        copy.start()
    load_scale.start()
    for chunk in range(CELLS // LANES):
        values, sums = ray_sums(tiles, shift, chunk)
        rowsum[:, chunk * LANES:(chunk + 1) * LANES] = sums
        for q in range(2):
            straight[pl.ds(q * 8 + chunk, ANGLES, stride=16), :] = values[q]
    sino[...] = straight[:512].astype(bf16)

    lane = lax.broadcasted_iota(jnp.int32, (ANGLES, LANES), 1)
    first = jnp.sum(jnp.where(lane == g * 32 + m, row_start[...], 0), axis=1, keepdims=True).astype(f32)
    table = jnp.concatenate([axial[...].reshape(16, ANGLES), jnp.zeros((16, LANES - ANGLES), f32)], axis=1)
    table = jnp.concatenate([table, jnp.zeros((LANES - 16, LANES), f32)], axis=0).T[:ANGLES]
    for number, column in ((16, first), (17, means[0]), (18, means[1])):
        table = jnp.where(lane == number, column, table)
    aux[...] = table.reshape(ANGLES, 1, LANES)

    pl.semaphore_wait(barrier, 64)

    for offset in OFFSETS:
        device = partner(offset)
        remote(
            aux.at[device[1]], every_aux.at[core * 64 + here_chip], aux_send.at[0], aux_recv.at[offset[0]], device
        ).start()
        remote(
            sino.at[slot(device[1])], every.at[slot(core * 64 + here_chip)], send_sem.at[0], recv_sem.at[offset[0]], device
        ).start()
    every[slot(core * 64 + here_chip)] = sino[slot(m)]
    every_aux[core * 64 + here_chip] = aux[m]

    for copy in load:
        copy.wait()

    def near_input(number, rows):
        target = (measured, norm)[number].at[rows]
        return remote(target, target, input_send.at[number], input_recv.at[number], sibling)

    near_input(0, mine).start()
    near_input(1, mine).start()

    rows = order[...].astype(f32)
    lower = jnp.concatenate([rows[i:i + 1] for i in range(3)], axis=1)
    upper = jnp.concatenate([rows[i:i + 1] for i in range(3, 6)], axis=1)
    rows = jnp.where(y % 2 == 0, lower, upper)
    own_sum = rowsum[pl.ds(m, 1), :]

    def first_slot(number, side):
        return pl.multiple_of(side * 64 + ys[(4 - number) % 4] * 16, 16)

    def near_rows(number, side):
        here = slot(first_slot(number, side), 16)
        return remote(every.at[here], every.at[here], near_send.at[number], near_recv.at[number], sibling)

    def near_aux(number, side):
        here = pl.ds(first_slot(number, side), 16)
        return remote(every_aux.at[here], every_aux.at[here], aux2_send.at[number], aux2_recv.at[number], sibling)

    def place(step, number, side, turn):
        low = first_slot(number, side)
        table = every_aux[pl.ds(low, 16)].reshape(16, LANES)
        offset = (rows - table[:, 16:17]).astype(jnp.int32)
        inside, entry = (offset >= 0) & (offset < FOOT), offset & (FOOT - 1)
        lane = lax.broadcasted_iota(jnp.int32, (16, LANES), 1)
        every_wide[...] = every[slot(low, 16), :].astype(f32)
        for q in range(2):
            value = jnp.where(inside, jnp.concatenate([
                jnp.take_along_axis(
                    table, entry[:, part * LANES:(part + 1) * LANES] + q * FOOT, axis=1, mode="promise_in_bounds"
                )
                for part in range(3)
            ], axis=1), 0.0)
            line = step * 64 + turn * 32 + q * 16
            tall[line:line + 16, :] = value
            if turn == 0:
                high, low_part = halves(value)
                weight[step * 32 + q * 16:step * 32 + q * 16 + 16, :] = high
                weight[128 + step * 32 + q * 16:128 + step * 32 + q * 16 + 16, :] = low_part
            for chunk in range(8):
                matrix[line:line + 16, chunk * LANES:(chunk + 1) * LANES] = (
                    every_wide[pl.ds(q * 8 + chunk, 16, stride=16), :].astype(bf16)
                )
            high, low_part = halves(table[:, 17 + q:18 + q])
            level = jnp.where(lane == 0, high.astype(f32), jnp.where(lane == 1, low_part.astype(f32), 0.0))
            matrix[line:line + 16, CELLS:CELLS + LANES] = level.astype(bf16)

    def own_rows(step, number):
        low, count = first_slot(number, core), 15 if number == 0 else 16
        arrived_all(every_aux.at[pl.ds(low, count)], aux_recv.at[number]).wait()
        near_aux(number, core).start()
        arrived_all(every.at[slot(low, count)], recv_sem.at[number]).wait()
        near_rows(number, core).start()
        if step < 3:
            place(step, number, core, 0)

    def sibling_rows(step, number):
        near_aux(number, 1 - core).wait_recv()
        near_rows(number, 1 - core).wait_recv()
        place(step, number, 1 - core, 1)

    def turn_over(part):
        high, low = halves(tall[part * LANES:(part + 1) * LANES, :].T)
        wide[part, :, 0:LANES] = high
        wide[part, :, LANES:2 * LANES] = low

    def product(part, here):
        right = matrix[part * LANES:(part + 1) * LANES, here]
        return dot(wide[part], jnp.concatenate([right, right], axis=0))

    def level_of(part):
        value = product(part, slice(CELLS, CELLS + LANES))
        return jnp.broadcast_to(value[:, 0:1] + value[:, 1:2], (2 * ROWS, LANES))

    def sums(part, pair, level):
        value = product(part, slice(pair * 256, (pair + 1) * 256))
        for side in range(2):
            here = slice((2 * pair + side) * LANES, (2 * pair + side + 1) * LANES)
            yield here, value[:, side * LANES:(side + 1) * LANES] + level * own_sum[:, here]

    sequence = (0, 1, 3, 2)
    own_rows(0, 0)
    own_rows(1, 1)
    sibling_rows(0, 0)
    own_rows(2, 3)
    sibling_rows(1, 1)
    turn_over(0)
    own_rows(3, 2)
    near_input(0, mine).wait_send()
    near_input(0, other).wait_recv()
    near_input(1, other).wait_recv()
    place(3, 2, core, 0)
    level = level_of(0)
    for pair in range(4):
        for here, found in sums(0, pair, level):
            measured[:, here] = measured[:, here] - found
    sibling_rows(2, 3)
    sibling_rows(3, 2)
    turn_over(1)

    level = level_of(1)

    def forward(pair):
        for here, found in sums(1, pair, level):
            rest = norm[:, here] * (measured[:, here] - found)
            remainder[:, here] = rest
            ratio[:, here] = rest.astype(bf16)

    def collect(pair):
        both = dot(weight[...], ratio[:, pair * 256:(pair + 1) * 256])
        value = both[:128] + both[128:]
        for step, number in enumerate(sequence):
            low = first_slot(number, 0) * 16
            for q in range(2):
                line = step * 32 + q * 16
                for side in range(2):
                    straight[pl.ds(low + q * 8 + 2 * pair + side, 16, stride=16), :] = (
                        value[line:line + 16, side * LANES:(side + 1) * LANES]
                    )

    for pair in range(4):
        forward(pair)
        collect(pair)

    arrival = (y % 2) * 32 + m
    for offset in OFFSETS:
        rows = slot(partner_slot(offset))
        linear[rows] = straight[rows].astype(bf16)
        remote(linear.at[rows], arrived.at[slot(arrival)], out_send.at[0], out_recv.at[0], partner(offset)).start()
    arrived[slot(arrival)] = straight[slot(here_chip)].astype(bf16)

    keep = [
        pltpu.make_async_copy(
            remainder.at[mine, pl.ds(chunk * LANES, LANES)], residual.at[:, chunk, :], load_sem.at[17 + chunk]
        )
        for chunk in range(8)
    ]
    for copy in keep:
        copy.start()
    sine_row = sines(subset, lax.broadcasted_iota(jnp.int32, (8, LANES), 1) % ANGLES)[:1]
    for part in range(PARTS):
        cell = (lax.broadcasted_iota(jnp.int32, (block, LANES), 0) + part * block).astype(f32)
        lane = lax.broadcasted_iota(jnp.int32, (block, LANES), 1)
        value = depth_weight(cell, sine_row)
        high = value.astype(bf16).astype(f32)
        depth[part * block:(part + 1) * block, :] = jnp.where(lane < 2 * ANGLES, high, value - high).astype(bf16)

    arrived_all(every.at[slot(0, 63)], send_sem.at[0]).wait()
    arrived_all(every_aux.at[pl.ds(0, 63)], aux_send.at[0]).wait()
    for number in range(4):
        near_rows(number, core).wait_send()
        near_aux(number, core).wait_send()
    near_input(1, mine).wait_send()
    load_scale.wait()
    for copy in keep:
        copy.wait()

    arrived_all(arrived.at[slot(0, 63)], out_recv.at[0]).wait()
    back[...] = arrived[...]
    arrived_all(linear.at[slot(0, 63)], out_send.at[0]).wait()


def final_kernel(moved, depth, back, volume, scale, residual_in, new_volume, residual, straight, spread, staged, sems, rest_sem):
    f32 = jnp.float32
    block = DEPTH // OUT_PARTS
    keep = pltpu.make_async_copy(residual_in, residual, rest_sem)
    keep.start()
    straight[...] = back[:512].astype(f32) + back[512:].astype(f32)
    shift = moved[...]
    copies = []
    for q in range(2):
        tiles = [straight[pl.ds(q * 8 + chunk, ANGLES, stride=16), :] for chunk in range(CELLS // LANES)]
        for chunk in range(COLS // LANES):
            high, low = halves(spread_rows(tiles, shift, chunk))
            here = slice(chunk * LANES, (chunk + 1) * LANES)
            spread[q, 0:ANGLES, here] = high
            spread[q, ANGLES:2 * ANGLES, here] = low
            spread[q, 2 * ANGLES:3 * ANGLES, here] = high
            spread[q, 3 * ANGLES:4 * ANGLES, here] = jnp.zeros_like(high)
        for part in range(OUT_PARTS):
            here = slice(part * block, (part + 1) * block)
            update = dot(depth[here, :], spread[q])
            staged[q, here, :] = jnp.maximum(0.0, volume[q, here, :] + scale[q, here, :] * update)
            rows = pl.ds(part * block, block)
            copies.append(pltpu.make_async_copy(staged.at[q, rows], new_volume.at[q, rows], sems.at[q * OUT_PARTS + part]))
            copies[-1].start()
    for copy in copies:
        copy.wait()
    keep.wait()


def shards(volume, voxel_norm, measured, ray_norm, axial_weights, row_start, row_order, subset):
    f32, bf16 = jnp.float32, jnp.bfloat16
    vmem = pl.BlockSpec(memory_space=pltpu.VMEM)
    hbm = pl.BlockSpec(memory_space=pltpu.HBM)
    dma = pltpu.SemaphoreType.DMA
    back, residual, volume_near, scale_near, moved, depth = pl.pallas_call(
        main_kernel,
        in_specs=[hbm] * 8,
        out_specs=(vmem, hbm, vmem, vmem, vmem, vmem),
        out_shape=(
            jax.ShapeDtypeStruct((1024, LANES), bf16), jax.ShapeDtypeStruct((ROWS, 8, LANES), f32),
            jax.ShapeDtypeStruct(volume.shape, f32), jax.ShapeDtypeStruct(volume.shape, f32),
            jax.ShapeDtypeStruct((ANGLES, LANES), f32), jax.ShapeDtypeStruct((DEPTH, LANES), bf16),
        ),
        scratch_shapes=[
            pltpu.SMEM((ANGLES,), jnp.int32), pltpu.VMEM((ANGLES, 4 * ANGLES), jnp.int32),
            pltpu.VMEM((6, LANES), jnp.int32), pltpu.VMEM((2, FOOT, ANGLES), f32),
            pltpu.VMEM((2 * ROWS, CELLS), f32), pltpu.VMEM((2 * ROWS, CELLS), f32),
            pltpu.VMEM((ANGLES, CELLS), f32), pltpu.VMEM((1024, LANES), f32), pltpu.VMEM((512, LANES), bf16),
            pltpu.VMEM((ANGLES, 1, LANES), f32), pltpu.VMEM((2048, LANES), bf16), pltpu.VMEM((128, 1, LANES), f32),
            pltpu.VMEM((256, LANES), f32), pltpu.VMEM((256, 2 * ROWS), f32), pltpu.VMEM((256, 2 * ROWS), bf16),
            pltpu.VMEM((2, 2 * ROWS, 256), bf16), pltpu.VMEM((256, CELLS + LANES), bf16),
            pltpu.VMEM((2 * ROWS, CELLS), f32), pltpu.VMEM((2 * ROWS, CELLS), bf16),
            pltpu.VMEM((1024, LANES), bf16), pltpu.VMEM((1024, LANES), bf16),
            dma((2 * PARTS,)), dma((4,)), dma((25,)), dma((1,)), dma((4,)), dma((1,)), dma((4,)),
            dma((4,)), dma((4,)), dma((4,)), dma((4,)), dma((2,)), dma((2,)), dma((1,)), dma((1,)),
        ],
        compiler_params=pltpu.CompilerParams(collective_id=0, has_side_effects=True, vmem_limit_bytes=28 << 20),
        cost_estimate=pl.CostEstimate(flops=10 ** 9, bytes_accessed=100 << 20, transcendentals=0),
        name="exchange",
    )(
        *[pltpu.with_memory_space_constraint(array, pltpu.HBM) for array in (
            subset, row_start, row_order.reshape(6, LANES), jnp.transpose(axial_weights, (0, 2, 1)), volume, voxel_norm,
            measured.reshape(ROWS, 8, LANES), ray_norm.reshape(ROWS, 8, LANES),
        )]
    )
    new_volume, residual = pl.pallas_call(
        final_kernel,
        in_specs=[vmem, vmem, vmem, vmem, vmem, pl.BlockSpec(memory_space=pl.ANY)],
        out_specs=(hbm, hbm),
        out_shape=(jax.ShapeDtypeStruct(volume.shape, f32), jax.ShapeDtypeStruct((ROWS, 8, LANES), f32)),
        scratch_shapes=[
            pltpu.VMEM((512, LANES), f32), pltpu.VMEM((2, LANES, COLS), bf16), pltpu.VMEM(volume.shape, f32),
            dma((2 * OUT_PARTS,)), dma,
        ],
        compiler_params=pltpu.CompilerParams(vmem_limit_bytes=28 << 20),
        cost_estimate=pl.CostEstimate(flops=6 * 64 * DEPTH * COLS, bytes_accessed=4 * 6 * DEPTH * COLS, transcendentals=0),
        name="final",
    )(moved, depth, back, volume_near, scale_near, residual)
    return new_volume, residual.reshape(measured.shape)


def solution(mesh):
    placed = (
        P(("grp", "blk"), None, None),
        P(("grp", "blk"), None, None),
        P("grp", "blk", None),
        P("grp", "blk", None),
        P(("grp", "blk"), None, None),
        P(),
        P(),
        P(),
    )
    return jax.shard_map(
        shards,
        mesh=mesh,
        in_specs=placed,
        out_specs=(P(("grp", "blk"), None, None), P("grp", "blk", None)),
        check_vma=False,
    )
```
